32 devices in a mesh: grp: 2 (over y), row: 8 (over z, x), layer: 2 (over core).
Axes of the slice: x: 2, y: 2, z: 4, core: 2. Of those that a mesh axis runs over, the one named last changes fastest.
Arguments:
- train_grads: bfloat16 [4096, 2, 4096], P(('grp', 'row'), 'layer'), parts along dimension 0, may hold values from -0.015991211 to 0.015991211
- query_grads: bfloat16 [3, 16, 2, 4096], P(None, 'row', 'layer'), may hold values from -6 to 6
- out_basis: float32 [2, 64, 64], P('layer')
- in_basis: float32 [2, 64, 64], P('layer')
- eigenvalues: float32 [2, 4096], P('layer'), may hold values from 0.05 to 5
- block_order: int32 [3], replicated, may hold values from 0 to 2, each once
- row_ids: int32 [16, 256], P(('grp', 'row')), parts along dimension 0, may hold values from 0 to 255, each once within a row
Outputs:
- scores: bfloat16 [3, 4096, 16], P(None, ('grp', 'row'), 'layer'), parts along dimension 1
The draws below stay inside these ranges and needn't reach their ends.
There are 2 independent parts, one for each index of `grp`. The reference program is written for one: setup_inputs(seed, part) draws one part's arguments, and reference() takes and returns one part's arrays. A program takes and returns all parts, laid end to end along the dimension named above; an argument that names none is the same for every part. Nothing has to cross between parts.
Inputs may be any that keep to these rules, and one draw needn't show every extreme that they name: Each row of row_ids holds every number of 0 to 255 once. block_order holds every number of 0 to 2 once.
All inputs are finite; a program needn't handle non-finite values.
Results may differ from the reference program's by a relative error of at most 0.0051.
Values may be sent and summed in bfloat16 or wider, within the bound.
No kernel may reach another device: no remote copies, remote signals or barrier semaphores. Data moves between devices by JAX's collectives and lax.ppermute only.
A program may use at most 64 MiB of HBM per device.

```python
import math
import jax
import jax.numpy as jnp
from jax import lax

D_PROJ = 64
PROJ = 4096
R_DEV = 256
BLOCKS = 3
LAYERS = 2
ROWS = 2048
QB_TOT = 16
N_ROW = 8


def orthogonal(key):
    noise = jax.random.normal(key, (LAYERS, D_PROJ, D_PROJ), jnp.float32) * (0.4 / 8.0)
    base = (jnp.eye(D_PROJ, dtype=jnp.float32)[None] + noise) / 1.5
    for step in range(16):
        cubed = jnp.einsum('lab,lcb,lcd->lad', base, base, base, precision=lax.Precision.HIGHEST)
        base = 1.5 * base - 0.5 * cubed
    return base


def draw_out_basis(key, part):
    key = jax.random.fold_in(key, 11)
    return orthogonal(key)


def draw_in_basis(key, part):
    key = jax.random.fold_in(key, 12)
    return orthogonal(key)


def levels(key, shape, split, low, high):
    loudness, own = 1.0, jax.random.fold_in(key, 6)
    for position, parts in split:
        draws = jnp.exp(jax.random.uniform(jax.random.fold_in(own, position), (parts,), jnp.float32, low / len(split), high / len(split)))
        loudness = loudness * jnp.repeat(draws, shape[position] // parts).reshape([-1 if axis == position else 1 for axis in range(len(shape))])
    return loudness


def centred(key, shape, deviation, bound, shards=(), held_as=jnp.bfloat16):
    drawn = jax.random.normal(key, shape, jnp.float32) * deviation
    if len(shards) > 0:
        drawn = levels(key, shape, shards, -0.22, 0.18) * drawn
    return jnp.clip(drawn, min=-bound, max=bound).astype(held_as)


def setup_inputs(seed: int = 0, part: int = 0) -> dict:
    arg_keys = jax.random.split(jax.random.key(seed), 8)
    part_keys = jax.random.split(jax.random.fold_in(arg_keys[7], part), 8)
    train_grads = centred(part_keys[0], (ROWS, LAYERS, PROJ), 0.002, 0.015991211, ((0, 8), (1, 2)))
    query_grads = centred(arg_keys[1], (BLOCKS, QB_TOT, LAYERS, PROJ), 1.0, 6.0, ((1, 8), (2, 2)))
    out_basis = draw_out_basis(jax.random.fold_in(arg_keys[7], 71), part)
    in_basis = draw_in_basis(jax.random.fold_in(arg_keys[7], 71), part)
    eigenvalues = jnp.clip(jnp.exp(math.log(5.0) - 4.6051702 * jax.random.uniform(arg_keys[4], (LAYERS, PROJ), jnp.float32) ** levels(arg_keys[4], (LAYERS, PROJ), ((0, 2),), -0.2, 0.2)), 0.05, 5.0)
    block_order = jax.random.permutation(arg_keys[5], BLOCKS).astype(jnp.int32)
    row_ids = jax.vmap(lambda own: jax.random.permutation(own, R_DEV))(jax.random.split(part_keys[6], N_ROW)).reshape((N_ROW, R_DEV)).astype(jnp.int32)
    return {"train_grads": train_grads, "query_grads": query_grads, "out_basis": out_basis, "in_basis": in_basis, "eigenvalues": eigenvalues, "block_order": block_order, "row_ids": row_ids}


DAMPING = 0.01


def precondition(raw, out_basis, in_basis, eigenvalues):
    count, layers, width = raw.shape
    side = out_basis.shape[1]
    grads = raw.astype(jnp.float32).reshape(count, layers, side, side)
    hp = lax.Precision.HIGHEST
    half = jnp.einsum('lao,nlab->nlob', out_basis, grads, precision=hp)
    rotated = jnp.einsum('nlob,lbi->nloi', half, in_basis, precision=hp)
    scaled = rotated / (eigenvalues.reshape(layers, side, side) + DAMPING)
    half_back = jnp.einsum('lao,nloi->nlai', out_basis, scaled, precision=hp)
    back = jnp.einsum('nlai,lbi->nlab', half_back, in_basis, precision=hp)
    return back.reshape(count, layers, width).astype(jnp.bfloat16)


def reference(train_grads, query_grads, out_basis, in_basis, eigenvalues, block_order, row_ids):
    blocks, qtot, layers, width = query_grads.shape
    ready = precondition(query_grads.reshape(blocks * qtot, layers, width), out_basis, in_basis, eigenvalues)
    ready = ready.reshape(blocks, qtot, layers, width)
    rows = train_grads.shape[0]
    groups = jnp.arange(rows, dtype=jnp.int32) // R_DEV
    source = groups * R_DEV + row_ids.reshape(-1).astype(jnp.int32)
    results = []
    for j in range(blocks):
        chosen = lax.dynamic_index_in_dim(ready, block_order[j], 0, keepdims=False)
        partial_value = jnp.zeros((rows, qtot), jnp.float32)
        for l in range(layers):
            partial_value = partial_value + jnp.dot(train_grads[:, l, :], chosen[:, l, :].T, preferred_element_type=jnp.float32)
        results.append(jnp.take(partial_value, source, axis=0).astype(jnp.bfloat16))
    return jnp.stack(results, axis=0)
```

```python
import jax
import jax.numpy as jnp
from jax import lax
from jax.sharding import PartitionSpec as P

DAMPING = 0.01


def precondition(raw, out_basis, in_basis, eigenvalues):
    count, layers, width = raw.shape
    side = out_basis.shape[1]
    grads = raw.astype(jnp.float32).reshape(count, layers, side, side)
    highest = lax.Precision.HIGHEST
    half = jnp.einsum("lao,nlab->nlob", out_basis, grads, precision=highest)
    rotated = jnp.einsum("nlob,lbi->nloi", half, in_basis, precision=highest)
    scaled = rotated / (eigenvalues.reshape(layers, side, side) + DAMPING)
    half_back = jnp.einsum("lao,nloi->nlai", out_basis, scaled, precision=highest)
    back = jnp.einsum("nlai,lbi->nlab", half_back, in_basis, precision=highest)
    return back.reshape(count, layers, width).astype(jnp.bfloat16)


def make_body(n_row, n_layer):
    def body(train_grads, query_grads, out_basis, in_basis, eigenvalues, block_order, row_ids):
        blocks, qdev, layers, width = query_grads.shape
        rows = train_grads.shape[0]
        own = precondition(
            query_grads.reshape(blocks * qdev, layers, width), out_basis, in_basis, eigenvalues
        )
        own = own.reshape(blocks * qdev, width)
        me = lax.axis_index("row")
        parts = [own]
        for m in range(1, n_row):
            parts.append(lax.ppermute(own, "row", [(i, i ^ m) for i in range(n_row)]))
        flat = jnp.concatenate(parts, axis=0)
        terms = jnp.dot(train_grads[:, 0, :], flat.T, preferred_element_type=jnp.float32)
        terms = terms.reshape(rows, n_row, blocks, qdev)
        source = jnp.arange(n_row, dtype=jnp.int32) ^ me
        terms = jnp.take(terms, source, axis=1)
        terms = terms.transpose(2, 0, 1, 3).reshape(blocks, rows, n_layer, n_row * qdev // n_layer)
        core = lax.axis_index("layer")
        mine = lax.dynamic_index_in_dim(terms, core, 2, keepdims=False)
        theirs = lax.dynamic_index_in_dim(terms, 1 - core, 2, keepdims=False)
        got = lax.ppermute(theirs, "layer", [(0, 1), (1, 0)])
        total = (mine + got).astype(jnp.bfloat16)
        return jnp.take(jnp.take(total, block_order, axis=0), row_ids[0], axis=1)

    return body


def solution(mesh):
    in_specs = (
        P(("grp", "row"), "layer", None),
        P(None, "row", "layer", None),
        P("layer", None, None),
        P("layer", None, None),
        P("layer", None),
        P(),
        P(("grp", "row"), None),
    )
    out_specs = P(None, ("grp", "row"), "layer")
    body = make_body(mesh.shape["row"], mesh.shape["layer"])
    return jax.shard_map(body, mesh=mesh, in_specs=in_specs, out_specs=out_specs, check_vma=False)
```

```python
import functools

import jax
import jax.numpy as jnp
from jax import lax
from jax.experimental import pallas as pl
from jax.experimental.pallas import tpu as pltpu
from jax.sharding import PartitionSpec as P

DAMPING = 0.01
LANES = 128
SEGMENTS = 4
F32, BF16 = jnp.float32, jnp.bfloat16
NT = (((1,), (1,)), ((), ()))


def split2(x):
    high = x.astype(BF16)
    return high, (x - high.astype(F32)).astype(BF16)


def mm(a, b):
    return jnp.dot(a, b, preferred_element_type=F32)


def mm_nt(a, b):
    return lax.dot_general(a, b, NT, preferred_element_type=F32)


def precondition_kernel(q_ref, out_basis_ref, in_basis_ref, eig_ref, sent_ref, x_scr, o_scr, eig_scr):
    blocks, qdev, width = q_ref.shape
    side = out_basis_ref.shape[1]
    half = side // 2
    count = blocks * qdev
    chunks = width // LANES
    for blk in range(blocks):
        flat = q_ref[blk].astype(F32)
        for k in range(chunks):
            x_scr[pl.ds(blk * qdev * chunks + k, qdev, stride=chunks), :] = flat[:, k * LANES:(k + 1) * LANES]
    scale = 1.0 / (eig_ref[...] + DAMPING)
    for k in range(chunks):
        for odd in range(2):
            at = k * LANES + odd * side
            eig_scr[2 * k + odd:2 * k + odd + 1, :side] = scale[:, at:at + side]
    scale = eig_scr[:, :side]
    o_scr[:, :side] = out_basis_ref[0]
    basis = jnp.concatenate(
        [o_scr[pl.ds(0, half, stride=2), :side], o_scr[pl.ds(1, half, stride=2), :side]], axis=0
    )
    b_hi, b_lo = split2(basis)
    t_hi, t_lo = split2(basis.T)
    left = jnp.concatenate([t_hi, t_hi, t_lo], axis=1)
    back = jnp.concatenate([b_hi, b_hi, b_lo], axis=1)
    i_hi, i_lo = split2(in_basis_ref[0])
    none = jnp.zeros_like(i_hi)
    raw = x_scr[...].astype(BF16)
    raw2 = jnp.concatenate([raw, raw], axis=1)
    even = mm(raw2, jnp.concatenate([i_hi, none, i_lo, none], axis=0))
    odd = mm(raw2, jnp.concatenate([none, i_hi, none, i_lo], axis=0))
    evens, odds = [], []
    for q in range(count):
        rows = slice(q * half, (q + 1) * half)
        hi, lo = split2(jnp.concatenate([even[rows], odd[rows]], axis=0))
        rotated = mm(left, jnp.concatenate([hi, lo, hi], axis=0))
        hi, lo = split2(rotated * scale)
        again = mm(back, jnp.concatenate([hi, lo, hi], axis=0))
        evens.append(again[:half])
        odds.append(again[half:])
    total = None
    for rows, lower in ((evens, False), (odds, True)):
        hi, lo = split2(jnp.concatenate(rows, axis=0))
        w_hi = jnp.concatenate([none, i_hi] if lower else [i_hi, none], axis=0)
        w_lo = jnp.concatenate([none, i_lo] if lower else [i_lo, none], axis=0)
        term = mm_nt(hi, w_hi) + mm_nt(lo, w_hi) + mm_nt(hi, w_lo)
        total = term if total is None else total + term
    x_scr[...] = total
    per = chunks // SEGMENTS
    for c in range(per):
        piece = x_scr[pl.ds(c, count * SEGMENTS, stride=per), :].astype(BF16)
        for d in range(sent_ref.shape[0]):
            sent_ref[d, :, c * LANES:(c + 1) * LANES] = piece


def precondition(query_grads, out_basis, in_basis, eigenvalues, copies):
    blocks, qdev, _, width = query_grads.shape
    count = blocks * qdev
    side = out_basis.shape[1]
    return pl.pallas_call(
        precondition_kernel,
        out_shape=jax.ShapeDtypeStruct((copies, count * SEGMENTS, width // SEGMENTS), BF16),
        in_specs=[pl.BlockSpec(memory_space=pltpu.VMEM)] * 4,
        out_specs=pl.BlockSpec(memory_space=pltpu.VMEM),
        scratch_shapes=[
            pltpu.VMEM((count * width // LANES, LANES), F32),
            pltpu.VMEM((side, LANES), F32),
            pltpu.VMEM((side, LANES), F32),
        ],
        name="precondition",
    )(query_grads.reshape(blocks, qdev, width), out_basis, in_basis, eigenvalues)


def exact_rows(pick, x):
    hi = x.astype(BF16)
    rest = x - hi.astype(F32)
    mid = rest.astype(BF16)
    low = (rest - mid.astype(F32)).astype(BF16)
    return hi, mid, low


def scores_kernel(n_row, blocks, qdev, core_ref, order_ref, train_ref, gathered_ref, ids_ref, mine_ref, other_ref):
    count = blocks * qdev
    seg = gathered_ref.shape[1]
    rows = train_ref.shape[0]
    queries = gathered_ref[...]
    lines = queries.shape[0]
    segment = lax.broadcasted_iota(jnp.int32, (lines, rows), 0) % SEGMENTS
    terms = jnp.zeros((lines, rows), F32)
    for j in range(SEGMENTS):
        terms = jnp.where(segment == j, mm_nt(queries, train_ref[:, j * seg:(j + 1) * seg]), terms)
    here = lax.broadcasted_iota(jnp.int32, (rows, rows), 0)
    place = (here == ids_ref[...]).astype(BF16)
    per = n_row * qdev // 2
    line = lax.broadcasted_iota(jnp.int32, (blocks * per, lines), 0)
    source = lax.broadcasted_iota(jnp.int32, (blocks * per, lines), 1) // SEGMENTS
    block = jnp.zeros_like(line)
    for j in range(blocks):
        block = jnp.where(line // per == j, order_ref[j], block)
    parts = exact_rows(None, terms)
    for which, ref in ((core_ref[0], mine_ref), (1 - core_ref[0], other_ref)):
        query = line % per + which * per
        pick = (source == (query // qdev) * count + block * qdev + query % qdev).astype(BF16)
        chosen = mm(pick, parts[0]) + mm(pick, parts[1]) + mm(pick, parts[2])
        a, b, c = exact_rows(None, chosen)
        ref[...] = mm(a, place) + mm(b, place) + mm(c, place)


def scores(n_row, core, block_order, train, gathered, row_ids, blocks, qdev):
    rows = train.shape[0]
    out = jax.ShapeDtypeStruct((blocks * n_row * qdev // 2, rows), F32)
    return pl.pallas_call(
        functools.partial(scores_kernel, n_row, blocks, qdev),
        out_shape=(out, out),
        in_specs=[pl.BlockSpec(memory_space=pltpu.SMEM)] * 2 + [pl.BlockSpec(memory_space=pltpu.VMEM)] * 3,
        out_specs=(pl.BlockSpec(memory_space=pltpu.VMEM),) * 2,
        compiler_params=pltpu.CompilerParams(vmem_limit_bytes=32 * 2**20),
        name="scores",
    )(core, block_order, train, gathered, row_ids)


def make_body(n_row):
    def body(train_grads, query_grads, out_basis, in_basis, eigenvalues, block_order, row_ids):
        blocks, qdev, _, width = query_grads.shape
        rows = train_grads.shape[0]
        sent = precondition(query_grads, out_basis, in_basis, eigenvalues, n_row)
        gathered = lax.all_to_all(sent, "row", 0, 0)
        gathered = gathered.reshape(-1, gathered.shape[-1])
        core = lax.axis_index("layer").reshape(1).astype(jnp.int32)
        mine, other = scores(
            n_row, core, block_order, train_grads.reshape(rows, width), gathered, row_ids, blocks, qdev
        )
        got = lax.ppermute(other, "layer", [(0, 1), (1, 0)])
        total = (mine + got).astype(BF16)
        return total.reshape(blocks, -1, rows).transpose(0, 2, 1)

    return body


def solution(mesh):
    in_specs = (
        P(("grp", "row"), "layer", None),
        P(None, "row", "layer", None),
        P("layer", None, None),
        P("layer", None, None),
        P("layer", None),
        P(),
        P(("grp", "row"), None),
    )
    out_specs = P(None, ("grp", "row"), "layer")
    body = make_body(mesh.shape["row"])
    return jax.shard_map(body, mesh=mesh, in_specs=in_specs, out_specs=out_specs, check_vma=False)
```

```python
import functools

import jax
import jax.numpy as jnp
from jax import lax
from jax.experimental import pallas as pl
from jax.experimental.pallas import tpu as pltpu
from jax.sharding import PartitionSpec as P

DAMPING = 0.01
LANES = 128
SEGMENTS = 4
F32, BF16 = jnp.float32, jnp.bfloat16
NT = (((1,), (1,)), ((), ()))


def split2(x):
    high = x.astype(BF16)
    return high, (x - high.astype(F32)).astype(BF16)


def mm(a, b):
    return jnp.dot(a, b, preferred_element_type=F32)


def mm_nt(a, b):
    return lax.dot_general(a, b, NT, preferred_element_type=F32)


def precondition_kernel(
    order_hbm, q_hbm, out_basis_hbm, in_basis_hbm, eig_hbm, ids_hbm, train_hbm,
    sent_ref, ids_out_ref, train_out_ref,
    order_ref, q_ref, out_basis_ref, in_basis_ref, eig_ref, x_scr, o_scr, eig_scr, sems,
):
    copies = [
        pltpu.make_async_copy(src, dst, sems.at[n])
        for n, (src, dst) in enumerate((
            (order_hbm, order_ref), (q_hbm, q_ref), (in_basis_hbm, in_basis_ref), (out_basis_hbm, out_basis_ref), (eig_hbm, eig_ref),
            (ids_hbm, ids_out_ref), (train_hbm, train_out_ref),
        ))
    ]
    for copy in copies:
        copy.start()
    for copy in copies[:5]:
        copy.wait()
    blocks, qdev, width = q_ref.shape
    side = out_basis_ref.shape[1]
    half = side // 2
    count = blocks * qdev
    chunks = width // LANES
    for j in range(blocks):
        flat = q_ref[order_ref[j]].astype(F32)
        for k in range(chunks):
            x_scr[pl.ds(j * qdev * chunks + k, qdev, stride=chunks), :] = flat[:, k * LANES:(k + 1) * LANES]
    scale = 1.0 / (eig_ref[...] + DAMPING)
    for k in range(chunks):
        for odd in range(2):
            at = k * LANES + odd * side
            eig_scr[2 * k + odd:2 * k + odd + 1, :side] = scale[:, at:at + side]
    scale = eig_scr[:, :side]
    o_scr[:, :side] = out_basis_ref[0]
    basis = jnp.concatenate(
        [o_scr[pl.ds(0, half, stride=2), :side], o_scr[pl.ds(1, half, stride=2), :side]], axis=0
    )
    b_hi, b_lo = split2(basis)
    t_hi, t_lo = split2(basis.T)
    left = jnp.concatenate([t_hi, t_hi, t_lo], axis=1)
    back = jnp.concatenate([b_hi, b_hi, b_lo], axis=1)
    i_hi, i_lo = split2(in_basis_ref[0])
    none = jnp.zeros_like(i_hi)
    raw = x_scr[...].astype(BF16)
    raw2 = jnp.concatenate([raw, raw], axis=1)
    even = mm(raw2, jnp.concatenate([i_hi, none, i_lo, none], axis=0))
    odd = mm(raw2, jnp.concatenate([none, i_hi, none, i_lo], axis=0))
    evens, odds = [], []
    for q in range(count):
        rows = slice(q * half, (q + 1) * half)
        hi, lo = split2(jnp.concatenate([even[rows], odd[rows]], axis=0))
        rotated = mm(left, jnp.concatenate([hi, lo, hi], axis=0))
        hi, lo = split2(rotated * scale)
        again = mm(back, jnp.concatenate([hi, lo, hi], axis=0))
        evens.append(again[:half])
        odds.append(again[half:])
    total = None
    for rows, lower in ((evens, False), (odds, True)):
        hi, lo = split2(jnp.concatenate(rows, axis=0))
        w_hi = jnp.concatenate([none, i_hi] if lower else [i_hi, none], axis=0)
        w_lo = jnp.concatenate([none, i_lo] if lower else [i_lo, none], axis=0)
        term = mm_nt(hi, w_hi) + mm_nt(lo, w_hi) + mm_nt(hi, w_lo)
        total = term if total is None else total + term
    x_scr[...] = total
    per = chunks // SEGMENTS
    for c in range(per):
        piece = x_scr[pl.ds(c, count * SEGMENTS, stride=per), :].astype(BF16)
        sent_ref[:, c * LANES:(c + 1) * LANES] = piece
    for copy in copies[5:]:
        copy.wait()


def precondition(block_order, query_grads, out_basis, in_basis, eigenvalues, row_ids, train):
    blocks, qdev, width = query_grads.shape
    count = blocks * qdev
    side = out_basis.shape[1]
    vmem = pl.BlockSpec(memory_space=pltpu.VMEM)
    hbm = pl.BlockSpec(memory_space=pltpu.HBM)
    free = pl.BlockSpec(memory_space=pl.ANY)
    return pl.pallas_call(
        precondition_kernel,
        out_shape=(
            jax.ShapeDtypeStruct((count * SEGMENTS, width // SEGMENTS), BF16),
            jax.ShapeDtypeStruct(row_ids.shape, row_ids.dtype),
            jax.ShapeDtypeStruct(train.shape, train.dtype),
        ),
        in_specs=[hbm] * 7,
        out_specs=(vmem, free, free),
        scratch_shapes=[
            pltpu.SMEM(block_order.shape, block_order.dtype),
            pltpu.VMEM(query_grads.shape, BF16),
            pltpu.VMEM(out_basis.shape, F32),
            pltpu.VMEM(in_basis.shape, F32),
            pltpu.VMEM(eigenvalues.shape, F32),
            pltpu.VMEM((count * width // LANES, LANES), F32),
            pltpu.VMEM((side, LANES), F32),
            pltpu.VMEM((side, LANES), F32),
            pltpu.SemaphoreType.DMA((7,)),
        ],
        compiler_params=pltpu.CompilerParams(vmem_limit_bytes=4 * 2**20),
        name="precondition",
    )(*(
        pltpu.with_memory_space_constraint(x, pltpu.HBM)
        for x in (block_order, query_grads, out_basis, in_basis, eigenvalues, row_ids, train)
    ))


def split3(x):
    hi = x.astype(BF16)
    rest = x - hi.astype(F32)
    mid = rest.astype(BF16)
    return hi, mid, (rest - mid.astype(F32)).astype(BF16)


def scores_kernel(masks, blocks, qdev, place_ref, train_ref, ids_ref, *refs):
    n_row = len(masks)
    parts, (mine_ref, other_ref, flat_scr, out_scr) = refs[:n_row], refs[n_row:]
    lines, seg = parts[0].shape
    rows = train_ref.shape[0]
    slot = 8
    per_seg = seg // LANES
    for b, part in enumerate(parts):
        flat = part[...].astype(F32)
        for c in range(per_seg):
            flat_scr[b, c, :lines, :] = flat[:, c * LANES:(c + 1) * LANES]
    terms = None
    for j in range(SEGMENTS):
        queries = jnp.concatenate([
            jnp.concatenate([flat_scr[b, c, pl.ds(j, slot, stride=SEGMENTS), :] for b in range(n_row)], axis=0)
            for c in range(per_seg)
        ], axis=1)
        term = mm_nt(queries.astype(BF16), train_ref[:, j * seg:(j + 1) * seg])
        terms = term if terms is None else terms + term
    here = lax.broadcasted_iota(jnp.int32, (rows, rows), 0)
    place = (here == ids_ref[...]).astype(BF16)
    a, b, c = split3(terms)
    ordered = mm(a, place) + mm(b, place) + mm(c, place)
    me, core = place_ref[0], place_ref[1]
    per = n_row // 2
    for b, mask in enumerate(masks):
        source = me ^ mask
        which = jnp.where(source // per == core, 0, 1)
        first = which * (blocks * per) + source % per
        for j in range(blocks):
            at = b * slot + j * qdev
            out_scr[first + j * per] = ordered[at:at + qdev]
    for i in range(blocks * per):
        mine_ref[i * qdev:(i + 1) * qdev, :] = out_scr[i]
        other_ref[i * qdev:(i + 1) * qdev, :] = out_scr[blocks * per + i]


def scores(masks, place, train, row_ids, parts, blocks, qdev):
    rows = train.shape[0]
    n_row = len(masks)
    lines, seg = parts[0].shape
    out = jax.ShapeDtypeStruct((blocks * n_row * qdev // 2, rows), F32)
    vmem = pl.BlockSpec(memory_space=pltpu.VMEM)
    return pl.pallas_call(
        functools.partial(scores_kernel, masks, blocks, qdev),
        out_shape=(out, out),
        in_specs=[pl.BlockSpec(memory_space=pltpu.SMEM)] + [vmem] * (2 + n_row),
        out_specs=(vmem, vmem),
        scratch_shapes=[
            pltpu.VMEM((n_row, seg // LANES, 8 * SEGMENTS, LANES), F32),
            pltpu.VMEM((blocks * n_row, qdev, rows), F32),
        ],
        compiler_params=pltpu.CompilerParams(vmem_limit_bytes=(16 if n_row <= 16 else 48) * 2**20),
        cost_estimate=pl.CostEstimate(flops=2 * n_row * 8 * rows * seg * SEGMENTS, bytes_accessed=train.size * 2 + n_row * lines * seg * 2, transcendentals=0),
        name="scores",
    )(place, train, row_ids, *parts)


def make_body(n_row):
    def swap(x, mask):
        return lax.ppermute(x, "row", [(i, i ^ mask) for i in range(n_row)])

    def body(train_grads, query_grads, out_basis, in_basis, eigenvalues, block_order, row_ids):
        blocks, qdev, _, width = query_grads.shape
        rows = train_grads.shape[0]
        own, row_ids, train = precondition(
            block_order, query_grads.reshape(blocks, qdev, width), out_basis, in_basis, eigenvalues, row_ids,
            train_grads.reshape(rows, width),
        )
        near = {0: own}
        for mask in [4, 6, 2] if n_row == 8 else range(2, n_row, 2):
            near[mask] = swap(own, mask)
        far = {mask ^ 1: swap(x, 1) for mask, x in near.items()}
        both = {**near, **far}
        place = jnp.stack([lax.axis_index("row"), lax.axis_index("layer")]).astype(jnp.int32)
        mine, other = scores(
            tuple(both), place, train, row_ids, tuple(both.values()), blocks, qdev
        )
        got = lax.ppermute(other, "layer", [(0, 1), (1, 0)])
        total = (mine + got).astype(BF16)
        return total.reshape(blocks, -1, rows).transpose(0, 2, 1)

    return body


def solution(mesh):
    in_specs = (
        P(("grp", "row"), "layer", None),
        P(None, "row", "layer", None),
        P("layer", None, None),
        P("layer", None, None),
        P("layer", None),
        P(),
        P(("grp", "row"), None),
    )
    out_specs = P(None, ("grp", "row"), "layer")
    body = make_body(mesh.shape["row"])
    return jax.shard_map(body, mesh=mesh, in_specs=in_specs, out_specs=out_specs, check_vma=False)
```

```python
import functools

import jax
import jax.numpy as jnp
from jax import lax
from jax.experimental import pallas as pl
from jax.experimental.pallas import tpu as pltpu
from jax.sharding import PartitionSpec as P

DAMPING = 0.01
LANES = 128
SEGMENTS = 4
F32, BF16 = jnp.float32, jnp.bfloat16
NT = (((1,), (1,)), ((), ()))


def split2(x):
    high = x.astype(BF16)
    return high, (x - high.astype(F32)).astype(BF16)


def mm(a, b):
    return jnp.dot(a, b, preferred_element_type=F32)


def mm_nt(a, b):
    return lax.dot_general(a, b, NT, preferred_element_type=F32)


def precondition_kernel(
    order_hbm, q_hbm, out_basis_hbm, in_basis_hbm, eig_hbm, ids_hbm, train_hbm,
    sent_ref, ids_out_ref, train_out_ref,
    order_ref, q_ref, out_basis_ref, in_basis_ref, eig_ref, x_scr, o_scr, eig_scr, sems,
):
    copies = [
        pltpu.make_async_copy(src, dst, sems.at[n])
        for n, (src, dst) in enumerate((
            (order_hbm, order_ref), (q_hbm, q_ref), (in_basis_hbm, in_basis_ref), (out_basis_hbm, out_basis_ref), (eig_hbm, eig_ref),
            (ids_hbm, ids_out_ref), (train_hbm, train_out_ref),
        ))
    ]
    for copy in copies:
        copy.start()
    for copy in copies[:5]:
        copy.wait()
    blocks, qdev, width = q_ref.shape
    side = out_basis_ref.shape[1]
    half = side // 2
    count = blocks * qdev
    chunks = width // LANES
    for j in range(blocks):
        flat = q_ref[order_ref[j]].astype(F32)
        for k in range(chunks):
            x_scr[pl.ds(j * qdev * chunks + k, qdev, stride=chunks), :] = flat[:, k * LANES:(k + 1) * LANES]
    scale = 1.0 / (eig_ref[...] + DAMPING)
    for k in range(chunks):
        for odd in range(2):
            at = k * LANES + odd * side
            eig_scr[2 * k + odd:2 * k + odd + 1, :side] = scale[:, at:at + side]
    scale = eig_scr[:, :side]
    o_scr[:, :side] = out_basis_ref[0]
    basis = jnp.concatenate(
        [o_scr[pl.ds(0, half, stride=2), :side], o_scr[pl.ds(1, half, stride=2), :side]], axis=0
    )
    b_hi, b_lo = split2(basis)
    t_hi, t_lo = split2(basis.T)
    left = jnp.concatenate([t_hi, t_hi, t_lo], axis=1)
    back = jnp.concatenate([b_hi, b_hi, b_lo], axis=1)
    i_hi, i_lo = split2(in_basis_ref[0])
    none = jnp.zeros_like(i_hi)
    raw = x_scr[...].astype(BF16)
    raw2 = jnp.concatenate([raw, raw], axis=1)
    even = mm(raw2, jnp.concatenate([i_hi, none, i_lo, none], axis=0))
    odd = mm(raw2, jnp.concatenate([none, i_hi, none, i_lo], axis=0))
    evens, odds = [], []
    for q in range(count):
        rows = slice(q * half, (q + 1) * half)
        hi, lo = split2(jnp.concatenate([even[rows], odd[rows]], axis=0))
        rotated = mm(left, jnp.concatenate([hi, lo, hi], axis=0))
        hi, lo = split2(rotated * scale)
        again = mm(back, jnp.concatenate([hi, lo, hi], axis=0))
        evens.append(again[:half])
        odds.append(again[half:])
    total = None
    for rows, lower in ((evens, False), (odds, True)):
        hi, lo = split2(jnp.concatenate(rows, axis=0))
        w_hi = jnp.concatenate([none, i_hi] if lower else [i_hi, none], axis=0)
        w_lo = jnp.concatenate([none, i_lo] if lower else [i_lo, none], axis=0)
        term = mm_nt(hi, w_hi) + mm_nt(lo, w_hi) + mm_nt(hi, w_lo)
        total = term if total is None else total + term
    x_scr[...] = total
    per = chunks // SEGMENTS
    for c in range(per):
        piece = x_scr[pl.ds(c, count * SEGMENTS, stride=per), :].astype(BF16)
        sent_ref[:, c * LANES:(c + 1) * LANES] = piece
    for copy in copies[5:]:
        copy.wait()


def precondition(block_order, query_grads, out_basis, in_basis, eigenvalues, row_ids, train):
    blocks, qdev, width = query_grads.shape
    count = blocks * qdev
    side = out_basis.shape[1]
    vmem = pl.BlockSpec(memory_space=pltpu.VMEM)
    hbm = pl.BlockSpec(memory_space=pltpu.HBM)
    free = pl.BlockSpec(memory_space=pl.ANY)
    return pl.pallas_call(
        precondition_kernel,
        out_shape=(
            jax.ShapeDtypeStruct((count * SEGMENTS, width // SEGMENTS), BF16),
            jax.ShapeDtypeStruct(row_ids.shape, row_ids.dtype),
            jax.ShapeDtypeStruct(train.shape, train.dtype),
        ),
        in_specs=[hbm] * 7,
        out_specs=(vmem, free, free),
        scratch_shapes=[
            pltpu.SMEM(block_order.shape, block_order.dtype),
            pltpu.VMEM(query_grads.shape, BF16),
            pltpu.VMEM(out_basis.shape, F32),
            pltpu.VMEM(in_basis.shape, F32),
            pltpu.VMEM(eigenvalues.shape, F32),
            pltpu.VMEM((count * width // LANES, LANES), F32),
            pltpu.VMEM((side, LANES), F32),
            pltpu.VMEM((side, LANES), F32),
            pltpu.SemaphoreType.DMA((7,)),
        ],
        compiler_params=pltpu.CompilerParams(vmem_limit_bytes=4 * 2**20),
        name="precondition",
    )(*(
        pltpu.with_memory_space_constraint(x, pltpu.HBM)
        for x in (block_order, query_grads, out_basis, in_basis, eigenvalues, row_ids, train)
    ))


def split3(x):
    hi = x.astype(BF16)
    rest = x - hi.astype(F32)
    mid = rest.astype(BF16)
    return hi, mid, (rest - mid.astype(F32)).astype(BF16)


def scores_kernel(masks, blocks, qdev, place_ref, train_ref, ids_ref, *refs):
    n_row = len(masks)
    parts, (mine_ref, other_ref, flat_scr, out_scr) = refs[:n_row], refs[n_row:]
    lines, seg = parts[0].shape
    rows = train_ref.shape[0]
    slot = 8
    per_seg = seg // LANES
    for b, part in enumerate(parts):
        flat = part[...].astype(F32)
        for c in range(per_seg):
            flat_scr[b, c, :lines, :] = flat[:, c * LANES:(c + 1) * LANES]
    terms = None
    for j in range(SEGMENTS):
        queries = jnp.concatenate([
            jnp.concatenate([flat_scr[b, c, pl.ds(j, slot, stride=SEGMENTS), :] for b in range(n_row)], axis=0)
            for c in range(per_seg)
        ], axis=1)
        term = mm_nt(queries.astype(BF16), train_ref[:, j * seg:(j + 1) * seg])
        terms = term if terms is None else terms + term
    here = lax.broadcasted_iota(jnp.int32, (rows, rows), 0)
    place = (here == ids_ref[...]).astype(BF16)
    a, b, c = split3(terms)
    ordered = mm(a, place) + mm(b, place) + mm(c, place)
    me, core = place_ref[0], place_ref[1]
    per = n_row // 2
    for b, mask in enumerate(masks):
        source = me ^ mask
        which = jnp.where(source // per == core, 0, 1)
        first = which * (blocks * per) + source % per
        for j in range(blocks):
            at = b * slot + j * qdev
            out_scr[first + j * per] = ordered[at:at + qdev]
    for i in range(blocks * per):
        mine_ref[i * qdev:(i + 1) * qdev, :] = out_scr[i]
        other_ref[i * qdev:(i + 1) * qdev, :] = out_scr[blocks * per + i]


def scores(masks, place, train, row_ids, parts, blocks, qdev):
    rows = train.shape[0]
    n_row = len(masks)
    lines, seg = parts[0].shape
    out = jax.ShapeDtypeStruct((blocks * n_row * qdev // 2, rows), F32)
    vmem = pl.BlockSpec(memory_space=pltpu.VMEM)
    return pl.pallas_call(
        functools.partial(scores_kernel, masks, blocks, qdev),
        out_shape=(out, out),
        in_specs=[pl.BlockSpec(memory_space=pltpu.SMEM)] + [vmem] * (2 + n_row),
        out_specs=(vmem, vmem),
        scratch_shapes=[
            pltpu.VMEM((n_row, seg // LANES, 8 * SEGMENTS, LANES), F32),
            pltpu.VMEM((blocks * n_row, qdev, rows), F32),
        ],
        compiler_params=pltpu.CompilerParams(vmem_limit_bytes=(16 if n_row <= 16 else 48) * 2**20),
        cost_estimate=pl.CostEstimate(flops=2 * n_row * 8 * rows * seg * SEGMENTS, bytes_accessed=train.size * 2 + n_row * lines * seg * 2, transcendentals=0),
        name="scores",
    )(place, train, row_ids, *parts)


def make_body(n_row):
    def swap(x, mask):
        return lax.ppermute(x, "row", [(i, i ^ mask) for i in range(n_row)])

    def body(train_grads, query_grads, out_basis, in_basis, eigenvalues, block_order, row_ids):
        blocks, qdev, _, width = query_grads.shape
        rows = train_grads.shape[0]
        own, row_ids, train = precondition(
            block_order, query_grads.reshape(blocks, qdev, width), out_basis, in_basis, eigenvalues, row_ids,
            train_grads.reshape(rows, width),
        )
        near = {0: own}
        far = {}
        if n_row == 8:
            near[2] = swap(own, 2)
            far[1] = swap(own, 1)
            near[4] = swap(own, 4)
            near[2], far[1], near[4] = lax.optimization_barrier((near[2], far[1], near[4]))
            near[6] = swap(near[4], 2)
        else:
            for mask in range(2, n_row, 2):
                near[mask] = swap(own, mask)
        for mask in near:
            if mask ^ 1 not in far:
                far[mask ^ 1] = swap(near[mask], 1)
        both = {**near, **far}
        place = jnp.stack([lax.axis_index("row"), lax.axis_index("layer")]).astype(jnp.int32)
        mine, other = scores(
            tuple(both), place, train, row_ids, tuple(both.values()), blocks, qdev
        )
        got = lax.ppermute(other, "layer", [(0, 1), (1, 0)])
        total = (mine + got).astype(BF16)
        return total.reshape(blocks, -1, rows).transpose(0, 2, 1)

    return body


def solution(mesh):
    in_specs = (
        P(("grp", "row"), "layer", None),
        P(None, "row", "layer", None),
        P("layer", None, None),
        P("layer", None, None),
        P("layer", None),
        P(),
        P(("grp", "row"), None),
    )
    out_specs = P(None, ("grp", "row"), "layer")
    body = make_body(mesh.shape["row"])
    return jax.shard_map(body, mesh=mesh, in_specs=in_specs, out_specs=out_specs, check_vma=False)
```

```python
import functools

import jax
import jax.numpy as jnp
from jax import lax
from jax.experimental import pallas as pl
from jax.experimental.pallas import tpu as pltpu
from jax.sharding import PartitionSpec as P

DAMPING = 0.01
LANES = 128
SEGMENTS = 4
F32, BF16 = jnp.float32, jnp.bfloat16
NT = (((1,), (1,)), ((), ()))


def split2(x):
    high = x.astype(BF16)
    return high, (x - high.astype(F32)).astype(BF16)


def mm(a, b):
    return jnp.dot(a, b, preferred_element_type=F32)


def mm_nt(a, b):
    return lax.dot_general(a, b, NT, preferred_element_type=F32)


def precondition_kernel(
    order_hbm, q_hbm, out_basis_hbm, in_basis_hbm, eig_hbm, ids_hbm, train_hbm,
    sent_ref, ids_out_ref, train_out_ref,
    order_ref, q_ref, out_basis_ref, in_basis_ref, eig_ref, x_scr, o_scr, eig_scr, sems,
):
    copies = [
        pltpu.make_async_copy(src, dst, sems.at[n])
        for n, (src, dst) in enumerate((
            (order_hbm, order_ref), (q_hbm, q_ref), (in_basis_hbm, in_basis_ref), (out_basis_hbm, out_basis_ref), (eig_hbm, eig_ref),
            (ids_hbm, ids_out_ref), (train_hbm, train_out_ref),
        ))
    ]
    for copy in copies:
        copy.start()
    for copy in copies[:5]:
        copy.wait()
    blocks, qdev, width = q_ref.shape
    side = out_basis_ref.shape[1]
    half = side // 2
    count = blocks * qdev
    chunks = width // LANES
    for j in range(blocks):
        flat = q_ref[order_ref[j]].astype(F32)
        for k in range(chunks):
            x_scr[pl.ds(j * qdev * chunks + k, qdev, stride=chunks), :] = flat[:, k * LANES:(k + 1) * LANES]
    scale = 1.0 / (eig_ref[...] + DAMPING)
    for k in range(chunks):
        for odd in range(2):
            at = k * LANES + odd * side
            eig_scr[2 * k + odd:2 * k + odd + 1, :side] = scale[:, at:at + side]
    scale = eig_scr[:, :side]
    o_scr[:, :side] = out_basis_ref[0]
    basis = jnp.concatenate(
        [o_scr[pl.ds(0, half, stride=2), :side], o_scr[pl.ds(1, half, stride=2), :side]], axis=0
    )
    b_hi, b_lo = split2(basis)
    t_hi, t_lo = split2(basis.T)
    left = jnp.concatenate([t_hi, t_hi, t_lo], axis=1)
    back = jnp.concatenate([b_hi, b_hi, b_lo], axis=1)
    i_hi, i_lo = split2(in_basis_ref[0])
    none = jnp.zeros_like(i_hi)
    raw = x_scr[...].astype(BF16)
    raw2 = jnp.concatenate([raw, raw], axis=1)
    even = mm(raw2, jnp.concatenate([i_hi, none, i_lo, none], axis=0))
    odd = mm(raw2, jnp.concatenate([none, i_hi, none, i_lo], axis=0))
    evens, odds = [], []
    for q in range(count):
        rows = slice(q * half, (q + 1) * half)
        hi, lo = split2(jnp.concatenate([even[rows], odd[rows]], axis=0))
        rotated = mm(left, jnp.concatenate([hi, lo, hi], axis=0))
        hi, lo = split2(rotated * scale)
        again = mm(back, jnp.concatenate([hi, lo, hi], axis=0))
        evens.append(again[:half])
        odds.append(again[half:])
    total = None
    for rows, lower in ((evens, False), (odds, True)):
        hi, lo = split2(jnp.concatenate(rows, axis=0))
        w_hi = jnp.concatenate([none, i_hi] if lower else [i_hi, none], axis=0)
        w_lo = jnp.concatenate([none, i_lo] if lower else [i_lo, none], axis=0)
        term = mm_nt(hi, w_hi) + mm_nt(lo, w_hi) + mm_nt(hi, w_lo)
        total = term if total is None else total + term
    x_scr[...] = total
    per = chunks // SEGMENTS
    for c in range(per):
        piece = x_scr[pl.ds(c, count * SEGMENTS, stride=per), :].astype(BF16)
        sent_ref[:, c * LANES:(c + 1) * LANES] = piece
    for copy in copies[5:]:
        copy.wait()


def precondition(block_order, query_grads, out_basis, in_basis, eigenvalues, row_ids, train):
    blocks, qdev, width = query_grads.shape
    count = blocks * qdev
    side = out_basis.shape[1]
    vmem = pl.BlockSpec(memory_space=pltpu.VMEM)
    hbm = pl.BlockSpec(memory_space=pltpu.HBM)
    free = pl.BlockSpec(memory_space=pl.ANY)
    return pl.pallas_call(
        precondition_kernel,
        out_shape=(
            jax.ShapeDtypeStruct((count * SEGMENTS, width // SEGMENTS), BF16),
            jax.ShapeDtypeStruct(row_ids.shape, row_ids.dtype),
            jax.ShapeDtypeStruct(train.shape, train.dtype),
        ),
        in_specs=[hbm] * 7,
        out_specs=(vmem, free, free),
        scratch_shapes=[
            pltpu.SMEM(block_order.shape, block_order.dtype),
            pltpu.VMEM(query_grads.shape, BF16),
            pltpu.VMEM(out_basis.shape, F32),
            pltpu.VMEM(in_basis.shape, F32),
            pltpu.VMEM(eigenvalues.shape, F32),
            pltpu.VMEM((count * width // LANES, LANES), F32),
            pltpu.VMEM((side, LANES), F32),
            pltpu.VMEM((side, LANES), F32),
            pltpu.SemaphoreType.DMA((7,)),
        ],
        compiler_params=pltpu.CompilerParams(vmem_limit_bytes=4 * 2**20),
        name="precondition",
    )(*(
        pltpu.with_memory_space_constraint(x, pltpu.HBM)
        for x in (block_order, query_grads, out_basis, in_basis, eigenvalues, row_ids, train)
    ))


def split3(x):
    hi = x.astype(BF16)
    rest = x - hi.astype(F32)
    mid = rest.astype(BF16)
    return hi, mid, (rest - mid.astype(F32)).astype(BF16)


def scores_kernel(masks, flips, blocks, qdev, place_ref, train_ref, ids_ref, *refs):
    n_row = len(masks)
    parts, (mine_ref, other_ref, flat_scr, out_scr) = refs[:n_row], refs[n_row:]
    lines, seg = parts[0].shape
    rows = train_ref.shape[0]
    slot = 8
    per_seg = seg // LANES
    for b, part in enumerate(parts):
        flat = part[...].astype(F32)
        for c in range(per_seg):
            flat_scr[b, c, :lines, :] = flat[:, c * LANES:(c + 1) * LANES]
    terms = None
    for j in range(SEGMENTS):
        queries = jnp.concatenate([
            jnp.concatenate([flat_scr[b, c, pl.ds(j, slot, stride=SEGMENTS), :] for b in range(n_row)], axis=0)
            for c in range(per_seg)
        ], axis=1)
        term = mm_nt(queries.astype(BF16), train_ref[:, j * seg:(j + 1) * seg])
        terms = term if terms is None else terms + term
    here = lax.broadcasted_iota(jnp.int32, (rows, rows), 0)
    place = (here == ids_ref[...]).astype(BF16)
    a, b, c = split3(terms)
    ordered = mm(a, place) + mm(b, place) + mm(c, place)
    me, core, group = place_ref[0], place_ref[1], place_ref[2]
    per = n_row // 2
    for b, (mask, flip) in enumerate(zip(masks, flips)):
        source = me ^ mask ^ (group * flip)
        which = jnp.where(source // per == core, 0, 1)
        first = which * (blocks * per) + source % per
        for j in range(blocks):
            at = b * slot + j * qdev
            out_scr[first + j * per] = ordered[at:at + qdev]
    for i in range(blocks * per):
        mine_ref[i * qdev:(i + 1) * qdev, :] = out_scr[i]
        other_ref[i * qdev:(i + 1) * qdev, :] = out_scr[blocks * per + i]


def scores(masks, flips, place, train, row_ids, parts, blocks, qdev):
    rows = train.shape[0]
    n_row = len(masks)
    lines, seg = parts[0].shape
    out = jax.ShapeDtypeStruct((blocks * n_row * qdev // 2, rows), F32)
    vmem = pl.BlockSpec(memory_space=pltpu.VMEM)
    return pl.pallas_call(
        functools.partial(scores_kernel, masks, flips, blocks, qdev),
        out_shape=(out, out),
        in_specs=[pl.BlockSpec(memory_space=pltpu.SMEM)] + [vmem] * (2 + n_row),
        out_specs=(vmem, vmem),
        scratch_shapes=[
            pltpu.VMEM((n_row, seg // LANES, 8 * SEGMENTS, LANES), F32),
            pltpu.VMEM((blocks * n_row, qdev, rows), F32),
        ],
        compiler_params=pltpu.CompilerParams(vmem_limit_bytes=(16 if n_row <= 16 else 48) * 2**20),
        cost_estimate=pl.CostEstimate(flops=2 * n_row * 8 * rows * seg * SEGMENTS, bytes_accessed=train.size * 2 + n_row * lines * seg * 2, transcendentals=0),
        name="scores",
    )(place, train, row_ids, *parts)


def make_body(n_grp, n_row):
    def swap(x, mask, other_mask=None, cross=0):
        pairs = []
        for g in range(n_grp):
            for r in range(n_row):
                to = r ^ (mask if g == 0 or other_mask is None else other_mask)
                pairs.append((g * n_row + r, (g ^ cross) * n_row + to))
        return lax.ppermute(x, ("grp", "row"), pairs)

    def gather(own):
        if n_row != 8 or n_grp != 2:
            near = [(0, 0, own)] + [(m, 0, swap(own, m)) for m in range(2, n_row, 2)]
            return near + [(m ^ 1, 0, swap(x, 1)) for m, _, x in near]
        far = swap(own, 4, 6)
        parts = [(0, 0, own)] + [(m, 0, swap(own, m)) for m in (1, 2, 3)]
        parts.append((4, 2, far))
        parts.append((6, 2, swap(far, 0, cross=1)))
        parts.append((5, 2, swap(far, 1)))
        parts.append((7, 2, swap(far, 1, cross=1)))
        return parts

    def body(train_grads, query_grads, out_basis, in_basis, eigenvalues, block_order, row_ids):
        blocks, qdev, _, width = query_grads.shape
        rows = train_grads.shape[0]
        own, row_ids, train = precondition(
            block_order, query_grads.reshape(blocks, qdev, width), out_basis, in_basis, eigenvalues, row_ids,
            train_grads.reshape(rows, width),
        )
        masks, flips, parts = zip(*gather(own))
        place = jnp.stack([lax.axis_index(name) for name in ("row", "layer", "grp")]).astype(jnp.int32)
        mine, other = scores(masks, flips, place, train, row_ids, parts, blocks, qdev)
        got = lax.ppermute(other, "layer", [(0, 1), (1, 0)])
        total = (mine + got).astype(BF16)
        return total.reshape(blocks, -1, rows).transpose(0, 2, 1)

    return body


def solution(mesh):
    in_specs = (
        P(("grp", "row"), "layer", None),
        P(None, "row", "layer", None),
        P("layer", None, None),
        P("layer", None, None),
        P("layer", None),
        P(),
        P(("grp", "row"), None),
    )
    out_specs = P(None, ("grp", "row"), "layer")
    body = make_body(mesh.shape["grp"], mesh.shape["row"])
    return jax.shard_map(body, mesh=mesh, in_specs=in_specs, out_specs=out_specs, check_vma=False)
```

```python
import functools

import jax
import jax.numpy as jnp
from jax import lax
from jax.experimental import pallas as pl
from jax.experimental.pallas import tpu as pltpu
from jax.sharding import PartitionSpec as P

DAMPING = 0.01
LANES = 128
SEGMENTS = 4
F32, BF16 = jnp.float32, jnp.bfloat16
NT = (((1,), (1,)), ((), ()))


def split2(x):
    high = x.astype(BF16)
    return high, (x - high.astype(F32)).astype(BF16)


def mm(a, b):
    return jnp.dot(a, b, preferred_element_type=F32)


def mm_nt(a, b):
    return lax.dot_general(a, b, NT, preferred_element_type=F32)


def precondition_kernel(
    order_hbm, q_hbm, out_basis_hbm, in_basis_hbm, eig_hbm, ids_hbm, train_hbm,
    sent_ref, ids_out_ref, train_out_ref,
    order_ref, q_ref, out_basis_ref, in_basis_ref, eig_ref, x_scr, o_scr, eig_scr, sems,
):
    copies = [
        pltpu.make_async_copy(src, dst, sems.at[n])
        for n, (src, dst) in enumerate((
            (order_hbm, order_ref), (q_hbm, q_ref), (in_basis_hbm, in_basis_ref), (out_basis_hbm, out_basis_ref), (eig_hbm, eig_ref),
            (ids_hbm, ids_out_ref), (train_hbm, train_out_ref),
        ))
    ]
    for copy in copies:
        copy.start()
    for copy in copies[:5]:
        copy.wait()
    blocks, qdev, width = q_ref.shape
    side = out_basis_ref.shape[1]
    half = side // 2
    count = blocks * qdev
    chunks = width // LANES
    for j in range(blocks):
        flat = q_ref[order_ref[j]].astype(F32)
        for k in range(chunks):
            x_scr[pl.ds(j * qdev * chunks + k, qdev, stride=chunks), :] = flat[:, k * LANES:(k + 1) * LANES]
    scale = 1.0 / (eig_ref[...] + DAMPING)
    for k in range(chunks):
        for odd in range(2):
            at = k * LANES + odd * side
            eig_scr[2 * k + odd:2 * k + odd + 1, :side] = scale[:, at:at + side]
    scale = eig_scr[:, :side]
    o_scr[:, :side] = out_basis_ref[0]
    basis = jnp.concatenate(
        [o_scr[pl.ds(0, half, stride=2), :side], o_scr[pl.ds(1, half, stride=2), :side]], axis=0
    )
    b_hi, b_lo = split2(basis)
    t_hi, t_lo = split2(basis.T)
    left = jnp.concatenate([t_hi, t_hi, t_lo], axis=1)
    back = jnp.concatenate([b_hi, b_hi, b_lo], axis=1)
    i_hi, i_lo = split2(in_basis_ref[0])
    none = jnp.zeros_like(i_hi)
    raw = x_scr[...].astype(BF16)
    raw2 = jnp.concatenate([raw, raw], axis=1)
    even = mm(raw2, jnp.concatenate([i_hi, none, i_lo, none], axis=0))
    odd = mm(raw2, jnp.concatenate([none, i_hi, none, i_lo], axis=0))
    evens, odds = [], []
    for q in range(count):
        rows = slice(q * half, (q + 1) * half)
        hi, lo = split2(jnp.concatenate([even[rows], odd[rows]], axis=0))
        rotated = mm(left, jnp.concatenate([hi, lo, hi], axis=0))
        hi, lo = split2(rotated * scale)
        again = mm(back, jnp.concatenate([hi, lo, hi], axis=0))
        evens.append(again[:half])
        odds.append(again[half:])
    total = None
    for rows, lower in ((evens, False), (odds, True)):
        hi, lo = split2(jnp.concatenate(rows, axis=0))
        w_hi = jnp.concatenate([none, i_hi] if lower else [i_hi, none], axis=0)
        w_lo = jnp.concatenate([none, i_lo] if lower else [i_lo, none], axis=0)
        term = mm_nt(hi, w_hi) + mm_nt(lo, w_hi) + mm_nt(hi, w_lo)
        total = term if total is None else total + term
    x_scr[...] = total
    per = chunks // SEGMENTS
    for c in range(per):
        piece = x_scr[pl.ds(c, count * SEGMENTS, stride=per), :].astype(BF16)
        sent_ref[:, c * LANES:(c + 1) * LANES] = piece
    for copy in copies[5:]:
        copy.wait()


def precondition(block_order, query_grads, out_basis, in_basis, eigenvalues, row_ids, train):
    blocks, qdev, width = query_grads.shape
    count = blocks * qdev
    side = out_basis.shape[1]
    vmem = pl.BlockSpec(memory_space=pltpu.VMEM)
    hbm = pl.BlockSpec(memory_space=pltpu.HBM)
    free = pl.BlockSpec(memory_space=pl.ANY)
    return pl.pallas_call(
        precondition_kernel,
        out_shape=(
            jax.ShapeDtypeStruct((count * SEGMENTS, width // SEGMENTS), BF16),
            jax.ShapeDtypeStruct(row_ids.shape, row_ids.dtype),
            jax.ShapeDtypeStruct(train.shape, train.dtype),
        ),
        in_specs=[hbm] * 7,
        out_specs=(vmem, free, free),
        scratch_shapes=[
            pltpu.SMEM(block_order.shape, block_order.dtype),
            pltpu.VMEM(query_grads.shape, BF16),
            pltpu.VMEM(out_basis.shape, F32),
            pltpu.VMEM(in_basis.shape, F32),
            pltpu.VMEM(eigenvalues.shape, F32),
            pltpu.VMEM((count * width // LANES, LANES), F32),
            pltpu.VMEM((side, LANES), F32),
            pltpu.VMEM((side, LANES), F32),
            pltpu.SemaphoreType.DMA((7,)),
        ],
        compiler_params=pltpu.CompilerParams(vmem_limit_bytes=4 * 2**20),
        name="precondition",
    )(*(
        pltpu.with_memory_space_constraint(x, pltpu.HBM)
        for x in (block_order, query_grads, out_basis, in_basis, eigenvalues, row_ids, train)
    ))


def split3(x):
    hi = x.astype(BF16)
    rest = x - hi.astype(F32)
    mid = rest.astype(BF16)
    return hi, mid, (rest - mid.astype(F32)).astype(BF16)


def scores_kernel(masks, flips, blocks, qdev, place_ref, train_ref, ids_ref, *refs):
    n_row = len(masks)
    parts, (mine_ref, other_ref, flat_scr, out_scr) = refs[:n_row], refs[n_row:]
    lines, seg = parts[0].shape
    rows = train_ref.shape[0]
    slot = 8
    per_seg = seg // LANES
    for b, part in enumerate(parts):
        flat = part[...].astype(F32)
        for c in range(per_seg):
            flat_scr[b, c, :lines, :] = flat[:, c * LANES:(c + 1) * LANES]
    terms = None
    for j in range(SEGMENTS):
        queries = jnp.concatenate([
            jnp.concatenate([flat_scr[b, c, pl.ds(j, slot, stride=SEGMENTS), :] for b in range(n_row)], axis=0)
            for c in range(per_seg)
        ], axis=1)
        term = mm_nt(queries.astype(BF16), train_ref[:, j * seg:(j + 1) * seg])
        terms = term if terms is None else terms + term
    here = lax.broadcasted_iota(jnp.int32, (rows, rows), 0)
    place = (here == ids_ref[...]).astype(BF16)
    a, b, c = split3(terms)
    ordered = mm(a, place) + mm(b, place) + mm(c, place)
    me, core, group = place_ref[0], place_ref[1], place_ref[2]
    per = n_row // 2
    for b, (mask, flip) in enumerate(zip(masks, flips)):
        source = me ^ mask ^ (group * flip)
        which = jnp.where(source // per == core, 0, 1)
        first = which * (blocks * per) + source % per
        for j in range(blocks):
            at = b * slot + j * qdev
            out_scr[first + j * per] = ordered[at:at + qdev]
    for i in range(blocks * per):
        mine_ref[i * qdev:(i + 1) * qdev, :] = out_scr[i]
        other_ref[i * qdev:(i + 1) * qdev, :] = out_scr[blocks * per + i]


def scores(masks, flips, place, train, row_ids, parts, blocks, qdev):
    rows = train.shape[0]
    n_row = len(masks)
    lines, seg = parts[0].shape
    out = jax.ShapeDtypeStruct((blocks * n_row * qdev // 2, rows), F32)
    vmem = pl.BlockSpec(memory_space=pltpu.VMEM)
    return pl.pallas_call(
        functools.partial(scores_kernel, masks, flips, blocks, qdev),
        out_shape=(out, out),
        in_specs=[pl.BlockSpec(memory_space=pltpu.SMEM)] + [vmem] * (2 + n_row),
        out_specs=(vmem, vmem),
        scratch_shapes=[
            pltpu.VMEM((n_row, seg // LANES, 8 * SEGMENTS, LANES), F32),
            pltpu.VMEM((blocks * n_row, qdev, rows), F32),
        ],
        compiler_params=pltpu.CompilerParams(vmem_limit_bytes=(16 if n_row <= 16 else 48) * 2**20),
        cost_estimate=pl.CostEstimate(flops=2 * n_row * 8 * rows * seg * SEGMENTS, bytes_accessed=train.size * 2 + n_row * lines * seg * 2, transcendentals=0),
        name="scores",
    )(place, train, row_ids, *parts)


def make_body(n_grp, n_row):
    def swap(x, mask, other_mask=None, cross=0):
        pairs = []
        for g in range(n_grp):
            for r in range(n_row):
                to = r ^ (mask if g == 0 or other_mask is None else other_mask)
                pairs.append((g * n_row + r, (g ^ cross) * n_row + to))
        return lax.ppermute(x, ("grp", "row"), pairs)

    def gather(own):
        if n_row != 8 or n_grp != 2:
            near = [(0, 0, own)] + [(m, 0, swap(own, m)) for m in range(2, n_row, 2)]
            return near + [(m ^ 1, 0, swap(x, 1)) for m, _, x in near]
        far = {m: swap(own, m) for m in (4, 6)}
        parts = [(0, 0, own)] + [(m, 0, swap(own, m)) for m in (3, 1, 2)]
        parts += [(m, 0, x) for m, x in far.items()]
        parts += [(m ^ 1, 0, swap(x, 1)) for m, x in far.items()]
        return parts

    def body(train_grads, query_grads, out_basis, in_basis, eigenvalues, block_order, row_ids):
        blocks, qdev, _, width = query_grads.shape
        rows = train_grads.shape[0]
        own, row_ids, train = precondition(
            block_order, query_grads.reshape(blocks, qdev, width), out_basis, in_basis, eigenvalues, row_ids,
            train_grads.reshape(rows, width),
        )
        masks, flips, parts = zip(*gather(own))
        place = jnp.stack([lax.axis_index(name) for name in ("row", "layer", "grp")]).astype(jnp.int32)
        mine, other = scores(masks, flips, place, train, row_ids, parts, blocks, qdev)
        got = lax.ppermute(other, "layer", [(0, 1), (1, 0)])
        total = (mine + got).astype(BF16)
        return total.reshape(blocks, -1, rows).transpose(0, 2, 1)

    return body


def solution(mesh):
    in_specs = (
        P(("grp", "row"), "layer", None),
        P(None, "row", "layer", None),
        P("layer", None, None),
        P("layer", None, None),
        P("layer", None),
        P(),
        P(("grp", "row"), None),
    )
    out_specs = P(None, ("grp", "row"), "layer")
    body = make_body(mesh.shape["grp"], mesh.shape["row"])
    return jax.shard_map(body, mesh=mesh, in_specs=in_specs, out_specs=out_specs, check_vma=False)
```

```python
import functools

import jax
import jax.numpy as jnp
from jax import lax
from jax.experimental import pallas as pl
from jax.experimental.pallas import tpu as pltpu
from jax.sharding import PartitionSpec as P

DAMPING = 0.01
LANES = 128
SEGMENTS = 4
SLOT = 8
F32, BF16 = jnp.float32, jnp.bfloat16
NT = (((1,), (1,)), ((), ()))


def split2(x):
    high = x.astype(BF16)
    return high, (x - high.astype(F32)).astype(BF16)


def mm(a, b):
    return jnp.dot(a, b, preferred_element_type=F32)


def mm_nt(a, b):
    return lax.dot_general(a, b, NT, preferred_element_type=F32)


def precondition_kernel(
    order_hbm, q_hbm, out_basis_hbm, in_basis_hbm, eig_hbm, ids_hbm, train_hbm,
    sent_ref, ids_out_ref, train_out_ref,
    order_ref, q_ref, out_basis_ref, in_basis_ref, eig_ref, x_scr, o_scr, eig_scr, sems,
):
    copies = [
        pltpu.make_async_copy(src, dst, sems.at[n])
        for n, (src, dst) in enumerate((
            (order_hbm, order_ref), (q_hbm, q_ref), (in_basis_hbm, in_basis_ref), (out_basis_hbm, out_basis_ref), (eig_hbm, eig_ref),
            (ids_hbm, ids_out_ref), (train_hbm, train_out_ref),
        ))
    ]
    for copy in copies:
        copy.start()
    for copy in copies[:5]:
        copy.wait()
    blocks, qdev, width = q_ref.shape
    side = out_basis_ref.shape[1]
    half = side // 2
    count = blocks * qdev
    chunks = width // LANES
    for j in range(blocks):
        flat = q_ref[order_ref[j]].astype(F32)
        for k in range(chunks):
            x_scr[pl.ds(j * qdev * chunks + k, qdev, stride=chunks), :] = flat[:, k * LANES:(k + 1) * LANES]
    scale = 1.0 / (eig_ref[...] + DAMPING)
    for k in range(chunks):
        for odd in range(2):
            at = k * LANES + odd * side
            eig_scr[2 * k + odd:2 * k + odd + 1, :side] = scale[:, at:at + side]
    scale = eig_scr[:, :side]
    o_scr[:, :side] = out_basis_ref[0]
    basis = jnp.concatenate(
        [o_scr[pl.ds(0, half, stride=2), :side], o_scr[pl.ds(1, half, stride=2), :side]], axis=0
    )
    b_hi, b_lo = split2(basis)
    t_hi, t_lo = split2(basis.T)
    left = jnp.concatenate([t_hi, t_hi, t_lo], axis=1)
    back = jnp.concatenate([b_hi, b_hi, b_lo], axis=1)
    i_hi, i_lo = split2(in_basis_ref[0])
    none = jnp.zeros_like(i_hi)
    raw = x_scr[...].astype(BF16)
    raw2 = jnp.concatenate([raw, raw], axis=1)
    even = mm(raw2, jnp.concatenate([i_hi, none, i_lo, none], axis=0))
    odd = mm(raw2, jnp.concatenate([none, i_hi, none, i_lo], axis=0))
    evens, odds = [], []
    for q in range(count):
        rows = slice(q * half, (q + 1) * half)
        hi, lo = split2(jnp.concatenate([even[rows], odd[rows]], axis=0))
        rotated = mm(left, jnp.concatenate([hi, lo, hi], axis=0))
        hi, lo = split2(rotated * scale)
        again = mm(back, jnp.concatenate([hi, lo, hi], axis=0))
        evens.append(again[:half])
        odds.append(again[half:])
    total = None
    for rows, lower in ((evens, False), (odds, True)):
        hi, lo = split2(jnp.concatenate(rows, axis=0))
        w_hi = jnp.concatenate([none, i_hi] if lower else [i_hi, none], axis=0)
        w_lo = jnp.concatenate([none, i_lo] if lower else [i_lo, none], axis=0)
        term = mm_nt(hi, w_hi) + mm_nt(lo, w_hi) + mm_nt(hi, w_lo)
        total = term if total is None else total + term
    x_scr[...] = total
    per = chunks // SEGMENTS
    for c in range(per):
        piece = x_scr[pl.ds(c, count * SEGMENTS, stride=per), :].astype(BF16)
        sent_ref[:, c * LANES:(c + 1) * LANES] = piece
    for copy in copies[5:]:
        copy.wait()


def precondition(block_order, query_grads, out_basis, in_basis, eigenvalues, row_ids, train):
    blocks, qdev, width = query_grads.shape
    count = blocks * qdev
    side = out_basis.shape[1]
    vmem = pl.BlockSpec(memory_space=pltpu.VMEM)
    hbm = pl.BlockSpec(memory_space=pltpu.HBM)
    free = pl.BlockSpec(memory_space=pl.ANY)
    return pl.pallas_call(
        precondition_kernel,
        out_shape=(
            jax.ShapeDtypeStruct((count * SEGMENTS, width // SEGMENTS), BF16),
            jax.ShapeDtypeStruct(row_ids.shape, row_ids.dtype),
            jax.ShapeDtypeStruct(train.shape, train.dtype),
        ),
        in_specs=[hbm] * 7,
        out_specs=(vmem, free, free),
        scratch_shapes=[
            pltpu.SMEM(block_order.shape, block_order.dtype),
            pltpu.VMEM(query_grads.shape, BF16),
            pltpu.VMEM(out_basis.shape, F32),
            pltpu.VMEM(in_basis.shape, F32),
            pltpu.VMEM(eigenvalues.shape, F32),
            pltpu.VMEM((count * width // LANES, LANES), F32),
            pltpu.VMEM((side, LANES), F32),
            pltpu.VMEM((side, LANES), F32),
            pltpu.SemaphoreType.DMA((7,)),
        ],
        compiler_params=pltpu.CompilerParams(vmem_limit_bytes=4 * 2**20),
        name="precondition",
    )(*(
        pltpu.with_memory_space_constraint(x, pltpu.HBM)
        for x in (block_order, query_grads, out_basis, in_basis, eigenvalues, row_ids, train)
    ))


def split3(x):
    hi = x.astype(BF16)
    rest = x - hi.astype(F32)
    mid = rest.astype(BF16)
    return hi, mid, (rest - mid.astype(F32)).astype(BF16)


def placed_terms(parts, train_ref, place, flat_scr):
    lines, seg = parts[0].shape
    per_seg = seg // LANES
    for b, part in enumerate(parts):
        flat = part[...].astype(F32)
        for c in range(per_seg):
            flat_scr[b, c, :lines, :] = flat[:, c * LANES:(c + 1) * LANES]
    terms = None
    for j in range(SEGMENTS):
        queries = jnp.concatenate([
            jnp.concatenate([flat_scr[b, c, pl.ds(j, SLOT, stride=SEGMENTS), :] for b in range(len(parts))], axis=0)
            for c in range(per_seg)
        ], axis=1)
        term = mm_nt(queries.astype(BF16), train_ref[:, j * seg:(j + 1) * seg])
        terms = term if terms is None else terms + term
    a, b, c = split3(terms)
    return mm(a, place) + mm(b, place) + mm(c, place)


def early_kernel(train_ref, ids_ref, *refs):
    parts, (terms_ref, place_ref, flat_scr) = refs[:-3], refs[-3:]
    rows = train_ref.shape[0]
    here = lax.broadcasted_iota(jnp.int32, (rows, rows), 0)
    place = (here == ids_ref[...]).astype(BF16)
    place_ref[...] = place
    terms_ref[...] = placed_terms(parts, train_ref, place, flat_scr)


def late_kernel(masks, blocks, qdev, where_ref, train_ref, place_ref, early_ref, *refs):
    parts, (mine_ref, other_ref, flat_scr, out_scr) = refs[:-4], refs[-4:]
    n_row = len(masks)
    ordered = jnp.concatenate(
        [early_ref[...], placed_terms(parts, train_ref, place_ref[...], flat_scr)], axis=0
    )
    me, core = where_ref[0], where_ref[1]
    per = n_row // 2
    for b, mask in enumerate(masks):
        source = me ^ mask
        which = jnp.where(source // per == core, 0, 1)
        first = which * (blocks * per) + source % per
        for j in range(blocks):
            at = b * SLOT + j * qdev
            out_scr[first + j * per] = ordered[at:at + qdev]
    for i in range(blocks * per):
        mine_ref[i * qdev:(i + 1) * qdev, :] = out_scr[i]
        other_ref[i * qdev:(i + 1) * qdev, :] = out_scr[blocks * per + i]


def scores(masks, early, where, train, row_ids, parts, blocks, qdev):
    rows, width = train.shape
    n_row = len(masks)
    lines, seg = parts[0].shape
    vmem = pl.BlockSpec(memory_space=pltpu.VMEM)
    params = pltpu.CompilerParams(vmem_limit_bytes=(16 if n_row <= 16 else 24) * 2**20)

    def flat(count):
        return pltpu.VMEM((count, seg // LANES, SLOT * SEGMENTS, LANES), F32)

    def cost(count):
        return pl.CostEstimate(
            flops=2 * count * SLOT * rows * width, bytes_accessed=2 * (rows * width + count * lines * seg),
            transcendentals=0,
        )

    terms, place = pl.pallas_call(
        early_kernel,
        out_shape=(
            jax.ShapeDtypeStruct((early * SLOT, rows), F32),
            jax.ShapeDtypeStruct((rows, rows), BF16),
        ),
        in_specs=[vmem] * (2 + early),
        out_specs=(vmem, vmem),
        scratch_shapes=[flat(early)],
        compiler_params=params,
        cost_estimate=cost(early),
        name="scores_early",
    )(train, row_ids, *parts[:early])
    late = n_row - early
    out = jax.ShapeDtypeStruct((blocks * n_row * qdev // 2, rows), F32)
    return pl.pallas_call(
        functools.partial(late_kernel, masks, blocks, qdev),
        out_shape=(out, out),
        in_specs=[pl.BlockSpec(memory_space=pltpu.SMEM)] + [vmem] * (3 + late),
        out_specs=(vmem, vmem),
        scratch_shapes=[flat(late), pltpu.VMEM((blocks * n_row, qdev, rows), F32)],
        compiler_params=params,
        cost_estimate=cost(late),
        name="scores_late",
    )(where, train, place, terms, *parts[early:])


def make_body(n_row):
    def swap(x, mask):
        return lax.ppermute(x, "row", [(r, r ^ mask) for r in range(n_row)])

    def gather(own):
        if n_row != 8:
            near = {0: own, **{m: swap(own, m) for m in range(2, n_row, 2)}}
            return {**near, **{m ^ 1: swap(x, 1) for m, x in near.items()}}, n_row // 2
        far = {m: swap(own, m) for m in (6, 4)}
        diagonal = {3: swap(own, 3)}
        near = {m: swap(own, m) for m in (2, 1)}
        return {0: own, **near, **far, **diagonal, **{m ^ 1: swap(x, 1) for m, x in far.items()}}, 5

    def body(train_grads, query_grads, out_basis, in_basis, eigenvalues, block_order, row_ids):
        blocks, qdev, _, width = query_grads.shape
        rows = train_grads.shape[0]
        own, row_ids, train = precondition(
            block_order, query_grads.reshape(blocks, qdev, width), out_basis, in_basis, eigenvalues, row_ids,
            train_grads.reshape(rows, width),
        )
        parts, early = gather(own)
        where = jnp.stack([lax.axis_index(name) for name in ("row", "layer")]).astype(jnp.int32)
        mine, other = scores(
            tuple(parts), early, where, train, row_ids, tuple(parts.values()), blocks, qdev
        )
        got = lax.ppermute(other, "layer", [(0, 1), (1, 0)])
        total = (mine + got).astype(BF16)
        return total.reshape(blocks, -1, rows).transpose(0, 2, 1)

    return body


def solution(mesh):
    in_specs = (
        P(("grp", "row"), "layer", None),
        P(None, "row", "layer", None),
        P("layer", None, None),
        P("layer", None, None),
        P("layer", None),
        P(),
        P(("grp", "row"), None),
    )
    out_specs = P(None, ("grp", "row"), "layer")
    body = make_body(mesh.shape["row"])
    return jax.shard_map(body, mesh=mesh, in_specs=in_specs, out_specs=out_specs, check_vma=False)
```

```python
import functools

import jax
import jax.numpy as jnp
from jax import lax
from jax.experimental import pallas as pl
from jax.experimental.pallas import tpu as pltpu
from jax.sharding import PartitionSpec as P

DAMPING = 0.01
LANES = 128
SEGMENTS = 4
F32, BF16 = jnp.float32, jnp.bfloat16
NT = (((1,), (1,)), ((), ()))


def split2(x):
    high = x.astype(BF16)
    return high, (x - high.astype(F32)).astype(BF16)


def mm(a, b):
    return jnp.dot(a, b, preferred_element_type=F32)


def mm_nt(a, b):
    return lax.dot_general(a, b, NT, preferred_element_type=F32)


def precondition_kernel(
    order_hbm, q_hbm, out_basis_hbm, in_basis_hbm, eig_hbm, ids_hbm, train_hbm,
    sent_ref, ids_out_ref, train_out_ref,
    order_ref, q_ref, out_basis_ref, in_basis_ref, eig_ref, x_scr, o_scr, eig_scr, sems,
):
    copies = [
        pltpu.make_async_copy(src, dst, sems.at[n])
        for n, (src, dst) in enumerate((
            (order_hbm, order_ref), (q_hbm, q_ref), (in_basis_hbm, in_basis_ref), (out_basis_hbm, out_basis_ref), (eig_hbm, eig_ref),
            (ids_hbm, ids_out_ref), (train_hbm, train_out_ref),
        ))
    ]
    for copy in copies:
        copy.start()
    for copy in copies[:5]:
        copy.wait()
    blocks, qdev, width = q_ref.shape
    side = out_basis_ref.shape[1]
    half = side // 2
    count = blocks * qdev
    chunks = width // LANES
    for j in range(blocks):
        flat = q_ref[order_ref[j]].astype(F32)
        for k in range(chunks):
            x_scr[pl.ds(j * qdev * chunks + k, qdev, stride=chunks), :] = flat[:, k * LANES:(k + 1) * LANES]
    scale = 1.0 / (eig_ref[...] + DAMPING)
    for k in range(chunks):
        for odd in range(2):
            at = k * LANES + odd * side
            eig_scr[2 * k + odd:2 * k + odd + 1, :side] = scale[:, at:at + side]
    scale = eig_scr[:, :side]
    o_scr[:, :side] = out_basis_ref[0]
    basis = jnp.concatenate(
        [o_scr[pl.ds(0, half, stride=2), :side], o_scr[pl.ds(1, half, stride=2), :side]], axis=0
    )
    b_hi, b_lo = split2(basis)
    t_hi, t_lo = split2(basis.T)
    left = jnp.concatenate([t_hi, t_hi, t_lo], axis=1)
    back = jnp.concatenate([b_hi, b_hi, b_lo], axis=1)
    i_hi, i_lo = split2(in_basis_ref[0])
    none = jnp.zeros_like(i_hi)
    raw = x_scr[...].astype(BF16)
    raw2 = jnp.concatenate([raw, raw], axis=1)
    even = mm(raw2, jnp.concatenate([i_hi, none, i_lo, none], axis=0))
    odd = mm(raw2, jnp.concatenate([none, i_hi, none, i_lo], axis=0))
    evens, odds = [], []
    for q in range(count):
        rows = slice(q * half, (q + 1) * half)
        hi, lo = split2(jnp.concatenate([even[rows], odd[rows]], axis=0))
        rotated = mm(left, jnp.concatenate([hi, lo, hi], axis=0))
        hi, lo = split2(rotated * scale)
        again = mm(back, jnp.concatenate([hi, lo, hi], axis=0))
        evens.append(again[:half])
        odds.append(again[half:])
    total = None
    for rows, lower in ((evens, False), (odds, True)):
        hi, lo = split2(jnp.concatenate(rows, axis=0))
        w_hi = jnp.concatenate([none, i_hi] if lower else [i_hi, none], axis=0)
        w_lo = jnp.concatenate([none, i_lo] if lower else [i_lo, none], axis=0)
        term = mm_nt(hi, w_hi) + mm_nt(lo, w_hi) + mm_nt(hi, w_lo)
        total = term if total is None else total + term
    x_scr[...] = total
    per = chunks // SEGMENTS
    for c in range(per):
        piece = x_scr[pl.ds(c, count * SEGMENTS, stride=per), :].astype(BF16)
        sent_ref[:, c * LANES:(c + 1) * LANES] = piece
    for copy in copies[5:]:
        copy.wait()


def precondition(block_order, query_grads, out_basis, in_basis, eigenvalues, row_ids, train):
    blocks, qdev, width = query_grads.shape
    count = blocks * qdev
    side = out_basis.shape[1]
    vmem = pl.BlockSpec(memory_space=pltpu.VMEM)
    hbm = pl.BlockSpec(memory_space=pltpu.HBM)
    free = pl.BlockSpec(memory_space=pl.ANY)
    return pl.pallas_call(
        precondition_kernel,
        out_shape=(
            jax.ShapeDtypeStruct((count * SEGMENTS, width // SEGMENTS), BF16),
            jax.ShapeDtypeStruct(row_ids.shape, row_ids.dtype),
            jax.ShapeDtypeStruct(train.shape, train.dtype),
        ),
        in_specs=[hbm] * 7,
        out_specs=(vmem, free, free),
        scratch_shapes=[
            pltpu.SMEM(block_order.shape, block_order.dtype),
            pltpu.VMEM(query_grads.shape, BF16),
            pltpu.VMEM(out_basis.shape, F32),
            pltpu.VMEM(in_basis.shape, F32),
            pltpu.VMEM(eigenvalues.shape, F32),
            pltpu.VMEM((count * width // LANES, LANES), F32),
            pltpu.VMEM((side, LANES), F32),
            pltpu.VMEM((side, LANES), F32),
            pltpu.SemaphoreType.DMA((7,)),
        ],
        compiler_params=pltpu.CompilerParams(vmem_limit_bytes=4 * 2**20),
        name="precondition",
    )(*(
        pltpu.with_memory_space_constraint(x, pltpu.HBM)
        for x in (block_order, query_grads, out_basis, in_basis, eigenvalues, row_ids, train)
    ))


def split3(x):
    hi = x.astype(BF16)
    rest = x - hi.astype(F32)
    mid = rest.astype(BF16)
    return hi, mid, (rest - mid.astype(F32)).astype(BF16)


def slot_of(where_ref, n_row, mask):
    source, per = where_ref[0] ^ mask, n_row // 2
    return jnp.where(source // per == where_ref[1], 0, per) + source % per


def placed_terms(where_ref, masks, parts, train_ref, place, flat_scr):
    lines, seg = parts[0].shape
    n_row = len(masks)
    per_seg = seg // LANES
    for b, mask in enumerate(masks):
        at = pl.ds(pl.multiple_of(slot_of(where_ref, n_row, mask) * lines, lines), lines)
        flat = parts[b][...].astype(F32) if b < len(parts) else jnp.zeros((lines, seg), F32)
        for c in range(per_seg):
            flat_scr[c, at, :] = flat[:, c * LANES:(c + 1) * LANES]
    terms = None
    for j in range(SEGMENTS):
        queries = jnp.concatenate([
            jnp.concatenate(
                [flat_scr[c, pl.ds(t + j, n_row, stride=lines), :] for t in range(0, lines, SEGMENTS)], axis=0
            )
            for c in range(per_seg)
        ], axis=1)
        term = mm_nt(queries.astype(BF16), train_ref[:, j * seg:(j + 1) * seg])
        terms = term if terms is None else terms + term
    a, b, c = split3(terms)
    return mm(a, place) + mm(b, place) + mm(c, place)


def early_kernel(masks, where_ref, train_ref, ids_ref, *refs):
    parts, (terms_ref, place_ref, flat_scr) = refs[:-3], refs[-3:]
    rows = train_ref.shape[0]
    here = lax.broadcasted_iota(jnp.int32, (rows, rows), 0)
    place = (here == ids_ref[...]).astype(BF16)
    place_ref[...] = place
    terms_ref[...] = placed_terms(where_ref, masks, parts, train_ref, place, flat_scr)


def late_kernel(masks, blocks, qdev, where_ref, train_ref, place_ref, early_ref, *refs):
    parts, (mine_ref, other_ref, flat_scr, out_scr) = refs[:-4], refs[-4:]
    n_row = len(masks)
    per = n_row // 2
    terms = early_ref[...] + placed_terms(where_ref, masks, parts, train_ref, place_ref[...], flat_scr)
    halves = terms.shape[1] // LANES
    half_rows = blocks * per * qdev
    for q in range(blocks * qdev):
        for which in range(2):
            first = which * half_rows + (q // qdev) * per * qdev + q % qdev
            at = q * n_row + which * per
            for h in range(halves):
                out_scr[h, pl.ds(first, per, stride=qdev), :] = terms[at:at + per, h * LANES:(h + 1) * LANES]
    for h in range(halves):
        mine_ref[:, h * LANES:(h + 1) * LANES] = out_scr[h, :half_rows]
        other_ref[:, h * LANES:(h + 1) * LANES] = out_scr[h, half_rows:]


def scores(masks, early, where, train, row_ids, parts, blocks, qdev):
    rows, width = train.shape
    n_row = len(masks)
    lines, seg = parts[0].shape
    queries = blocks * n_row * qdev
    vmem = pl.BlockSpec(memory_space=pltpu.VMEM)
    smem = pl.BlockSpec(memory_space=pltpu.SMEM)
    params = pltpu.CompilerParams(vmem_limit_bytes=(16 if n_row <= 16 else 40) * 2**20)
    cost = pl.CostEstimate(
        flops=2 * queries * rows * width, bytes_accessed=2 * (rows * width + n_row * lines * seg // 2),
        transcendentals=0,
    )
    flat_scr = pltpu.VMEM((seg // LANES, n_row * lines, LANES), F32)
    terms, place = pl.pallas_call(
        functools.partial(early_kernel, masks),
        out_shape=(
            jax.ShapeDtypeStruct((queries, rows), F32),
            jax.ShapeDtypeStruct((rows, rows), BF16),
        ),
        in_specs=[smem] + [vmem] * (2 + early),
        out_specs=(vmem, vmem),
        scratch_shapes=[flat_scr],
        compiler_params=params,
        cost_estimate=cost,
        name="scores_early",
    )(where, train, row_ids, *parts[:early])
    out = jax.ShapeDtypeStruct((queries // 2, rows), F32)
    return pl.pallas_call(
        functools.partial(late_kernel, masks[early:] + masks[:early], blocks, qdev),
        out_shape=(out, out),
        in_specs=[smem] + [vmem] * (3 + n_row - early),
        out_specs=(vmem, vmem),
        scratch_shapes=[flat_scr, pltpu.VMEM((rows // LANES, queries, LANES), F32)],
        compiler_params=params,
        cost_estimate=cost,
        name="scores_late",
    )(where, train, place, terms, *parts[early:])


def make_body(n_row):
    def swap(x, mask):
        return lax.ppermute(x, "row", [(r, r ^ mask) for r in range(n_row)])

    def gather(own):
        if n_row != 8:
            near = {0: own, **{m: swap(own, m) for m in range(2, n_row, 2)}}
            return {**near, **{m ^ 1: swap(x, 1) for m, x in near.items()}}, n_row // 2
        far = {m: swap(own, m) for m in (6, 4)}
        diagonal = {3: swap(own, 3)}
        near = {m: swap(own, m) for m in (2, 1)}
        return {0: own, **near, **far, **diagonal, **{m ^ 1: swap(x, 1) for m, x in far.items()}}, 5

    def body(train_grads, query_grads, out_basis, in_basis, eigenvalues, block_order, row_ids):
        blocks, qdev, _, width = query_grads.shape
        rows = train_grads.shape[0]
        own, row_ids, train = precondition(
            block_order, query_grads.reshape(blocks, qdev, width), out_basis, in_basis, eigenvalues, row_ids,
            train_grads.reshape(rows, width),
        )
        parts, early = gather(own)
        where = jnp.stack([lax.axis_index(name) for name in ("row", "layer")]).astype(jnp.int32)
        mine, other = scores(
            tuple(parts), early, where, train, row_ids, tuple(parts.values()), blocks, qdev
        )
        got = lax.ppermute(other, "layer", [(0, 1), (1, 0)])
        total = (mine + got).astype(BF16)
        return total.reshape(blocks, -1, rows).transpose(0, 2, 1)

    return body


def solution(mesh):
    in_specs = (
        P(("grp", "row"), "layer", None),
        P(None, "row", "layer", None),
        P("layer", None, None),
        P("layer", None, None),
        P("layer", None),
        P(),
        P(("grp", "row"), None),
    )
    out_specs = P(None, ("grp", "row"), "layer")
    body = make_body(mesh.shape["row"])
    return jax.shard_map(body, mesh=mesh, in_specs=in_specs, out_specs=out_specs, check_vma=False)
```

```python
import functools

import jax
import jax.numpy as jnp
from jax import lax
from jax.experimental import pallas as pl
from jax.experimental.pallas import tpu as pltpu
from jax.sharding import PartitionSpec as P

DAMPING = 0.01
LANES = 128
SEGMENTS = 4
F32, BF16 = jnp.float32, jnp.bfloat16
NT = (((1,), (1,)), ((), ()))


def split2(x):
    high = x.astype(BF16)
    return high, (x - high.astype(F32)).astype(BF16)


def mm(a, b):
    return jnp.dot(a, b, preferred_element_type=F32)


def mm_nt(a, b):
    return lax.dot_general(a, b, NT, preferred_element_type=F32)


def precondition_kernel(
    order_hbm, q_hbm, out_basis_hbm, in_basis_hbm, eig_hbm, ids_hbm, train_hbm,
    sent_ref, ids_out_ref, train_out_ref,
    order_ref, q_ref, out_basis_ref, in_basis_ref, eig_ref, x_scr, o_scr, eig_scr, sems,
):
    copies = [
        pltpu.make_async_copy(src, dst, sems.at[n])
        for n, (src, dst) in enumerate((
            (order_hbm, order_ref), (q_hbm, q_ref), (in_basis_hbm, in_basis_ref), (out_basis_hbm, out_basis_ref), (eig_hbm, eig_ref),
            (ids_hbm, ids_out_ref), (train_hbm, train_out_ref),
        ))
    ]
    for copy in copies:
        copy.start()
    for copy in copies[:5]:
        copy.wait()
    blocks, qdev, width = q_ref.shape
    side = out_basis_ref.shape[1]
    half = side // 2
    count = blocks * qdev
    chunks = width // LANES
    for j in range(blocks):
        flat = q_ref[order_ref[j]].astype(F32)
        for k in range(chunks):
            x_scr[pl.ds(j * qdev * chunks + k, qdev, stride=chunks), :] = flat[:, k * LANES:(k + 1) * LANES]
    scale = 1.0 / (eig_ref[...] + DAMPING)
    for k in range(chunks):
        for odd in range(2):
            at = k * LANES + odd * side
            eig_scr[2 * k + odd:2 * k + odd + 1, :side] = scale[:, at:at + side]
    scale = eig_scr[:, :side]
    o_scr[:, :side] = out_basis_ref[0]
    basis = jnp.concatenate(
        [o_scr[pl.ds(0, half, stride=2), :side], o_scr[pl.ds(1, half, stride=2), :side]], axis=0
    )
    b_hi, b_lo = split2(basis)
    t_hi, t_lo = split2(basis.T)
    left = jnp.concatenate([t_hi, t_hi, t_lo], axis=1)
    back = jnp.concatenate([b_hi, b_hi, b_lo], axis=1)
    i_hi, i_lo = split2(in_basis_ref[0])
    none = jnp.zeros_like(i_hi)
    raw = x_scr[...].astype(BF16)
    raw2 = jnp.concatenate([raw, raw], axis=1)
    even = mm(raw2, jnp.concatenate([i_hi, none, i_lo, none], axis=0))
    odd = mm(raw2, jnp.concatenate([none, i_hi, none, i_lo], axis=0))
    evens, odds = [], []
    for q in range(count):
        rows = slice(q * half, (q + 1) * half)
        hi, lo = split2(jnp.concatenate([even[rows], odd[rows]], axis=0))
        rotated = mm(left, jnp.concatenate([hi, lo, hi], axis=0))
        hi, lo = split2(rotated * scale)
        again = mm(back, jnp.concatenate([hi, lo, hi], axis=0))
        evens.append(again[:half])
        odds.append(again[half:])
    total = None
    for rows, lower in ((evens, False), (odds, True)):
        hi, lo = split2(jnp.concatenate(rows, axis=0))
        w_hi = jnp.concatenate([none, i_hi] if lower else [i_hi, none], axis=0)
        w_lo = jnp.concatenate([none, i_lo] if lower else [i_lo, none], axis=0)
        term = mm_nt(hi, w_hi) + mm_nt(lo, w_hi) + mm_nt(hi, w_lo)
        total = term if total is None else total + term
    x_scr[...] = total
    per = chunks // SEGMENTS
    for c in range(per):
        piece = x_scr[pl.ds(c, count * SEGMENTS, stride=per), :].astype(BF16)
        sent_ref[:, c * LANES:(c + 1) * LANES] = piece
    for copy in copies[5:]:
        copy.wait()


def precondition(block_order, query_grads, out_basis, in_basis, eigenvalues, row_ids, train):
    blocks, qdev, width = query_grads.shape
    count = blocks * qdev
    side = out_basis.shape[1]
    vmem = pl.BlockSpec(memory_space=pltpu.VMEM)
    hbm = pl.BlockSpec(memory_space=pltpu.HBM)
    free = pl.BlockSpec(memory_space=pl.ANY)
    return pl.pallas_call(
        precondition_kernel,
        out_shape=(
            jax.ShapeDtypeStruct((count * SEGMENTS, width // SEGMENTS), BF16),
            jax.ShapeDtypeStruct(row_ids.shape, row_ids.dtype),
            jax.ShapeDtypeStruct(train.shape, train.dtype),
        ),
        in_specs=[hbm] * 7,
        out_specs=(vmem, free, free),
        scratch_shapes=[
            pltpu.SMEM(block_order.shape, block_order.dtype),
            pltpu.VMEM(query_grads.shape, BF16),
            pltpu.VMEM(out_basis.shape, F32),
            pltpu.VMEM(in_basis.shape, F32),
            pltpu.VMEM(eigenvalues.shape, F32),
            pltpu.VMEM((count * width // LANES, LANES), F32),
            pltpu.VMEM((side, LANES), F32),
            pltpu.VMEM((side, LANES), F32),
            pltpu.SemaphoreType.DMA((7,)),
        ],
        compiler_params=pltpu.CompilerParams(vmem_limit_bytes=4 * 2**20),
        name="precondition",
    )(*(
        pltpu.with_memory_space_constraint(x, pltpu.HBM)
        for x in (block_order, query_grads, out_basis, in_basis, eigenvalues, row_ids, train)
    ))


def split3(x):
    hi = x.astype(BF16)
    rest = x - hi.astype(F32)
    mid = rest.astype(BF16)
    return hi, mid, (rest - mid.astype(F32)).astype(BF16)


def slot_of(n_row, mask):
    source, per = lax.axis_index("row") ^ mask, n_row // 2
    return source ^ (lax.axis_index("layer") * per)


def placed_terms(masks, parts, train_ref, place, flat_scr):
    lines, seg = parts[0].shape
    n_row = len(masks)
    per_seg = seg // LANES
    for b, mask in enumerate(masks):
        at = pl.ds(pl.multiple_of(slot_of(n_row, mask) * lines, lines), lines)
        flat = parts[b][...].astype(F32) if b < len(parts) else jnp.zeros((lines, seg), F32)
        for c in range(per_seg):
            flat_scr[c, at, :] = flat[:, c * LANES:(c + 1) * LANES]
    terms = None
    for j in range(SEGMENTS):
        queries = jnp.concatenate([
            jnp.concatenate(
                [flat_scr[c, pl.ds(t + j, n_row, stride=lines), :] for t in range(0, lines, SEGMENTS)], axis=0
            )
            for c in range(per_seg)
        ], axis=1)
        term = mm_nt(queries.astype(BF16), train_ref[:, j * seg:(j + 1) * seg])
        terms = term if terms is None else terms + term
    a, b, c = split3(terms)
    return mm(a, place) + mm(b, place) + mm(c, place)


def early_kernel(masks, train_ref, ids_ref, *refs):
    parts, (terms_ref, place_ref, flat_scr) = refs[:-3], refs[-3:]
    rows = train_ref.shape[0]
    here = lax.broadcasted_iota(jnp.int32, (rows, rows), 0)
    place = (here == ids_ref[...]).astype(BF16)
    place_ref[...] = place
    terms_ref[...] = placed_terms(masks, parts, train_ref, place, flat_scr)


def late_kernel(masks, blocks, qdev, train_ref, place_ref, early_ref, *refs):
    parts, (mine_ref, other_ref, flat_scr, out_scr) = refs[:-4], refs[-4:]
    n_row = len(masks)
    per = n_row // 2
    terms = early_ref[...] + placed_terms(masks, parts, train_ref, place_ref[...], flat_scr)
    halves = terms.shape[1] // LANES
    half_rows = blocks * per * qdev
    for q in range(blocks * qdev):
        for which in range(2):
            first = which * half_rows + (q // qdev) * per * qdev + q % qdev
            at = q * n_row + which * per
            for h in range(halves):
                out_scr[h, pl.ds(first, per, stride=qdev), :] = terms[at:at + per, h * LANES:(h + 1) * LANES]
    for h in range(halves):
        mine_ref[:, h * LANES:(h + 1) * LANES] = out_scr[h, :half_rows]
        other_ref[:, h * LANES:(h + 1) * LANES] = out_scr[h, half_rows:]


def scores(masks, early, train, row_ids, parts, blocks, qdev):
    rows, width = train.shape
    n_row = len(masks)
    lines, seg = parts[0].shape
    queries = blocks * n_row * qdev
    vmem = pl.BlockSpec(memory_space=pltpu.VMEM)
    params = pltpu.CompilerParams(vmem_limit_bytes=(16 if n_row <= 16 else 40) * 2**20)
    cost = pl.CostEstimate(
        flops=2 * queries * rows * width, bytes_accessed=2 * (rows * width + n_row * lines * seg // 2),
        transcendentals=0,
    )
    flat_scr = pltpu.VMEM((seg // LANES, n_row * lines, LANES), F32)
    terms, place = pl.pallas_call(
        functools.partial(early_kernel, masks),
        out_shape=(
            jax.ShapeDtypeStruct((queries, rows), F32),
            jax.ShapeDtypeStruct((rows, rows), BF16),
        ),
        in_specs=[vmem] * (2 + early),
        out_specs=(vmem, vmem),
        scratch_shapes=[flat_scr],
        compiler_params=params,
        cost_estimate=cost,
        name="scores_early",
    )(train, row_ids, *parts[:early])
    out = jax.ShapeDtypeStruct((queries // 2, rows), F32)
    return pl.pallas_call(
        functools.partial(late_kernel, masks[early:] + masks[:early], blocks, qdev),
        out_shape=(out, out),
        in_specs=[vmem] * (3 + n_row - early),
        out_specs=(vmem, vmem),
        scratch_shapes=[flat_scr, pltpu.VMEM((rows // LANES, queries, LANES), F32)],
        compiler_params=params,
        cost_estimate=cost,
        name="scores_late",
    )(train, place, terms, *parts[early:])


def make_body(n_row):
    def swap(x, mask):
        return lax.ppermute(x, "row", [(r, r ^ mask) for r in range(n_row)])

    def gather(own):
        if n_row != 8:
            near = {0: own, **{m: swap(own, m) for m in range(2, n_row, 2)}}
            return {**near, **{m ^ 1: swap(x, 1) for m, x in near.items()}}, n_row // 2
        far = {m: swap(own, m) for m in (6, 4)}
        diagonal = {3: swap(own, 3)}
        near = {m: swap(own, m) for m in (2, 1)}
        return {0: own, **near, **far, **diagonal, **{m ^ 1: swap(x, 1) for m, x in far.items()}}, 5

    def body(train_grads, query_grads, out_basis, in_basis, eigenvalues, block_order, row_ids):
        blocks, qdev, _, width = query_grads.shape
        rows = train_grads.shape[0]
        own, row_ids, train = precondition(
            block_order, query_grads.reshape(blocks, qdev, width), out_basis, in_basis, eigenvalues, row_ids,
            train_grads.reshape(rows, width),
        )
        parts, early = gather(own)
        mine, other = scores(tuple(parts), early, train, row_ids, tuple(parts.values()), blocks, qdev)
        got = lax.ppermute(other, "layer", [(0, 1), (1, 0)])
        total = (mine + got).astype(BF16)
        return total.reshape(blocks, -1, rows).transpose(0, 2, 1)

    return body


def solution(mesh):
    in_specs = (
        P(("grp", "row"), "layer", None),
        P(None, "row", "layer", None),
        P("layer", None, None),
        P("layer", None, None),
        P("layer", None),
        P(),
        P(("grp", "row"), None),
    )
    out_specs = P(None, ("grp", "row"), "layer")
    body = make_body(mesh.shape["row"])
    return jax.shard_map(body, mesh=mesh, in_specs=in_specs, out_specs=out_specs, check_vma=False)
```

```python
import functools

import jax
import jax.numpy as jnp
from jax import lax
from jax.experimental import pallas as pl
from jax.experimental.pallas import tpu as pltpu
from jax.sharding import PartitionSpec as P

DAMPING = 0.01
LANES = 128
SEGMENTS = 4
F32, BF16 = jnp.float32, jnp.bfloat16
NT = (((1,), (1,)), ((), ()))


def split2(x):
    high = x.astype(BF16)
    return high, (x - high.astype(F32)).astype(BF16)


def mm(a, b):
    return jnp.dot(a, b, preferred_element_type=F32)


def mm_nt(a, b):
    return lax.dot_general(a, b, NT, preferred_element_type=F32)


def precondition_kernel(
    order_hbm, q_hbm, out_basis_hbm, in_basis_hbm, eig_hbm, ids_hbm, train_hbm,
    sent_ref, ids_out_ref, train_out_ref,
    order_ref, q_ref, out_basis_ref, in_basis_ref, eig_ref, x_scr, o_scr, eig_scr, sems,
):
    copies = [
        pltpu.make_async_copy(src, dst, sems.at[n])
        for n, (src, dst) in enumerate((
            (order_hbm, order_ref), (q_hbm, q_ref), (in_basis_hbm, in_basis_ref), (out_basis_hbm, out_basis_ref), (eig_hbm, eig_ref),
            (ids_hbm, ids_out_ref), (train_hbm, train_out_ref),
        ))
    ]
    for copy in copies:
        copy.start()
    for copy in copies[:5]:
        copy.wait()
    blocks, qdev, width = q_ref.shape
    side = out_basis_ref.shape[1]
    half = side // 2
    count = blocks * qdev
    chunks = width // LANES
    for j in range(blocks):
        flat = q_ref[order_ref[j]].astype(F32)
        for k in range(chunks):
            x_scr[pl.ds(j * qdev * chunks + k, qdev, stride=chunks), :] = flat[:, k * LANES:(k + 1) * LANES]
    scale = 1.0 / (eig_ref[...] + DAMPING)
    for k in range(chunks):
        for odd in range(2):
            at = k * LANES + odd * side
            eig_scr[2 * k + odd:2 * k + odd + 1, :side] = scale[:, at:at + side]
    scale = eig_scr[:, :side]
    o_scr[:, :side] = out_basis_ref[0]
    basis = jnp.concatenate(
        [o_scr[pl.ds(0, half, stride=2), :side], o_scr[pl.ds(1, half, stride=2), :side]], axis=0
    )
    b_hi, b_lo = split2(basis)
    t_hi, t_lo = split2(basis.T)
    left = jnp.concatenate([t_hi, t_hi, t_lo], axis=1)
    back = jnp.concatenate([b_hi, b_hi, b_lo], axis=1)
    i_hi, i_lo = split2(in_basis_ref[0])
    none = jnp.zeros_like(i_hi)
    raw = x_scr[...].astype(BF16)
    raw2 = jnp.concatenate([raw, raw], axis=1)
    even = mm(raw2, jnp.concatenate([i_hi, none, i_lo, none], axis=0))
    odd = mm(raw2, jnp.concatenate([none, i_hi, none, i_lo], axis=0))
    evens, odds = [], []
    for q in range(count):
        rows = slice(q * half, (q + 1) * half)
        hi, lo = split2(jnp.concatenate([even[rows], odd[rows]], axis=0))
        rotated = mm(left, jnp.concatenate([hi, lo, hi], axis=0))
        hi, lo = split2(rotated * scale)
        again = mm(back, jnp.concatenate([hi, lo, hi], axis=0))
        evens.append(again[:half])
        odds.append(again[half:])
    total = None
    for rows, lower in ((evens, False), (odds, True)):
        hi, lo = split2(jnp.concatenate(rows, axis=0))
        w_hi = jnp.concatenate([none, i_hi] if lower else [i_hi, none], axis=0)
        w_lo = jnp.concatenate([none, i_lo] if lower else [i_lo, none], axis=0)
        term = mm_nt(hi, w_hi) + mm_nt(lo, w_hi) + mm_nt(hi, w_lo)
        total = term if total is None else total + term
    x_scr[...] = total
    per = chunks // SEGMENTS
    for c in range(per):
        piece = x_scr[pl.ds(c, count * SEGMENTS, stride=per), :].astype(BF16)
        sent_ref[:, c * LANES:(c + 1) * LANES] = piece
    for copy in copies[5:]:
        copy.wait()


def precondition(block_order, query_grads, out_basis, in_basis, eigenvalues, row_ids, train):
    blocks, qdev, width = query_grads.shape
    count = blocks * qdev
    side = out_basis.shape[1]
    vmem = pl.BlockSpec(memory_space=pltpu.VMEM)
    hbm = pl.BlockSpec(memory_space=pltpu.HBM)
    free = pl.BlockSpec(memory_space=pl.ANY)
    return pl.pallas_call(
        precondition_kernel,
        out_shape=(
            jax.ShapeDtypeStruct((count * SEGMENTS, width // SEGMENTS), BF16),
            jax.ShapeDtypeStruct(row_ids.shape, row_ids.dtype),
            jax.ShapeDtypeStruct(train.shape, train.dtype),
        ),
        in_specs=[hbm] * 7,
        out_specs=(vmem, free, free),
        scratch_shapes=[
            pltpu.SMEM(block_order.shape, block_order.dtype),
            pltpu.VMEM(query_grads.shape, BF16),
            pltpu.VMEM(out_basis.shape, F32),
            pltpu.VMEM(in_basis.shape, F32),
            pltpu.VMEM(eigenvalues.shape, F32),
            pltpu.VMEM((count * width // LANES, LANES), F32),
            pltpu.VMEM((side, LANES), F32),
            pltpu.VMEM((side, LANES), F32),
            pltpu.SemaphoreType.DMA((7,)),
        ],
        compiler_params=pltpu.CompilerParams(vmem_limit_bytes=4 * 2**20),
        name="precondition",
    )(*(
        pltpu.with_memory_space_constraint(x, pltpu.HBM)
        for x in (block_order, query_grads, out_basis, in_basis, eigenvalues, row_ids, train)
    ))


def split3(x):
    hi = x.astype(BF16)
    rest = x - hi.astype(F32)
    mid = rest.astype(BF16)
    return hi, mid, (rest - mid.astype(F32)).astype(BF16)


def slot_of(n_row, mask):
    source, per = lax.axis_index("row") ^ mask, n_row // 2
    return source ^ (lax.axis_index("layer") * per)


def placed_terms(masks, parts, train_ref, place, flat_scr):
    lines, seg = parts[0].shape
    n_row = len(masks)
    per_seg = seg // LANES
    for b, mask in enumerate(masks):
        at = pl.ds(pl.multiple_of(slot_of(n_row, mask) * lines, lines), lines)
        flat = parts[b][...].astype(F32) if b < len(parts) else jnp.zeros((lines, seg), F32)
        for c in range(per_seg):
            flat_scr[c, at, :] = flat[:, c * LANES:(c + 1) * LANES]
    terms = None
    for j in range(SEGMENTS):
        queries = jnp.concatenate([
            jnp.concatenate(
                [flat_scr[c, pl.ds(t + j, n_row, stride=lines), :] for t in range(0, lines, SEGMENTS)], axis=0
            )
            for c in range(per_seg)
        ], axis=1)
        term = mm_nt(queries.astype(BF16), train_ref[:, j * seg:(j + 1) * seg])
        terms = term if terms is None else terms + term
    a, b, c = split3(terms)
    return mm(a, place) + mm(b, place) + mm(c, place)


def early_kernel(masks, train_ref, ids_ref, *refs):
    parts, (terms_ref, place_ref, flat_scr) = refs[:-3], refs[-3:]
    rows = train_ref.shape[0]
    here = lax.broadcasted_iota(jnp.int32, (rows, rows), 0)
    place = (here == ids_ref[...]).astype(BF16)
    place_ref[...] = place
    terms_ref[...] = placed_terms(masks, parts, train_ref, place, flat_scr)


def late_kernel(masks, blocks, qdev, train_ref, place_ref, early_ref, *refs):
    parts, (mine_ref, other_ref, flat_scr, out_scr) = refs[:-4], refs[-4:]
    n_row = len(masks)
    per = n_row // 2
    terms = early_ref[...] + placed_terms(masks, parts, train_ref, place_ref[...], flat_scr)
    halves = terms.shape[1] // LANES
    half_rows = blocks * per * qdev
    for q in range(blocks * qdev):
        for which in range(2):
            first = which * half_rows + (q // qdev) * per * qdev + q % qdev
            at = q * n_row + which * per
            for h in range(halves):
                out_scr[h, pl.ds(first, per, stride=qdev), :] = terms[at:at + per, h * LANES:(h + 1) * LANES]
    for h in range(halves):
        mine_ref[:, h * LANES:(h + 1) * LANES] = out_scr[h, :half_rows]
        other_ref[:, h * LANES:(h + 1) * LANES] = out_scr[h, half_rows:]


def scores(masks, early, train, row_ids, parts, blocks, qdev):
    rows, width = train.shape
    n_row = len(masks)
    lines, seg = parts[0].shape
    queries = blocks * n_row * qdev
    vmem = pl.BlockSpec(memory_space=pltpu.VMEM)
    params = pltpu.CompilerParams(vmem_limit_bytes=(16 if n_row <= 16 else 40) * 2**20)
    cost = pl.CostEstimate(
        flops=2 * queries * rows * width, bytes_accessed=2 * (rows * width + n_row * lines * seg // 2),
        transcendentals=0,
    )
    flat_scr = pltpu.VMEM((seg // LANES, n_row * lines, LANES), F32)
    terms, place = pl.pallas_call(
        functools.partial(early_kernel, masks),
        out_shape=(
            jax.ShapeDtypeStruct((queries, rows), F32),
            jax.ShapeDtypeStruct((rows, rows), BF16),
        ),
        in_specs=[vmem] * (2 + early),
        out_specs=(vmem, vmem),
        scratch_shapes=[flat_scr],
        compiler_params=params,
        cost_estimate=cost,
        name="scores_early",
    )(train, row_ids, *parts[:early])
    out = jax.ShapeDtypeStruct((queries // 2, rows), F32)
    return pl.pallas_call(
        functools.partial(late_kernel, masks[early:] + masks[:early], blocks, qdev),
        out_shape=(out, out),
        in_specs=[vmem] * (3 + n_row - early),
        out_specs=(vmem, vmem),
        scratch_shapes=[flat_scr, pltpu.VMEM((rows // LANES, queries, LANES), F32)],
        compiler_params=params,
        cost_estimate=cost,
        name="scores_late",
    )(train, place, terms, *parts[early:])


def make_body(n_row):
    def swap(x, mask):
        return lax.ppermute(x, "row", [(r, r ^ mask) for r in range(n_row)])

    def gather(own):
        if n_row != 8:
            near = {0: own, **{m: swap(own, m) for m in range(2, n_row, 2)}}
            return {**near, **{m ^ 1: swap(x, 1) for m, x in near.items()}}, n_row // 2
        far = {m: swap(own, m) for m in (6, 4)}
        across = {m: swap(own, m) for m in (3, 1)}
        far[6], across[1] = lax.optimization_barrier((far[6], across[1]))
        near = {2: swap(own, 2)}
        return {0: own, **across, **far, **near, **{m ^ 1: swap(x, 1) for m, x in far.items()}}, 5

    def body(train_grads, query_grads, out_basis, in_basis, eigenvalues, block_order, row_ids):
        blocks, qdev, _, width = query_grads.shape
        rows = train_grads.shape[0]
        own, row_ids, train = precondition(
            block_order, query_grads.reshape(blocks, qdev, width), out_basis, in_basis, eigenvalues, row_ids,
            train_grads.reshape(rows, width),
        )
        parts, early = gather(own)
        mine, other = scores(tuple(parts), early, train, row_ids, tuple(parts.values()), blocks, qdev)
        got = lax.ppermute(other, "layer", [(0, 1), (1, 0)])
        total = (mine + got).astype(BF16)
        return total.reshape(blocks, -1, rows).transpose(0, 2, 1)

    return body


def solution(mesh):
    in_specs = (
        P(("grp", "row"), "layer", None),
        P(None, "row", "layer", None),
        P("layer", None, None),
        P("layer", None, None),
        P("layer", None),
        P(),
        P(("grp", "row"), None),
    )
    out_specs = P(None, ("grp", "row"), "layer")
    body = make_body(mesh.shape["row"])
    return jax.shard_map(body, mesh=mesh, in_specs=in_specs, out_specs=out_specs, check_vma=False)
```

```python
import functools

import jax
import jax.numpy as jnp
from jax import lax
from jax.experimental import pallas as pl
from jax.experimental.pallas import tpu as pltpu
from jax.sharding import PartitionSpec as P

DAMPING = 0.01
LANES = 128
SEGMENTS = 4
F32, BF16 = jnp.float32, jnp.bfloat16
NT = (((1,), (1,)), ((), ()))


def split2(x):
    high = x.astype(BF16)
    return high, (x - high.astype(F32)).astype(BF16)


def mm(a, b):
    return jnp.dot(a, b, preferred_element_type=F32)


def mm_nt(a, b):
    return lax.dot_general(a, b, NT, preferred_element_type=F32)


def precondition_kernel(
    order_hbm, q_hbm, out_basis_hbm, in_basis_hbm, eig_hbm, ids_hbm, train_hbm,
    sent_ref, ids_out_ref, train_out_ref,
    order_ref, q_ref, out_basis_ref, in_basis_ref, eig_ref, x_scr, o_scr, eig_scr, sems,
):
    copies = [
        pltpu.make_async_copy(src, dst, sems.at[n])
        for n, (src, dst) in enumerate((
            (order_hbm, order_ref), (q_hbm, q_ref), (in_basis_hbm, in_basis_ref), (out_basis_hbm, out_basis_ref), (eig_hbm, eig_ref),
            (ids_hbm, ids_out_ref), (train_hbm, train_out_ref),
        ))
    ]
    for copy in copies:
        copy.start()
    for copy in copies[:5]:
        copy.wait()
    blocks, qdev, width = q_ref.shape
    side = out_basis_ref.shape[1]
    half = side // 2
    count = blocks * qdev
    chunks = width // LANES
    for j in range(blocks):
        flat = q_ref[order_ref[j]].astype(F32)
        for k in range(chunks):
            x_scr[pl.ds(j * qdev * chunks + k, qdev, stride=chunks), :] = flat[:, k * LANES:(k + 1) * LANES]
    scale = 1.0 / (eig_ref[...] + DAMPING)
    for k in range(chunks):
        for odd in range(2):
            at = k * LANES + odd * side
            eig_scr[2 * k + odd:2 * k + odd + 1, :side] = scale[:, at:at + side]
    scale = eig_scr[:, :side]
    o_scr[:, :side] = out_basis_ref[0]
    basis = jnp.concatenate(
        [o_scr[pl.ds(0, half, stride=2), :side], o_scr[pl.ds(1, half, stride=2), :side]], axis=0
    )
    b_hi, b_lo = split2(basis)
    t_hi, t_lo = split2(basis.T)
    left = jnp.concatenate([t_hi, t_hi, t_lo], axis=1)
    back = jnp.concatenate([b_hi, b_hi, b_lo], axis=1)
    i_hi, i_lo = split2(in_basis_ref[0])
    none = jnp.zeros_like(i_hi)
    raw = x_scr[...].astype(BF16)
    raw2 = jnp.concatenate([raw, raw], axis=1)
    even = mm(raw2, jnp.concatenate([i_hi, none, i_lo, none], axis=0))
    odd = mm(raw2, jnp.concatenate([none, i_hi, none, i_lo], axis=0))
    evens, odds = [], []
    for q in range(count):
        rows = slice(q * half, (q + 1) * half)
        hi, lo = split2(jnp.concatenate([even[rows], odd[rows]], axis=0))
        rotated = mm(left, jnp.concatenate([hi, lo, hi], axis=0))
        hi, lo = split2(rotated * scale)
        again = mm(back, jnp.concatenate([hi, lo, hi], axis=0))
        evens.append(again[:half])
        odds.append(again[half:])
    total = None
    for rows, lower in ((evens, False), (odds, True)):
        hi, lo = split2(jnp.concatenate(rows, axis=0))
        w_hi = jnp.concatenate([none, i_hi] if lower else [i_hi, none], axis=0)
        w_lo = jnp.concatenate([none, i_lo] if lower else [i_lo, none], axis=0)
        term = mm_nt(hi, w_hi) + mm_nt(lo, w_hi) + mm_nt(hi, w_lo)
        total = term if total is None else total + term
    x_scr[...] = total
    per = chunks // SEGMENTS
    for c in range(per):
        piece = x_scr[pl.ds(c, count * SEGMENTS, stride=per), :].astype(BF16)
        sent_ref[:, c * LANES:(c + 1) * LANES] = piece
    for copy in copies[5:]:
        copy.wait()


def precondition(block_order, query_grads, out_basis, in_basis, eigenvalues, row_ids, train):
    blocks, qdev, width = query_grads.shape
    count = blocks * qdev
    side = out_basis.shape[1]
    vmem = pl.BlockSpec(memory_space=pltpu.VMEM)
    hbm = pl.BlockSpec(memory_space=pltpu.HBM)
    free = pl.BlockSpec(memory_space=pl.ANY)
    return pl.pallas_call(
        precondition_kernel,
        out_shape=(
            jax.ShapeDtypeStruct((count * SEGMENTS, width // SEGMENTS), BF16),
            jax.ShapeDtypeStruct(row_ids.shape, row_ids.dtype),
            jax.ShapeDtypeStruct(train.shape, train.dtype),
        ),
        in_specs=[hbm] * 7,
        out_specs=(vmem, free, free),
        scratch_shapes=[
            pltpu.SMEM(block_order.shape, block_order.dtype),
            pltpu.VMEM(query_grads.shape, BF16),
            pltpu.VMEM(out_basis.shape, F32),
            pltpu.VMEM(in_basis.shape, F32),
            pltpu.VMEM(eigenvalues.shape, F32),
            pltpu.VMEM((count * width // LANES, LANES), F32),
            pltpu.VMEM((side, LANES), F32),
            pltpu.VMEM((side, LANES), F32),
            pltpu.SemaphoreType.DMA((7,)),
        ],
        compiler_params=pltpu.CompilerParams(vmem_limit_bytes=4 * 2**20),
        name="precondition",
    )(*(
        pltpu.with_memory_space_constraint(x, pltpu.HBM)
        for x in (block_order, query_grads, out_basis, in_basis, eigenvalues, row_ids, train)
    ))


def split3(x):
    hi = x.astype(BF16)
    rest = x - hi.astype(F32)
    mid = rest.astype(BF16)
    return hi, mid, (rest - mid.astype(F32)).astype(BF16)


def slot_of(n_row, mask):
    mask, flip = mask
    source, per = lax.axis_index("row") ^ mask ^ (lax.axis_index("grp") * flip), n_row // 2
    return source ^ (lax.axis_index("layer") * per)


def placed_terms(masks, parts, train_ref, place, flat_scr):
    lines, seg = parts[0].shape
    n_row = len(masks)
    per_seg = seg // LANES
    for b, mask in enumerate(masks):
        at = pl.ds(pl.multiple_of(slot_of(n_row, mask) * lines, lines), lines)
        flat = parts[b][...].astype(F32) if b < len(parts) else jnp.zeros((lines, seg), F32)
        for c in range(per_seg):
            flat_scr[c, at, :] = flat[:, c * LANES:(c + 1) * LANES]
    terms = None
    for j in range(SEGMENTS):
        queries = jnp.concatenate([
            jnp.concatenate(
                [flat_scr[c, pl.ds(t + j, n_row, stride=lines), :] for t in range(0, lines, SEGMENTS)], axis=0
            )
            for c in range(per_seg)
        ], axis=1)
        term = mm_nt(queries.astype(BF16), train_ref[:, j * seg:(j + 1) * seg])
        terms = term if terms is None else terms + term
    a, b, c = split3(terms)
    return mm(a, place) + mm(b, place) + mm(c, place)


def early_kernel(masks, train_ref, ids_ref, *refs):
    parts, (terms_ref, place_ref, flat_scr) = refs[:-3], refs[-3:]
    rows = train_ref.shape[0]
    here = lax.broadcasted_iota(jnp.int32, (rows, rows), 0)
    place = (here == ids_ref[...]).astype(BF16)
    place_ref[...] = place
    terms_ref[...] = placed_terms(masks, parts, train_ref, place, flat_scr)


def late_kernel(masks, blocks, qdev, train_ref, place_ref, early_ref, *refs):
    parts, (mine_ref, other_ref, flat_scr, out_scr) = refs[:-4], refs[-4:]
    n_row = len(masks)
    per = n_row // 2
    terms = early_ref[...] + placed_terms(masks, parts, train_ref, place_ref[...], flat_scr)
    halves = terms.shape[1] // LANES
    half_rows = blocks * per * qdev
    for q in range(blocks * qdev):
        for which in range(2):
            first = which * half_rows + (q // qdev) * per * qdev + q % qdev
            at = q * n_row + which * per
            for h in range(halves):
                out_scr[h, pl.ds(first, per, stride=qdev), :] = terms[at:at + per, h * LANES:(h + 1) * LANES]
    for h in range(halves):
        mine_ref[:, h * LANES:(h + 1) * LANES] = out_scr[h, :half_rows]
        other_ref[:, h * LANES:(h + 1) * LANES] = out_scr[h, half_rows:]


def scores(masks, early, train, row_ids, parts, blocks, qdev):
    rows, width = train.shape
    n_row = len(masks)
    lines, seg = parts[0].shape
    queries = blocks * n_row * qdev
    vmem = pl.BlockSpec(memory_space=pltpu.VMEM)
    params = pltpu.CompilerParams(vmem_limit_bytes=(16 if n_row <= 16 else 40) * 2**20)
    cost = pl.CostEstimate(
        flops=2 * queries * rows * width, bytes_accessed=2 * (rows * width + n_row * lines * seg // 2),
        transcendentals=0,
    )
    flat_scr = pltpu.VMEM((seg // LANES, n_row * lines, LANES), F32)
    terms, place = pl.pallas_call(
        functools.partial(early_kernel, masks),
        out_shape=(
            jax.ShapeDtypeStruct((queries, rows), F32),
            jax.ShapeDtypeStruct((rows, rows), BF16),
        ),
        in_specs=[vmem] * (2 + early),
        out_specs=(vmem, vmem),
        scratch_shapes=[flat_scr],
        compiler_params=params,
        cost_estimate=cost,
        name="scores_early",
    )(train, row_ids, *parts[:early])
    out = jax.ShapeDtypeStruct((queries // 2, rows), F32)
    return pl.pallas_call(
        functools.partial(late_kernel, masks[early:] + masks[:early], blocks, qdev),
        out_shape=(out, out),
        in_specs=[vmem] * (3 + n_row - early),
        out_specs=(vmem, vmem),
        scratch_shapes=[flat_scr, pltpu.VMEM((rows // LANES, queries, LANES), F32)],
        compiler_params=params,
        cost_estimate=cost,
        name="scores_late",
    )(train, place, terms, *parts[early:])


def make_body(n_grp, n_row):
    def swap(x, mask, flip=0, cross=0):
        pairs = [
            (g * n_row + r, (g ^ cross) * n_row + (r ^ mask ^ (g * flip))) for g in range(n_grp) for r in range(n_row)
        ]
        return lax.ppermute(x, ("grp", "row"), pairs)

    def gather(own):
        if (n_grp, n_row) != (2, 8):
            near = {0: own, **{m: swap(own, m) for m in range(2, n_row, 2)}}
            parts = {**near, **{m ^ 1: swap(x, 1) for m, x in near.items()}}
            return {(m, 0): x for m, x in parts.items()}, n_row // 2
        far = swap(own, 4, 2)
        return {
            (0, 0): own, (7, 2): swap(own, 7, 2), (2, 0): swap(own, 2), (1, 0): swap(own, 1), (4, 2): far,
            (3, 0): swap(own, 3), (5, 2): swap(far, 1), (6, 2): swap(far, 0, cross=1),
        }, 5

    def body(train_grads, query_grads, out_basis, in_basis, eigenvalues, block_order, row_ids):
        blocks, qdev, _, width = query_grads.shape
        rows = train_grads.shape[0]
        own, row_ids, train = precondition(
            block_order, query_grads.reshape(blocks, qdev, width), out_basis, in_basis, eigenvalues, row_ids,
            train_grads.reshape(rows, width),
        )
        parts, early = gather(own)
        mine, other = scores(tuple(parts), early, train, row_ids, tuple(parts.values()), blocks, qdev)
        got = lax.ppermute(other, "layer", [(0, 1), (1, 0)])
        total = (mine + got).astype(BF16)
        return total.reshape(blocks, -1, rows).transpose(0, 2, 1)

    return body


def solution(mesh):
    in_specs = (
        P(("grp", "row"), "layer", None),
        P(None, "row", "layer", None),
        P("layer", None, None),
        P("layer", None, None),
        P("layer", None),
        P(),
        P(("grp", "row"), None),
    )
    out_specs = P(None, ("grp", "row"), "layer")
    body = make_body(mesh.shape["grp"], mesh.shape["row"])
    return jax.shard_map(body, mesh=mesh, in_specs=in_specs, out_specs=out_specs, check_vma=False)
```

```python
import functools

import jax
import jax.numpy as jnp
from jax import lax
from jax.experimental import pallas as pl
from jax.experimental.pallas import tpu as pltpu
from jax.sharding import PartitionSpec as P

DAMPING = 0.01
LANES = 128
SEGMENTS = 4
F32, BF16 = jnp.float32, jnp.bfloat16
NT = (((1,), (1,)), ((), ()))


def split2(x):
    high = x.astype(BF16)
    return high, (x - high.astype(F32)).astype(BF16)


def mm(a, b):
    return jnp.dot(a, b, preferred_element_type=F32)


def mm_nt(a, b):
    return lax.dot_general(a, b, NT, preferred_element_type=F32)


def precondition_kernel(
    order_hbm, q_hbm, out_basis_hbm, in_basis_hbm, eig_hbm, ids_hbm, train_hbm,
    sent_ref, ids_out_ref, train_out_ref,
    order_ref, q_ref, out_basis_ref, in_basis_ref, eig_ref, x_scr, even_scr, odd_scr, o_scr, eig_scr, sems,
):
    copies = [
        pltpu.make_async_copy(src, dst, sems.at[n])
        for n, (src, dst) in enumerate((
            (order_hbm, order_ref), (q_hbm, q_ref), (in_basis_hbm, in_basis_ref), (out_basis_hbm, out_basis_ref), (eig_hbm, eig_ref),
            (ids_hbm, ids_out_ref), (train_hbm, train_out_ref),
        ))
    ]
    for copy in copies:
        copy.start()
    for copy in copies[:5]:
        copy.wait()
    blocks, lines, _ = q_ref.shape
    chunks = eig_ref.shape[0]
    side = out_basis_ref.shape[1]
    half = side // 2
    qdev = lines // chunks
    count = blocks * qdev
    scale = 1.0 / (eig_ref[...] + DAMPING)
    eig_scr[pl.ds(0, half, stride=2), :side] = scale[:, :side]
    eig_scr[pl.ds(1, half, stride=2), :side] = scale[:, side:]
    scale = eig_scr[:, :side]
    o_scr[:, :side] = out_basis_ref[0]
    basis = jnp.concatenate(
        [o_scr[pl.ds(0, half, stride=2), :side], o_scr[pl.ds(1, half, stride=2), :side]], axis=0
    )
    b_hi, b_lo = split2(basis)
    t_hi, t_lo = split2(basis.T)
    left = jnp.concatenate([t_hi, t_hi, t_lo], axis=1)
    back = jnp.concatenate([b_hi, b_hi, b_lo], axis=1)
    i_hi, i_lo = split2(in_basis_ref[0])
    none = jnp.zeros_like(i_hi)
    raw = jnp.concatenate([q_ref[order_ref[j]] for j in range(blocks)], axis=0)
    raw2 = jnp.concatenate([raw, raw], axis=1)
    even = mm(raw2, jnp.concatenate([i_hi, none, i_lo, none], axis=0))
    odd = mm(raw2, jnp.concatenate([none, i_hi, none, i_lo], axis=0))
    even_scr[:, :side] = even
    odd_scr[:, :side] = odd
    evens, odds = [], []
    for q in range(count):
        rows = pl.ds(q // qdev * lines + q % qdev, half, stride=qdev)
        hi, lo = split2(jnp.concatenate([even_scr[rows, :side], odd_scr[rows, :side]], axis=0))
        rotated = mm(left, jnp.concatenate([hi, lo, hi], axis=0))
        hi, lo = split2(rotated * scale)
        again = mm(back, jnp.concatenate([hi, lo, hi], axis=0))
        evens.append(again[:half])
        odds.append(again[half:])
    total = None
    for rows, lower in ((evens, False), (odds, True)):
        hi, lo = split2(jnp.concatenate(rows, axis=0))
        w_hi = jnp.concatenate([none, i_hi] if lower else [i_hi, none], axis=0)
        w_lo = jnp.concatenate([none, i_lo] if lower else [i_lo, none], axis=0)
        term = mm_nt(hi, w_hi) + mm_nt(lo, w_hi) + mm_nt(hi, w_lo)
        total = term if total is None else total + term
    x_scr[...] = total
    per = chunks // SEGMENTS
    for c in range(per):
        piece = x_scr[pl.ds(c, count * SEGMENTS, stride=per), :].astype(BF16)
        sent_ref[:, c * LANES:(c + 1) * LANES] = piece
    for copy in copies[5:]:
        copy.wait()


def precondition(block_order, query_grads, out_basis, in_basis, eigenvalues, row_ids, train):
    blocks, qdev, width = query_grads.shape
    count = blocks * qdev
    side = out_basis.shape[1]
    chunks = width // LANES
    query_grads = query_grads.reshape(blocks, qdev, chunks, LANES).swapaxes(1, 2).reshape(blocks, -1, LANES)
    eigenvalues = eigenvalues.reshape(chunks, LANES)
    vmem = pl.BlockSpec(memory_space=pltpu.VMEM)
    hbm = pl.BlockSpec(memory_space=pltpu.HBM)
    free = pl.BlockSpec(memory_space=pl.ANY)
    rows = pltpu.VMEM((count * chunks, LANES), F32)
    return pl.pallas_call(
        precondition_kernel,
        out_shape=(
            jax.ShapeDtypeStruct((count * SEGMENTS, width // SEGMENTS), BF16),
            jax.ShapeDtypeStruct(row_ids.shape, row_ids.dtype),
            jax.ShapeDtypeStruct(train.shape, train.dtype),
        ),
        in_specs=[hbm] * 7,
        out_specs=(vmem, free, free),
        scratch_shapes=[
            pltpu.SMEM(block_order.shape, block_order.dtype),
            pltpu.VMEM(query_grads.shape, BF16),
            pltpu.VMEM(out_basis.shape, F32),
            pltpu.VMEM(in_basis.shape, F32),
            pltpu.VMEM(eigenvalues.shape, F32),
            rows, rows, rows,
            pltpu.VMEM((side, LANES), F32),
            pltpu.VMEM((side, LANES), F32),
            pltpu.SemaphoreType.DMA((7,)),
        ],
        compiler_params=pltpu.CompilerParams(vmem_limit_bytes=4 * 2**20),
        name="precondition",
    )(*(
        pltpu.with_memory_space_constraint(x, pltpu.HBM)
        for x in (block_order, query_grads, out_basis, in_basis, eigenvalues, row_ids, train)
    ))


def split3(x):
    hi = x.astype(BF16)
    rest = x - hi.astype(F32)
    mid = rest.astype(BF16)
    return hi, mid, (rest - mid.astype(F32)).astype(BF16)


def slot_of(n_row, mask):
    source, per = lax.axis_index("row") ^ mask, n_row // 2
    return source ^ (lax.axis_index("layer") * per)


def placed_terms(masks, parts, train_ref, place, flat_scr):
    lines, seg = parts[0].shape
    n_row = len(masks)
    per_seg = seg // LANES
    for b, mask in enumerate(masks):
        at = pl.ds(pl.multiple_of(slot_of(n_row, mask) * lines, lines), lines)
        flat = parts[b][...].astype(F32) if b < len(parts) else jnp.zeros((lines, seg), F32)
        for c in range(per_seg):
            flat_scr[c, at, :] = flat[:, c * LANES:(c + 1) * LANES]
    terms = None
    for j in range(SEGMENTS):
        queries = jnp.concatenate([
            jnp.concatenate(
                [flat_scr[c, pl.ds(t + j, n_row, stride=lines), :] for t in range(0, lines, SEGMENTS)], axis=0
            )
            for c in range(per_seg)
        ], axis=1)
        term = mm_nt(queries.astype(BF16), train_ref[:, j * seg:(j + 1) * seg])
        terms = term if terms is None else terms + term
    a, b, c = split3(terms)
    return mm(a, place) + mm(b, place) + mm(c, place)


def early_kernel(masks, train_ref, ids_ref, *refs):
    parts, (terms_ref, place_ref, flat_scr) = refs[:-3], refs[-3:]
    rows = train_ref.shape[0]
    here = lax.broadcasted_iota(jnp.int32, (rows, rows), 0)
    place = (here == ids_ref[...]).astype(BF16)
    place_ref[...] = place
    terms_ref[...] = placed_terms(masks, parts, train_ref, place, flat_scr)


def late_kernel(masks, blocks, qdev, train_ref, place_ref, early_ref, *refs):
    parts, (mine_ref, other_ref, flat_scr, out_scr) = refs[:-4], refs[-4:]
    n_row = len(masks)
    per = n_row // 2
    terms = early_ref[...] + placed_terms(masks, parts, train_ref, place_ref[...], flat_scr)
    halves = terms.shape[1] // LANES
    half_rows = blocks * per * qdev
    for q in range(blocks * qdev):
        for which in range(2):
            first = which * half_rows + (q // qdev) * per * qdev + q % qdev
            at = q * n_row + which * per
            for h in range(halves):
                out_scr[h, pl.ds(first, per, stride=qdev), :] = terms[at:at + per, h * LANES:(h + 1) * LANES]
    for h in range(halves):
        mine_ref[:, h * LANES:(h + 1) * LANES] = out_scr[h, :half_rows]
        other_ref[:, h * LANES:(h + 1) * LANES] = out_scr[h, half_rows:]


def scores(masks, early, train, row_ids, parts, blocks, qdev):
    rows, width = train.shape
    n_row = len(masks)
    lines, seg = parts[0].shape
    queries = blocks * n_row * qdev
    vmem = pl.BlockSpec(memory_space=pltpu.VMEM)
    params = pltpu.CompilerParams(vmem_limit_bytes=(16 if n_row <= 16 else 40) * 2**20)
    cost = pl.CostEstimate(
        flops=2 * queries * rows * width, bytes_accessed=2 * (rows * width + n_row * lines * seg // 2),
        transcendentals=0,
    )
    flat_scr = pltpu.VMEM((seg // LANES, n_row * lines, LANES), F32)
    terms, place = pl.pallas_call(
        functools.partial(early_kernel, masks),
        out_shape=(
            jax.ShapeDtypeStruct((queries, rows), F32),
            jax.ShapeDtypeStruct((rows, rows), BF16),
        ),
        in_specs=[vmem] * (2 + early),
        out_specs=(vmem, vmem),
        scratch_shapes=[flat_scr],
        compiler_params=params,
        cost_estimate=cost,
        name="scores_early",
    )(train, row_ids, *parts[:early])
    out = jax.ShapeDtypeStruct((queries // 2, rows), F32)
    return pl.pallas_call(
        functools.partial(late_kernel, masks[early:] + masks[:early], blocks, qdev),
        out_shape=(out, out),
        in_specs=[vmem] * (3 + n_row - early),
        out_specs=(vmem, vmem),
        scratch_shapes=[flat_scr, pltpu.VMEM((rows // LANES, queries, LANES), F32)],
        compiler_params=params,
        cost_estimate=cost,
        name="scores_late",
    )(train, place, terms, *parts[early:])


def make_body(n_row):
    def swap(x, mask):
        return lax.ppermute(x, "row", [(r, r ^ mask) for r in range(n_row)])

    def gather(own):
        if n_row != 8:
            near = {0: own, **{m: swap(own, m) for m in range(2, n_row, 2)}}
            return {**near, **{m ^ 1: swap(x, 1) for m, x in near.items()}}, n_row // 2
        far = {m: swap(own, m) for m in (6, 4)}
        diagonal = {3: swap(own, 3)}
        near = {m: swap(own, m) for m in (2, 1)}
        return {0: own, **near, **far, **diagonal, **{m ^ 1: swap(x, 1) for m, x in far.items()}}, 5

    def body(train_grads, query_grads, out_basis, in_basis, eigenvalues, block_order, row_ids):
        blocks, qdev, _, width = query_grads.shape
        rows = train_grads.shape[0]
        own, row_ids, train = precondition(
            block_order, query_grads.reshape(blocks, qdev, width), out_basis, in_basis, eigenvalues, row_ids,
            train_grads.reshape(rows, width),
        )
        parts, early = gather(own)
        mine, other = scores(tuple(parts), early, train, row_ids, tuple(parts.values()), blocks, qdev)
        got = lax.ppermute(other, "layer", [(0, 1), (1, 0)])
        total = (mine + got).astype(BF16)
        return total.reshape(blocks, -1, rows).transpose(0, 2, 1)

    return body


def solution(mesh):
    in_specs = (
        P(("grp", "row"), "layer", None),
        P(None, "row", "layer", None),
        P("layer", None, None),
        P("layer", None, None),
        P("layer", None),
        P(),
        P(("grp", "row"), None),
    )
    out_specs = P(None, ("grp", "row"), "layer")
    body = make_body(mesh.shape["row"])
    return jax.shard_map(body, mesh=mesh, in_specs=in_specs, out_specs=out_specs, check_vma=False)
```

```python
import functools

import jax
import jax.numpy as jnp
from jax import lax
from jax.experimental import pallas as pl
from jax.experimental.pallas import tpu as pltpu
from jax.sharding import PartitionSpec as P

DAMPING = 0.01
LANES = 128
SEGMENTS = 4
F32, BF16 = jnp.float32, jnp.bfloat16
NT = (((1,), (1,)), ((), ()))


def split2(x):
    high = x.astype(BF16)
    return high, (x - high.astype(F32)).astype(BF16)


def mm(a, b):
    return jnp.dot(a, b, preferred_element_type=F32)


def mm_nt(a, b):
    return lax.dot_general(a, b, NT, preferred_element_type=F32)


def precondition_kernel(
    order_hbm, q_hbm, out_basis_hbm, in_basis_hbm, eig_hbm, ids_hbm,
    sent_ref, ids_out_ref,
    order_ref, q_ref, out_basis_ref, in_basis_ref, eig_ref, x_scr, even_scr, odd_scr, o_scr, eig_scr, sems,
):
    copies = [
        pltpu.make_async_copy(src, dst, sems.at[n])
        for n, (src, dst) in enumerate((
            (order_hbm, order_ref), (q_hbm, q_ref), (in_basis_hbm, in_basis_ref), (out_basis_hbm, out_basis_ref), (eig_hbm, eig_ref),
            (ids_hbm, ids_out_ref),
        ))
    ]
    for copy in copies:
        copy.start()
    for copy in copies[:5]:
        copy.wait()
    blocks, lines, _ = q_ref.shape
    chunks = eig_ref.shape[0]
    side = out_basis_ref.shape[1]
    half = side // 2
    qdev = lines // chunks
    count = blocks * qdev
    scale = 1.0 / (eig_ref[...] + DAMPING)
    eig_scr[pl.ds(0, half, stride=2), :side] = scale[:, :side]
    eig_scr[pl.ds(1, half, stride=2), :side] = scale[:, side:]
    scale = eig_scr[:, :side]
    o_scr[:, :side] = out_basis_ref[0]
    basis = jnp.concatenate(
        [o_scr[pl.ds(0, half, stride=2), :side], o_scr[pl.ds(1, half, stride=2), :side]], axis=0
    )
    b_hi, b_lo = split2(basis)
    t_hi, t_lo = split2(basis.T)
    left = jnp.concatenate([t_hi, t_hi, t_lo], axis=1)
    back = jnp.concatenate([b_hi, b_hi, b_lo], axis=1)
    i_hi, i_lo = split2(in_basis_ref[0])
    none = jnp.zeros_like(i_hi)
    raw = jnp.concatenate([q_ref[order_ref[j]] for j in range(blocks)], axis=0)
    raw2 = jnp.concatenate([raw, raw], axis=1)
    even = mm(raw2, jnp.concatenate([i_hi, none, i_lo, none], axis=0))
    odd = mm(raw2, jnp.concatenate([none, i_hi, none, i_lo], axis=0))
    even_scr[:, :side] = even
    odd_scr[:, :side] = odd
    evens, odds = [], []
    for q in range(count):
        rows = pl.ds(q // qdev * lines + q % qdev, half, stride=qdev)
        hi, lo = split2(jnp.concatenate([even_scr[rows, :side], odd_scr[rows, :side]], axis=0))
        rotated = mm(left, jnp.concatenate([hi, lo, hi], axis=0))
        hi, lo = split2(rotated * scale)
        again = mm(back, jnp.concatenate([hi, lo, hi], axis=0))
        evens.append(again[:half])
        odds.append(again[half:])
    total = None
    for rows, lower in ((evens, False), (odds, True)):
        hi, lo = split2(jnp.concatenate(rows, axis=0))
        w_hi = jnp.concatenate([none, i_hi] if lower else [i_hi, none], axis=0)
        w_lo = jnp.concatenate([none, i_lo] if lower else [i_lo, none], axis=0)
        term = mm_nt(hi, w_hi) + mm_nt(lo, w_hi) + mm_nt(hi, w_lo)
        total = term if total is None else total + term
    x_scr[...] = total
    per = chunks // SEGMENTS
    for c in range(per):
        piece = x_scr[pl.ds(c, count * SEGMENTS, stride=per), :].astype(BF16)
        sent_ref[:, c * LANES:(c + 1) * LANES] = piece
    for copy in copies[5:]:
        copy.wait()


def precondition(block_order, query_grads, out_basis, in_basis, eigenvalues, row_ids):
    blocks, qdev, width = query_grads.shape
    count = blocks * qdev
    side = out_basis.shape[1]
    chunks = width // LANES
    query_grads = query_grads.reshape(blocks, qdev, chunks, LANES).swapaxes(1, 2).reshape(blocks, -1, LANES)
    eigenvalues = eigenvalues.reshape(chunks, LANES)
    vmem = pl.BlockSpec(memory_space=pltpu.VMEM)
    hbm = pl.BlockSpec(memory_space=pltpu.HBM)
    free = pl.BlockSpec(memory_space=pl.ANY)
    rows = pltpu.VMEM((count * chunks, LANES), F32)
    return pl.pallas_call(
        precondition_kernel,
        out_shape=(
            jax.ShapeDtypeStruct((count * SEGMENTS, width // SEGMENTS), BF16),
            jax.ShapeDtypeStruct(row_ids.shape, row_ids.dtype),
        ),
        in_specs=[hbm] * 6,
        out_specs=(vmem, free),
        scratch_shapes=[
            pltpu.SMEM(block_order.shape, block_order.dtype),
            pltpu.VMEM(query_grads.shape, BF16),
            pltpu.VMEM(out_basis.shape, F32),
            pltpu.VMEM(in_basis.shape, F32),
            pltpu.VMEM(eigenvalues.shape, F32),
            rows, rows, rows,
            pltpu.VMEM((side, LANES), F32),
            pltpu.VMEM((side, LANES), F32),
            pltpu.SemaphoreType.DMA((6,)),
        ],
        compiler_params=pltpu.CompilerParams(vmem_limit_bytes=4 * 2**20),
        name="precondition",
    )(*(
        pltpu.with_memory_space_constraint(x, pltpu.HBM)
        for x in (block_order, query_grads, out_basis, in_basis, eigenvalues, row_ids)
    ))


def split3(x):
    hi = x.astype(BF16)
    rest = x - hi.astype(F32)
    mid = rest.astype(BF16)
    return hi, mid, (rest - mid.astype(F32)).astype(BF16)


def slot_of(n_row, mask):
    source, per = lax.axis_index("row") ^ mask, n_row // 2
    return source ^ (lax.axis_index("layer") * per)


def placed_terms(masks, parts, train_ref, place, flat_scr, copies=()):
    lines, seg = parts[0].shape
    n_row = len(masks)
    per_seg = seg // LANES
    for b, mask in enumerate(masks):
        at = pl.ds(pl.multiple_of(slot_of(n_row, mask) * lines, lines), lines)
        flat = parts[b][...].astype(F32) if b < len(parts) else jnp.zeros((lines, seg), F32)
        for c in range(per_seg):
            flat_scr[c, at, :] = flat[:, c * LANES:(c + 1) * LANES]
    terms = None
    for j in range(SEGMENTS):
        queries = jnp.concatenate([
            jnp.concatenate(
                [flat_scr[c, pl.ds(t + j, n_row, stride=lines), :] for t in range(0, lines, SEGMENTS)], axis=0
            )
            for c in range(per_seg)
        ], axis=1)
        if copies:
            copies[j].wait()
        term = mm_nt(queries.astype(BF16), train_ref[:, j * seg:(j + 1) * seg])
        terms = term if terms is None else terms + term
    a, b, c = split3(terms)
    return mm(a, place) + mm(b, place) + mm(c, place)


def early_kernel(masks, train_hbm, ids_ref, *refs):
    parts, (terms_ref, place_ref, train_ref, flat_scr, sems) = refs[:-5], refs[-5:]
    rows, width = train_ref.shape
    seg = width // SEGMENTS
    copies = []
    for j in range(SEGMENTS):
        columns = (slice(None), pl.ds(j * seg, seg))
        copies.append(pltpu.make_async_copy(train_hbm.at[columns], train_ref.at[columns], sems.at[j]))
        copies[j].start()
    here = lax.broadcasted_iota(jnp.int32, (rows, rows), 0)
    place = (here == ids_ref[...]).astype(BF16)
    place_ref[...] = place
    terms_ref[...] = placed_terms(masks, parts, train_ref, place, flat_scr, copies)


def late_kernel(masks, blocks, qdev, train_ref, place_ref, early_ref, *refs):
    parts, (mine_ref, other_ref, flat_scr, out_scr) = refs[:-4], refs[-4:]
    n_row = len(masks)
    per = n_row // 2
    terms = early_ref[...] + placed_terms(masks, parts, train_ref, place_ref[...], flat_scr)
    halves = terms.shape[1] // LANES
    half_rows = blocks * per * qdev
    for q in range(blocks * qdev):
        for which in range(2):
            first = which * half_rows + (q // qdev) * per * qdev + q % qdev
            at = q * n_row + which * per
            for h in range(halves):
                out_scr[h, pl.ds(first, per, stride=qdev), :] = terms[at:at + per, h * LANES:(h + 1) * LANES]
    for h in range(halves):
        mine_ref[:, h * LANES:(h + 1) * LANES] = out_scr[h, :half_rows]
        other_ref[:, h * LANES:(h + 1) * LANES] = out_scr[h, half_rows:]


def scores(masks, early, train, row_ids, parts, blocks, qdev):
    rows, width = train.shape
    n_row = len(masks)
    lines, seg = parts[0].shape
    queries = blocks * n_row * qdev
    vmem = pl.BlockSpec(memory_space=pltpu.VMEM)
    params = pltpu.CompilerParams(vmem_limit_bytes=(16 if n_row <= 16 else 40) * 2**20)
    cost = pl.CostEstimate(
        flops=2 * queries * rows * width, bytes_accessed=2 * (rows * width + n_row * lines * seg // 2),
        transcendentals=0,
    )
    flat_scr = pltpu.VMEM((seg // LANES, n_row * lines, LANES), F32)
    terms, place, train = pl.pallas_call(
        functools.partial(early_kernel, masks),
        out_shape=(
            jax.ShapeDtypeStruct((queries, rows), F32),
            jax.ShapeDtypeStruct((rows, rows), BF16),
            jax.ShapeDtypeStruct(train.shape, train.dtype),
        ),
        in_specs=[pl.BlockSpec(memory_space=pltpu.HBM)] + [vmem] * (1 + early),
        out_specs=(vmem, vmem, vmem),
        scratch_shapes=[flat_scr, pltpu.SemaphoreType.DMA((SEGMENTS,))],
        compiler_params=params,
        cost_estimate=cost,
        name="scores_early",
    )(pltpu.with_memory_space_constraint(train, pltpu.HBM), row_ids, *parts[:early])
    out = jax.ShapeDtypeStruct((queries // 2, rows), F32)
    return pl.pallas_call(
        functools.partial(late_kernel, masks[early:] + masks[:early], blocks, qdev),
        out_shape=(out, out),
        in_specs=[vmem] * (3 + n_row - early),
        out_specs=(vmem, vmem),
        scratch_shapes=[flat_scr, pltpu.VMEM((rows // LANES, queries, LANES), F32)],
        compiler_params=params,
        cost_estimate=cost,
        name="scores_late",
    )(train, place, terms, *parts[early:])


def make_body(n_row):
    def swap(x, mask):
        return lax.ppermute(x, "row", [(r, r ^ mask) for r in range(n_row)])

    def gather(own):
        if n_row != 8:
            near = {0: own, **{m: swap(own, m) for m in range(2, n_row, 2)}}
            return {**near, **{m ^ 1: swap(x, 1) for m, x in near.items()}}, n_row // 2
        far = {m: swap(own, m) for m in (6, 4)}
        diagonal = {3: swap(own, 3)}
        near = {m: swap(own, m) for m in (2, 1)}
        return {0: own, **near, **far, **diagonal, **{m ^ 1: swap(x, 1) for m, x in far.items()}}, 5

    def body(train_grads, query_grads, out_basis, in_basis, eigenvalues, block_order, row_ids):
        blocks, qdev, _, width = query_grads.shape
        rows = train_grads.shape[0]
        own, row_ids = precondition(
            block_order, query_grads.reshape(blocks, qdev, width), out_basis, in_basis, eigenvalues, row_ids
        )
        train = train_grads.reshape(rows, width)
        parts, early = gather(own)
        mine, other = scores(tuple(parts), early, train, row_ids, tuple(parts.values()), blocks, qdev)
        got = lax.ppermute(other, "layer", [(0, 1), (1, 0)])
        total = (mine + got).astype(BF16)
        return total.reshape(blocks, -1, rows).transpose(0, 2, 1)

    return body


def solution(mesh):
    in_specs = (
        P(("grp", "row"), "layer", None),
        P(None, "row", "layer", None),
        P("layer", None, None),
        P("layer", None, None),
        P("layer", None),
        P(),
        P(("grp", "row"), None),
    )
    out_specs = P(None, ("grp", "row"), "layer")
    body = make_body(mesh.shape["row"])
    return jax.shard_map(body, mesh=mesh, in_specs=in_specs, out_specs=out_specs, check_vma=False)
```

```python
import functools

import jax
import jax.numpy as jnp
from jax import lax
from jax.experimental import pallas as pl
from jax.experimental.pallas import tpu as pltpu
from jax.sharding import PartitionSpec as P

DAMPING = 0.01
LANES = 128
SEGMENTS = 4
F32, BF16 = jnp.float32, jnp.bfloat16
NT = (((1,), (1,)), ((), ()))


def split2(x):
    high = x.astype(BF16)
    return high, (x - high.astype(F32)).astype(BF16)


def mm(a, b):
    return jnp.dot(a, b, preferred_element_type=F32)


def mm_nt(a, b):
    return lax.dot_general(a, b, NT, preferred_element_type=F32)


def precondition_kernel(
    order_hbm, q_hbm, out_basis_hbm, in_basis_hbm, eig_hbm, ids_hbm, train_hbm,
    sent_ref, ids_out_ref, train_out_ref,
    order_ref, q_ref, out_basis_ref, in_basis_ref, eig_ref, x_scr, even_scr, odd_scr, o_scr, eig_scr, sems,
):
    copies = [
        pltpu.make_async_copy(src, dst, sems.at[n])
        for n, (src, dst) in enumerate((
            (in_basis_hbm, in_basis_ref), (q_hbm, q_ref), (out_basis_hbm, out_basis_ref), (eig_hbm, eig_ref),
            (order_hbm, order_ref), (ids_hbm, ids_out_ref), (train_hbm, train_out_ref),
        ))
    ]
    for copy in copies:
        copy.start()
    for copy in copies[:2]:
        copy.wait()
    blocks, lines, _ = q_ref.shape
    chunks = eig_ref.shape[0]
    side = out_basis_ref.shape[1]
    half = side // 2
    qdev = lines // chunks
    count = blocks * qdev
    i_hi, i_lo = split2(in_basis_ref[0])
    none = jnp.zeros_like(i_hi)
    raw = jnp.concatenate([q_ref[b] for b in range(blocks)], axis=0)
    raw2 = jnp.concatenate([raw, raw], axis=1)
    even = mm(raw2, jnp.concatenate([i_hi, none, i_lo, none], axis=0))
    odd = mm(raw2, jnp.concatenate([none, i_hi, none, i_lo], axis=0))
    even_scr[:, :side] = even
    odd_scr[:, :side] = odd
    for copy in copies[2:4]:
        copy.wait()
    scale = 1.0 / (eig_ref[...] + DAMPING)
    eig_scr[pl.ds(0, half, stride=2), :side] = scale[:, :side]
    eig_scr[pl.ds(1, half, stride=2), :side] = scale[:, side:]
    scale = eig_scr[:, :side]
    o_scr[:, :side] = out_basis_ref[0]
    basis = jnp.concatenate(
        [o_scr[pl.ds(0, half, stride=2), :side], o_scr[pl.ds(1, half, stride=2), :side]], axis=0
    )
    b_hi, b_lo = split2(basis)
    t_hi, t_lo = split2(basis.T)
    left = jnp.concatenate([t_hi, t_hi, t_lo], axis=1)
    back = jnp.concatenate([b_hi, b_hi, b_lo], axis=1)
    evens, odds = [], []
    for q in range(count):
        rows = pl.ds(q // qdev * lines + q % qdev, half, stride=qdev)
        hi, lo = split2(jnp.concatenate([even_scr[rows, :side], odd_scr[rows, :side]], axis=0))
        rotated = mm(left, jnp.concatenate([hi, lo, hi], axis=0))
        hi, lo = split2(rotated * scale)
        again = mm(back, jnp.concatenate([hi, lo, hi], axis=0))
        evens.append(again[:half])
        odds.append(again[half:])
    total = None
    for rows, lower in ((evens, False), (odds, True)):
        hi, lo = split2(jnp.concatenate(rows, axis=0))
        w_hi = jnp.concatenate([none, i_hi] if lower else [i_hi, none], axis=0)
        w_lo = jnp.concatenate([none, i_lo] if lower else [i_lo, none], axis=0)
        term = mm_nt(hi, w_hi) + mm_nt(lo, w_hi) + mm_nt(hi, w_lo)
        total = term if total is None else total + term
    x_scr[...] = total.reshape(x_scr.shape)
    copies[4].wait()
    per = chunks // SEGMENTS
    lines = qdev * SEGMENTS
    for c in range(per):
        piece = [x_scr[order_ref[j], pl.ds(c, lines, stride=per), :] for j in range(blocks)]
        sent_ref[:, c * LANES:(c + 1) * LANES] = jnp.concatenate(piece, axis=0).astype(BF16)
    for copy in copies[5:]:
        copy.wait()


def precondition(block_order, query_grads, out_basis, in_basis, eigenvalues, row_ids, train):
    blocks, qdev, width = query_grads.shape
    count = blocks * qdev
    side = out_basis.shape[1]
    chunks = width // LANES
    query_grads = query_grads.reshape(blocks, qdev, chunks, LANES).swapaxes(1, 2).reshape(blocks, -1, LANES)
    eigenvalues = eigenvalues.reshape(chunks, LANES)
    vmem = pl.BlockSpec(memory_space=pltpu.VMEM)
    hbm = pl.BlockSpec(memory_space=pltpu.HBM)
    free = pl.BlockSpec(memory_space=pl.ANY)
    rows = pltpu.VMEM((count * chunks, LANES), F32)
    return pl.pallas_call(
        precondition_kernel,
        out_shape=(
            jax.ShapeDtypeStruct((count * SEGMENTS, width // SEGMENTS), BF16),
            jax.ShapeDtypeStruct(row_ids.shape, row_ids.dtype),
            jax.ShapeDtypeStruct(train.shape, train.dtype),
        ),
        in_specs=[hbm] * 7,
        out_specs=(vmem, free, free),
        scratch_shapes=[
            pltpu.SMEM(block_order.shape, block_order.dtype),
            pltpu.VMEM(query_grads.shape, BF16),
            pltpu.VMEM(out_basis.shape, F32),
            pltpu.VMEM(in_basis.shape, F32),
            pltpu.VMEM(eigenvalues.shape, F32),
            pltpu.VMEM((blocks, qdev * chunks, LANES), F32),
            rows, rows,
            pltpu.VMEM((side, LANES), F32),
            pltpu.VMEM((side, LANES), F32),
            pltpu.SemaphoreType.DMA((7,)),
        ],
        compiler_params=pltpu.CompilerParams(vmem_limit_bytes=4 * 2**20),
        name="precondition",
    )(*(
        pltpu.with_memory_space_constraint(x, pltpu.HBM)
        for x in (block_order, query_grads, out_basis, in_basis, eigenvalues, row_ids, train)
    ))


def split3(x):
    hi = x.astype(BF16)
    rest = x - hi.astype(F32)
    mid = rest.astype(BF16)
    return hi, mid, (rest - mid.astype(F32)).astype(BF16)


def slot_of(n_row, mask):
    source, per = lax.axis_index("row") ^ mask, n_row // 2
    return source ^ (lax.axis_index("layer") * per)


def placed_terms(masks, parts, train_ref, place, flat_scr):
    lines, seg = parts[0].shape
    n_row = len(masks)
    per_seg = seg // LANES
    for b, mask in enumerate(masks):
        at = pl.ds(pl.multiple_of(slot_of(n_row, mask) * lines, lines), lines)
        flat = parts[b][...].astype(F32) if b < len(parts) else jnp.zeros((lines, seg), F32)
        for c in range(per_seg):
            flat_scr[c, at, :] = flat[:, c * LANES:(c + 1) * LANES]
    terms = None
    for j in range(SEGMENTS):
        queries = jnp.concatenate([
            jnp.concatenate(
                [flat_scr[c, pl.ds(t + j, n_row, stride=lines), :] for t in range(0, lines, SEGMENTS)], axis=0
            )
            for c in range(per_seg)
        ], axis=1)
        term = mm_nt(queries.astype(BF16), train_ref[:, j * seg:(j + 1) * seg])
        terms = term if terms is None else terms + term
    a, b, c = split3(terms)
    return mm(a, place) + mm(b, place) + mm(c, place)


def early_kernel(masks, train_ref, ids_ref, *refs):
    parts, (terms_ref, place_ref, flat_scr) = refs[:-3], refs[-3:]
    rows = train_ref.shape[0]
    here = lax.broadcasted_iota(jnp.int32, (rows, rows), 0)
    place = (here == ids_ref[...]).astype(BF16)
    place_ref[...] = place
    terms_ref[...] = placed_terms(masks, parts, train_ref, place, flat_scr)


def late_kernel(masks, blocks, qdev, train_ref, place_ref, early_ref, *refs):
    parts, (mine_ref, other_ref, flat_scr, out_scr) = refs[:-4], refs[-4:]
    n_row = len(masks)
    per = n_row // 2
    terms = early_ref[...] + placed_terms(masks, parts, train_ref, place_ref[...], flat_scr)
    halves = terms.shape[1] // LANES
    half_rows = blocks * per * qdev
    for q in range(blocks * qdev):
        for which in range(2):
            first = which * half_rows + (q // qdev) * per * qdev + q % qdev
            at = q * n_row + which * per
            for h in range(halves):
                out_scr[h, pl.ds(first, per, stride=qdev), :] = terms[at:at + per, h * LANES:(h + 1) * LANES]
    for h in range(halves):
        mine_ref[:, h * LANES:(h + 1) * LANES] = out_scr[h, :half_rows]
        other_ref[:, h * LANES:(h + 1) * LANES] = out_scr[h, half_rows:]


def scores(masks, early, train, row_ids, parts, blocks, qdev):
    rows, width = train.shape
    n_row = len(masks)
    lines, seg = parts[0].shape
    queries = blocks * n_row * qdev
    vmem = pl.BlockSpec(memory_space=pltpu.VMEM)
    params = pltpu.CompilerParams(vmem_limit_bytes=(16 if n_row <= 16 else 40) * 2**20)
    cost = pl.CostEstimate(
        flops=2 * queries * rows * width, bytes_accessed=2 * (rows * width + n_row * lines * seg // 2),
        transcendentals=0,
    )
    flat_scr = pltpu.VMEM((seg // LANES, n_row * lines, LANES), F32)
    terms, place = pl.pallas_call(
        functools.partial(early_kernel, masks),
        out_shape=(
            jax.ShapeDtypeStruct((queries, rows), F32),
            jax.ShapeDtypeStruct((rows, rows), BF16),
        ),
        in_specs=[vmem] * (2 + early),
        out_specs=(vmem, vmem),
        scratch_shapes=[flat_scr],
        compiler_params=params,
        cost_estimate=cost,
        name="scores_early",
    )(train, row_ids, *parts[:early])
    out = jax.ShapeDtypeStruct((queries // 2, rows), F32)
    return pl.pallas_call(
        functools.partial(late_kernel, masks[early:] + masks[:early], blocks, qdev),
        out_shape=(out, out),
        in_specs=[vmem] * (3 + n_row - early),
        out_specs=(vmem, vmem),
        scratch_shapes=[flat_scr, pltpu.VMEM((rows // LANES, queries, LANES), F32)],
        compiler_params=params,
        cost_estimate=cost,
        name="scores_late",
    )(train, place, terms, *parts[early:])


def make_body(n_row):
    def swap(x, mask):
        return lax.ppermute(x, "row", [(r, r ^ mask) for r in range(n_row)])

    def gather(own):
        if n_row != 8:
            near = {0: own, **{m: swap(own, m) for m in range(2, n_row, 2)}}
            return {**near, **{m ^ 1: swap(x, 1) for m, x in near.items()}}, n_row // 2
        far = {m: swap(own, m) for m in (6, 4)}
        diagonal = {3: swap(own, 3)}
        near = {m: swap(own, m) for m in (2, 1)}
        return {0: own, **near, **far, **diagonal, **{m ^ 1: swap(x, 1) for m, x in far.items()}}, 5

    def body(train_grads, query_grads, out_basis, in_basis, eigenvalues, block_order, row_ids):
        blocks, qdev, _, width = query_grads.shape
        rows = train_grads.shape[0]
        own, row_ids, train = precondition(
            block_order, query_grads.reshape(blocks, qdev, width), out_basis, in_basis, eigenvalues, row_ids,
            train_grads.reshape(rows, width),
        )
        parts, early = gather(own)
        mine, other = scores(tuple(parts), early, train, row_ids, tuple(parts.values()), blocks, qdev)
        got = lax.ppermute(other, "layer", [(0, 1), (1, 0)])
        total = (mine + got).astype(BF16)
        return total.reshape(blocks, -1, rows).transpose(0, 2, 1)

    return body


def solution(mesh):
    in_specs = (
        P(("grp", "row"), "layer", None),
        P(None, "row", "layer", None),
        P("layer", None, None),
        P("layer", None, None),
        P("layer", None),
        P(),
        P(("grp", "row"), None),
    )
    out_specs = P(None, ("grp", "row"), "layer")
    body = make_body(mesh.shape["row"])
    return jax.shard_map(body, mesh=mesh, in_specs=in_specs, out_specs=out_specs, check_vma=False)
```

```python
import functools

import jax
import jax.numpy as jnp
from jax import lax
from jax.experimental import pallas as pl
from jax.experimental.pallas import tpu as pltpu
from jax.sharding import PartitionSpec as P

DAMPING = 0.01
LANES = 128
SEGMENTS = 4
F32, BF16 = jnp.float32, jnp.bfloat16
NT = (((1,), (1,)), ((), ()))


def split2(x):
    high = x.astype(BF16)
    return high, (x - high.astype(F32)).astype(BF16)


def mm(a, b):
    return jnp.dot(a, b, preferred_element_type=F32)


def mm_nt(a, b):
    return lax.dot_general(a, b, NT, preferred_element_type=F32)


def precondition_kernel(
    order_hbm, q_hbm, out_basis_hbm, in_basis_hbm, eig_hbm, ids_hbm, train_hbm,
    sent_ref, ids_out_ref, train_out_ref,
    order_ref, q_ref, out_basis_ref, in_basis_ref, eig_ref, x_scr, even_scr, odd_scr, o_scr, eig_scr, sems,
):
    copies = [
        pltpu.make_async_copy(src, dst, sems.at[n])
        for n, (src, dst) in enumerate((
            (order_hbm, order_ref), (q_hbm, q_ref), (in_basis_hbm, in_basis_ref), (out_basis_hbm, out_basis_ref), (eig_hbm, eig_ref),
            (ids_hbm, ids_out_ref), (train_hbm, train_out_ref),
        ))
    ]
    for copy in copies:
        copy.start()
    for copy in copies[:5]:
        copy.wait()
    blocks, lines, _ = q_ref.shape
    chunks = eig_ref.shape[0]
    side = out_basis_ref.shape[1]
    half = side // 2
    count = blocks * (lines // chunks)
    left_lanes = lax.broadcasted_iota(jnp.int32, (half, LANES), 1) < side

    def swapped(x):
        return jnp.concatenate([x[:, side:], x[:, :side]], axis=1)

    scale = 1.0 / (eig_ref[...] + DAMPING)
    turned = swapped(scale)
    eig_scr[pl.ds(0, half, stride=2), :] = jnp.where(left_lanes, scale, turned)
    eig_scr[pl.ds(1, half, stride=2), :] = jnp.where(left_lanes, turned, scale)
    scale = jnp.concatenate([eig_scr[...]] * blocks, axis=1)
    o_scr[:, :side] = out_basis_ref[0]
    basis = jnp.concatenate(
        [o_scr[pl.ds(0, half, stride=2), :side], o_scr[pl.ds(1, half, stride=2), :side]], axis=0
    )
    b_hi, b_lo = split2(basis)
    t_hi, t_lo = split2(basis.T)
    left = jnp.concatenate([t_hi, t_hi, t_lo], axis=1)
    back = jnp.concatenate([b_hi, b_hi, b_lo], axis=1)
    twice_hi, twice_lo = split2(jnp.concatenate([in_basis_ref[0]] * 2, axis=1))
    none = jnp.zeros_like(twice_hi)
    raw = jnp.concatenate([q_ref[order_ref[j]] for j in range(blocks)], axis=0)
    rotated = mm(jnp.concatenate([raw, raw], axis=1), jnp.concatenate([
        jnp.concatenate([twice_hi, none, twice_lo, none], axis=0),
        jnp.concatenate([none, twice_hi, none, twice_lo], axis=0),
    ], axis=1))
    even_scr[...] = rotated[:, :LANES]
    odd_scr[...] = rotated[:, LANES:]
    pairs = []
    for j in range(blocks):
        first, second = pl.ds(j * lines, half, stride=2), pl.ds(j * lines + 1, half, stride=2)
        pairs.append(jnp.concatenate(
            [jnp.where(left_lanes, scr[first, :], scr[second, :]) for scr in (even_scr, odd_scr)], axis=0
        ))
    hi, lo = split2(jnp.concatenate(pairs, axis=1))
    rotated = mm(left, jnp.concatenate([hi, lo, hi], axis=0))
    hi, lo = split2(rotated * scale)
    again = mm(back, jnp.concatenate([hi, lo, hi], axis=0))
    rows = jnp.concatenate([
        jnp.concatenate([again[at:at + half, j * LANES:(j + 1) * LANES] for j in range(blocks)], axis=0)
        for at in (0, half)
    ], axis=1)
    hi, lo = split2(rows)
    left_side = lax.broadcasted_iota(jnp.int32, (side, LANES), 1) < side

    def placed(twice):
        one, two = jnp.where(left_side, twice, 0), jnp.where(left_side, 0, twice)
        zero = jnp.zeros_like(one)
        return jnp.concatenate([
            jnp.concatenate([one, zero], axis=1), jnp.concatenate([zero, one], axis=1),
            jnp.concatenate([two, zero], axis=1), jnp.concatenate([zero, two], axis=1),
        ], axis=0).astype(BF16)

    w_hi, w_lo = placed(twice_hi.astype(F32)), placed(twice_lo.astype(F32))
    total = mm_nt(hi, w_hi) + mm_nt(lo, w_hi) + mm_nt(hi, w_lo)
    for j in range(blocks):
        for e in range(2):
            at = (2 * j + e) * chunks
            x_scr[at:at + chunks, :] = total[j * half:(j + 1) * half, e * LANES:(e + 1) * LANES]
    per = chunks // SEGMENTS
    for c in range(per):
        piece = x_scr[pl.ds(c, count * SEGMENTS, stride=per), :].astype(BF16)
        sent_ref[:, c * LANES:(c + 1) * LANES] = piece
    for copy in copies[5:]:
        copy.wait()


def precondition(block_order, query_grads, out_basis, in_basis, eigenvalues, row_ids, train):
    blocks, qdev, width = query_grads.shape
    count = blocks * qdev
    side = out_basis.shape[1]
    chunks = width // LANES
    query_grads = query_grads.reshape(blocks, qdev, chunks, LANES).swapaxes(1, 2).reshape(blocks, -1, LANES)
    eigenvalues = eigenvalues.reshape(chunks, LANES)
    vmem = pl.BlockSpec(memory_space=pltpu.VMEM)
    hbm = pl.BlockSpec(memory_space=pltpu.HBM)
    free = pl.BlockSpec(memory_space=pl.ANY)
    rows = pltpu.VMEM((count * chunks, LANES), F32)
    return pl.pallas_call(
        precondition_kernel,
        out_shape=(
            jax.ShapeDtypeStruct((count * SEGMENTS, width // SEGMENTS), BF16),
            jax.ShapeDtypeStruct(row_ids.shape, row_ids.dtype),
            jax.ShapeDtypeStruct(train.shape, train.dtype),
        ),
        in_specs=[hbm] * 7,
        out_specs=(vmem, free, free),
        scratch_shapes=[
            pltpu.SMEM(block_order.shape, block_order.dtype),
            pltpu.VMEM(query_grads.shape, BF16),
            pltpu.VMEM(out_basis.shape, F32),
            pltpu.VMEM(in_basis.shape, F32),
            pltpu.VMEM(eigenvalues.shape, F32),
            rows, rows, rows,
            pltpu.VMEM((side, LANES), F32),
            pltpu.VMEM((side, LANES), F32),
            pltpu.SemaphoreType.DMA((7,)),
        ],
        compiler_params=pltpu.CompilerParams(vmem_limit_bytes=4 * 2**20),
        name="precondition",
    )(*(
        pltpu.with_memory_space_constraint(x, pltpu.HBM)
        for x in (block_order, query_grads, out_basis, in_basis, eigenvalues, row_ids, train)
    ))


def split3(x):
    hi = x.astype(BF16)
    rest = x - hi.astype(F32)
    mid = rest.astype(BF16)
    return hi, mid, (rest - mid.astype(F32)).astype(BF16)


def slot_of(n_row, mask):
    source, per = lax.axis_index("row") ^ mask, n_row // 2
    return source ^ (lax.axis_index("layer") * per)


def placed_terms(masks, parts, train_ref, place, flat_scr):
    lines, seg = parts[0].shape
    n_row = len(masks)
    per_seg = seg // LANES
    for b, mask in enumerate(masks):
        at = pl.ds(pl.multiple_of(slot_of(n_row, mask) * lines, lines), lines)
        flat = parts[b][...].astype(F32) if b < len(parts) else jnp.zeros((lines, seg), F32)
        for c in range(per_seg):
            flat_scr[c, at, :] = flat[:, c * LANES:(c + 1) * LANES]
    terms = None
    for j in range(SEGMENTS):
        queries = jnp.concatenate([
            jnp.concatenate(
                [flat_scr[c, pl.ds(t + j, n_row, stride=lines), :] for t in range(0, lines, SEGMENTS)], axis=0
            )
            for c in range(per_seg)
        ], axis=1)
        term = mm_nt(queries.astype(BF16), train_ref[:, j * seg:(j + 1) * seg])
        terms = term if terms is None else terms + term
    a, b, c = split3(terms)
    return mm(a, place) + mm(b, place) + mm(c, place)


def early_kernel(masks, train_ref, ids_ref, *refs):
    parts, (terms_ref, place_ref, flat_scr) = refs[:-3], refs[-3:]
    rows = train_ref.shape[0]
    here = lax.broadcasted_iota(jnp.int32, (rows, rows), 0)
    place = (here == ids_ref[...]).astype(BF16)
    place_ref[...] = place
    terms_ref[...] = placed_terms(masks, parts, train_ref, place, flat_scr)


def late_kernel(masks, blocks, qdev, train_ref, place_ref, early_ref, *refs):
    parts, (mine_ref, other_ref, flat_scr, out_scr) = refs[:-4], refs[-4:]
    n_row = len(masks)
    per = n_row // 2
    terms = early_ref[...] + placed_terms(masks, parts, train_ref, place_ref[...], flat_scr)
    halves = terms.shape[1] // LANES
    half_rows = blocks * per * qdev
    for q in range(blocks * qdev):
        for which in range(2):
            first = which * half_rows + (q // qdev) * per * qdev + q % qdev
            at = q * n_row + which * per
            for h in range(halves):
                out_scr[h, pl.ds(first, per, stride=qdev), :] = terms[at:at + per, h * LANES:(h + 1) * LANES]
    for h in range(halves):
        mine_ref[:, h * LANES:(h + 1) * LANES] = out_scr[h, :half_rows]
        other_ref[:, h * LANES:(h + 1) * LANES] = out_scr[h, half_rows:]


def scores(masks, early, train, row_ids, parts, blocks, qdev):
    rows, width = train.shape
    n_row = len(masks)
    lines, seg = parts[0].shape
    queries = blocks * n_row * qdev
    vmem = pl.BlockSpec(memory_space=pltpu.VMEM)
    params = pltpu.CompilerParams(vmem_limit_bytes=(16 if n_row <= 16 else 40) * 2**20)
    cost = pl.CostEstimate(
        flops=2 * queries * rows * width, bytes_accessed=2 * (rows * width + n_row * lines * seg // 2),
        transcendentals=0,
    )
    flat_scr = pltpu.VMEM((seg // LANES, n_row * lines, LANES), F32)
    terms, place = pl.pallas_call(
        functools.partial(early_kernel, masks),
        out_shape=(
            jax.ShapeDtypeStruct((queries, rows), F32),
            jax.ShapeDtypeStruct((rows, rows), BF16),
        ),
        in_specs=[vmem] * (2 + early),
        out_specs=(vmem, vmem),
        scratch_shapes=[flat_scr],
        compiler_params=params,
        cost_estimate=cost,
        name="scores_early",
    )(train, row_ids, *parts[:early])
    out = jax.ShapeDtypeStruct((queries // 2, rows), F32)
    return pl.pallas_call(
        functools.partial(late_kernel, masks[early:] + masks[:early], blocks, qdev),
        out_shape=(out, out),
        in_specs=[vmem] * (3 + n_row - early),
        out_specs=(vmem, vmem),
        scratch_shapes=[flat_scr, pltpu.VMEM((rows // LANES, queries, LANES), F32)],
        compiler_params=params,
        cost_estimate=cost,
        name="scores_late",
    )(train, place, terms, *parts[early:])


def make_body(n_row):
    def swap(x, mask):
        return lax.ppermute(x, "row", [(r, r ^ mask) for r in range(n_row)])

    def gather(own):
        if n_row != 8:
            near = {0: own, **{m: swap(own, m) for m in range(2, n_row, 2)}}
            return {**near, **{m ^ 1: swap(x, 1) for m, x in near.items()}}, n_row // 2
        far = {m: swap(own, m) for m in (6, 4)}
        diagonal = {3: swap(own, 3)}
        near = {m: swap(own, m) for m in (2, 1)}
        return {0: own, **near, **far, **diagonal, **{m ^ 1: swap(x, 1) for m, x in far.items()}}, 5

    def body(train_grads, query_grads, out_basis, in_basis, eigenvalues, block_order, row_ids):
        blocks, qdev, _, width = query_grads.shape
        rows = train_grads.shape[0]
        own, row_ids, train = precondition(
            block_order, query_grads.reshape(blocks, qdev, width), out_basis, in_basis, eigenvalues, row_ids,
            train_grads.reshape(rows, width),
        )
        parts, early = gather(own)
        mine, other = scores(tuple(parts), early, train, row_ids, tuple(parts.values()), blocks, qdev)
        got = lax.ppermute(other, "layer", [(0, 1), (1, 0)])
        total = (mine + got).astype(BF16)
        return total.reshape(blocks, -1, rows).transpose(0, 2, 1)

    return body


def solution(mesh):
    in_specs = (
        P(("grp", "row"), "layer", None),
        P(None, "row", "layer", None),
        P("layer", None, None),
        P("layer", None, None),
        P("layer", None),
        P(),
        P(("grp", "row"), None),
    )
    out_specs = P(None, ("grp", "row"), "layer")
    body = make_body(mesh.shape["row"])
    return jax.shard_map(body, mesh=mesh, in_specs=in_specs, out_specs=out_specs, check_vma=False)
```

```python
import functools

import jax
import jax.numpy as jnp
from jax import lax
from jax.experimental import pallas as pl
from jax.experimental.pallas import tpu as pltpu
from jax.sharding import PartitionSpec as P

DAMPING = 0.01
LANES = 128
SEGMENTS = 4
F32, BF16 = jnp.float32, jnp.bfloat16
NT = (((1,), (1,)), ((), ()))


def split2(x):
    high = x.astype(BF16)
    return high, (x - high.astype(F32)).astype(BF16)


def mm(a, b):
    return jnp.dot(a, b, preferred_element_type=F32)


def mm_nt(a, b):
    return lax.dot_general(a, b, NT, preferred_element_type=F32)


def precondition_kernel(
    order_hbm, q_hbm, out_basis_hbm, in_basis_hbm, eig_hbm, ids_hbm, train_hbm,
    sent_ref, ids_out_ref, train_out_ref,
    order_ref, q_ref, out_basis_ref, in_basis_ref, eig_ref, x_scr, even_scr, odd_scr, o_scr, eig_scr, sems,
):
    copies = [
        pltpu.make_async_copy(src, dst, sems.at[n])
        for n, (src, dst) in enumerate((
            (q_hbm, q_ref), (in_basis_hbm, in_basis_ref), (out_basis_hbm, out_basis_ref), (eig_hbm, eig_ref),
            (order_hbm, order_ref), (ids_hbm, ids_out_ref), (train_hbm, train_out_ref),
        ))
    ]
    for copy in copies:
        copy.start()
    for copy in copies[:4]:
        copy.wait()
    blocks, lines, _ = q_ref.shape
    chunks = eig_ref.shape[0]
    side = out_basis_ref.shape[1]
    half = side // 2
    left_lanes = lax.broadcasted_iota(jnp.int32, (half, LANES), 1) < side

    def swapped(x):
        return jnp.concatenate([x[:, side:], x[:, :side]], axis=1)

    scale = 1.0 / (eig_ref[...] + DAMPING)
    turned = swapped(scale)
    eig_scr[pl.ds(0, half, stride=2), :] = jnp.where(left_lanes, scale, turned)
    eig_scr[pl.ds(1, half, stride=2), :] = jnp.where(left_lanes, turned, scale)
    scale = jnp.concatenate([eig_scr[...]] * blocks, axis=1)
    o_scr[:, :side] = out_basis_ref[0]
    basis = jnp.concatenate(
        [o_scr[pl.ds(0, half, stride=2), :side], o_scr[pl.ds(1, half, stride=2), :side]], axis=0
    )
    b_hi, b_lo = split2(basis)
    t_hi, t_lo = split2(basis.T)
    left = jnp.concatenate([t_hi, t_hi, t_lo], axis=1)
    back = jnp.concatenate([b_hi, b_hi, b_lo], axis=1)
    twice_hi, twice_lo = split2(jnp.concatenate([in_basis_ref[0]] * 2, axis=1))
    none = jnp.zeros_like(twice_hi)
    raw = jnp.concatenate([q_ref[j] for j in range(blocks)], axis=0)
    rotated = mm(jnp.concatenate([raw, raw], axis=1), jnp.concatenate([
        jnp.concatenate([twice_hi, none, twice_lo, none], axis=0),
        jnp.concatenate([none, twice_hi, none, twice_lo], axis=0),
    ], axis=1))
    even_scr[...] = rotated[:, :LANES]
    odd_scr[...] = rotated[:, LANES:]
    pairs = []
    for j in range(blocks):
        first, second = pl.ds(j * lines, half, stride=2), pl.ds(j * lines + 1, half, stride=2)
        pairs.append(jnp.concatenate(
            [jnp.where(left_lanes, scr[first, :], scr[second, :]) for scr in (even_scr, odd_scr)], axis=0
        ))
    hi, lo = split2(jnp.concatenate(pairs, axis=1))
    rotated = mm(left, jnp.concatenate([hi, lo, hi], axis=0))
    hi, lo = split2(rotated * scale)
    again = mm(back, jnp.concatenate([hi, lo, hi], axis=0))
    rows = jnp.concatenate([
        jnp.concatenate([again[at:at + half, j * LANES:(j + 1) * LANES] for j in range(blocks)], axis=0)
        for at in (0, half)
    ], axis=1)
    hi, lo = split2(rows)
    left_side = lax.broadcasted_iota(jnp.int32, (side, LANES), 1) < side

    def placed(twice):
        one, two = jnp.where(left_side, twice, 0), jnp.where(left_side, 0, twice)
        zero = jnp.zeros_like(one)
        return jnp.concatenate([
            jnp.concatenate([one, zero], axis=1), jnp.concatenate([zero, one], axis=1),
            jnp.concatenate([two, zero], axis=1), jnp.concatenate([zero, two], axis=1),
        ], axis=0).astype(BF16)

    w_hi, w_lo = placed(twice_hi.astype(F32)), placed(twice_lo.astype(F32))
    total = mm_nt(hi, w_hi) + mm_nt(lo, w_hi) + mm_nt(hi, w_lo)
    for j in range(blocks):
        for e in range(2):
            x_scr[j, e * chunks:(e + 1) * chunks, :] = total[j * half:(j + 1) * half, e * LANES:(e + 1) * LANES]
    copies[4].wait()
    per = chunks // SEGMENTS
    for c in range(per):
        piece = [x_scr[order_ref[j], pl.ds(c, 2 * SEGMENTS, stride=per), :] for j in range(blocks)]
        sent_ref[:, c * LANES:(c + 1) * LANES] = jnp.concatenate(piece, axis=0).astype(BF16)
    for copy in copies[5:]:
        copy.wait()


def precondition(block_order, query_grads, out_basis, in_basis, eigenvalues, row_ids, train):
    blocks, qdev, width = query_grads.shape
    count = blocks * qdev
    side = out_basis.shape[1]
    chunks = width // LANES
    query_grads = query_grads.reshape(blocks, qdev, chunks, LANES).swapaxes(1, 2).reshape(blocks, -1, LANES)
    eigenvalues = eigenvalues.reshape(chunks, LANES)
    vmem = pl.BlockSpec(memory_space=pltpu.VMEM)
    hbm = pl.BlockSpec(memory_space=pltpu.HBM)
    free = pl.BlockSpec(memory_space=pl.ANY)
    rows = pltpu.VMEM((count * chunks, LANES), F32)
    return pl.pallas_call(
        precondition_kernel,
        out_shape=(
            jax.ShapeDtypeStruct((count * SEGMENTS, width // SEGMENTS), BF16),
            jax.ShapeDtypeStruct(row_ids.shape, row_ids.dtype),
            jax.ShapeDtypeStruct(train.shape, train.dtype),
        ),
        in_specs=[hbm] * 7,
        out_specs=(vmem, free, free),
        scratch_shapes=[
            pltpu.SMEM(block_order.shape, block_order.dtype),
            pltpu.VMEM(query_grads.shape, BF16),
            pltpu.VMEM(out_basis.shape, F32),
            pltpu.VMEM(in_basis.shape, F32),
            pltpu.VMEM(eigenvalues.shape, F32),
            pltpu.VMEM((blocks, qdev * chunks, LANES), F32),
            rows, rows,
            pltpu.VMEM((side, LANES), F32),
            pltpu.VMEM((side, LANES), F32),
            pltpu.SemaphoreType.DMA((7,)),
        ],
        compiler_params=pltpu.CompilerParams(vmem_limit_bytes=4 * 2**20),
        name="precondition",
    )(*(
        pltpu.with_memory_space_constraint(x, pltpu.HBM)
        for x in (block_order, query_grads, out_basis, in_basis, eigenvalues, row_ids, train)
    ))


def slot_of(n_row, mask):
    source, per = lax.axis_index("row") ^ mask, n_row // 2
    return source ^ (lax.axis_index("layer") * per)


def placed_terms(masks, parts, train_ref, place, flat_scr):
    lines, seg = parts[0].shape
    n_row = len(masks)
    per_seg = seg // LANES
    for b, mask in enumerate(masks):
        at = pl.ds(pl.multiple_of(slot_of(n_row, mask) * lines, lines), lines)
        flat = parts[b][...].astype(F32) if b < len(parts) else jnp.zeros((lines, seg), F32)
        for c in range(per_seg):
            flat_scr[c, at, :] = flat[:, c * LANES:(c + 1) * LANES]
    terms = None
    for j in range(SEGMENTS):
        queries = jnp.concatenate([
            jnp.concatenate(
                [flat_scr[c, pl.ds(t + j, n_row, stride=lines), :] for t in range(0, lines, SEGMENTS)], axis=0
            )
            for c in range(per_seg)
        ], axis=1)
        term = mm_nt(queries.astype(BF16), train_ref[:, j * seg:(j + 1) * seg])
        terms = term if terms is None else terms + term
    hi, lo = split2(terms)
    return mm(hi, place) + mm(lo, place)


def early_kernel(masks, train_ref, ids_ref, *refs):
    parts, (terms_ref, place_ref, flat_scr) = refs[:-3], refs[-3:]
    rows = train_ref.shape[0]
    here = lax.broadcasted_iota(jnp.int32, (rows, rows), 0)
    place = (here == ids_ref[...]).astype(BF16)
    place_ref[...] = place
    terms_ref[...] = placed_terms(masks, parts, train_ref, place, flat_scr)


def late_kernel(masks, blocks, qdev, train_ref, place_ref, early_ref, *refs):
    parts, (mine_ref, other_ref, flat_scr, out_scr) = refs[:-4], refs[-4:]
    n_row = len(masks)
    per = n_row // 2
    terms = early_ref[...] + placed_terms(masks, parts, train_ref, place_ref[...], flat_scr)
    halves = terms.shape[1] // LANES
    half_rows = blocks * per * qdev
    for q in range(blocks * qdev):
        for which in range(2):
            first = which * half_rows + (q // qdev) * per * qdev + q % qdev
            at = q * n_row + which * per
            for h in range(halves):
                out_scr[h, pl.ds(first, per, stride=qdev), :] = terms[at:at + per, h * LANES:(h + 1) * LANES]
    for h in range(halves):
        mine_ref[:, h * LANES:(h + 1) * LANES] = out_scr[h, :half_rows]
        other_ref[:, h * LANES:(h + 1) * LANES] = out_scr[h, half_rows:].astype(BF16)


def scores(masks, early, train, row_ids, parts, blocks, qdev):
    rows, width = train.shape
    n_row = len(masks)
    lines, seg = parts[0].shape
    queries = blocks * n_row * qdev
    vmem = pl.BlockSpec(memory_space=pltpu.VMEM)
    params = pltpu.CompilerParams(vmem_limit_bytes=(16 if n_row <= 16 else 40) * 2**20)
    cost = pl.CostEstimate(
        flops=2 * queries * rows * width, bytes_accessed=2 * (rows * width + n_row * lines * seg // 2),
        transcendentals=0,
    )
    flat_scr = pltpu.VMEM((seg // LANES, n_row * lines, LANES), F32)
    terms, place = pl.pallas_call(
        functools.partial(early_kernel, masks),
        out_shape=(
            jax.ShapeDtypeStruct((queries, rows), F32),
            jax.ShapeDtypeStruct((rows, rows), BF16),
        ),
        in_specs=[vmem] * (2 + early),
        out_specs=(vmem, vmem),
        scratch_shapes=[flat_scr],
        compiler_params=params,
        cost_estimate=cost,
        name="scores_early",
    )(train, row_ids, *parts[:early])
    half = (queries // 2, rows)
    return pl.pallas_call(
        functools.partial(late_kernel, masks[early:] + masks[:early], blocks, qdev),
        out_shape=(jax.ShapeDtypeStruct(half, F32), jax.ShapeDtypeStruct(half, BF16)),
        in_specs=[vmem] * (3 + n_row - early),
        out_specs=(vmem, vmem),
        scratch_shapes=[flat_scr, pltpu.VMEM((rows // LANES, queries, LANES), F32)],
        compiler_params=params,
        cost_estimate=cost,
        name="scores_late",
    )(train, place, terms, *parts[early:])


def make_body(n_row):
    def swap(x, mask):
        return lax.ppermute(x, "row", [(r, r ^ mask) for r in range(n_row)])

    def gather(own):
        if n_row != 8:
            near = {0: own, **{m: swap(own, m) for m in range(2, n_row, 2)}}
            return {**near, **{m ^ 1: swap(x, 1) for m, x in near.items()}}, n_row // 2
        far = {m: swap(own, m) for m in (6, 4)}
        diagonal = {3: swap(own, 3)}
        near = {m: swap(own, m) for m in (2, 1)}
        return {0: own, **near, **far, **diagonal, **{m ^ 1: swap(x, 1) for m, x in far.items()}}, 5

    def body(train_grads, query_grads, out_basis, in_basis, eigenvalues, block_order, row_ids):
        blocks, qdev, _, width = query_grads.shape
        rows = train_grads.shape[0]
        own, row_ids, train = precondition(
            block_order, query_grads.reshape(blocks, qdev, width), out_basis, in_basis, eigenvalues, row_ids,
            train_grads.reshape(rows, width),
        )
        parts, early = gather(own)
        mine, other = scores(tuple(parts), early, train, row_ids, tuple(parts.values()), blocks, qdev)
        got = lax.ppermute(other, "layer", [(0, 1), (1, 0)])
        total = (mine + got.astype(F32)).astype(BF16)
        return total.reshape(blocks, -1, rows).transpose(0, 2, 1)

    return body


def solution(mesh):
    in_specs = (
        P(("grp", "row"), "layer", None),
        P(None, "row", "layer", None),
        P("layer", None, None),
        P("layer", None, None),
        P("layer", None),
        P(),
        P(("grp", "row"), None),
    )
    out_specs = P(None, ("grp", "row"), "layer")
    body = make_body(mesh.shape["row"])
    return jax.shard_map(body, mesh=mesh, in_specs=in_specs, out_specs=out_specs, check_vma=False)
```

```python
import functools

import jax
import jax.numpy as jnp
from jax import lax
from jax.experimental import pallas as pl
from jax.experimental.pallas import tpu as pltpu
from jax.sharding import PartitionSpec as P

DAMPING = 0.01
LANES = 128
SEGMENTS = 4
F32, BF16 = jnp.float32, jnp.bfloat16
NT = (((1,), (1,)), ((), ()))


def split2(x):
    high = x.astype(BF16)
    return high, (x - high.astype(F32)).astype(BF16)


def mm(a, b):
    return jnp.dot(a, b, preferred_element_type=F32)


def mm_nt(a, b):
    return lax.dot_general(a, b, NT, preferred_element_type=F32)


def precondition_kernel(
    order_hbm, q_hbm, out_basis_hbm, in_basis_hbm, eig_hbm, ids_hbm, train_hbm,
    sent_ref, ids_out_ref, train_out_ref,
    order_ref, q_ref, out_basis_ref, in_basis_ref, eig_ref, x_scr, even_scr, odd_scr, o_scr, eig_scr, sems,
):
    copies = [
        pltpu.make_async_copy(src, dst, sems.at[n])
        for n, (src, dst) in enumerate((
            (order_hbm, order_ref), (q_hbm, q_ref), (in_basis_hbm, in_basis_ref), (out_basis_hbm, out_basis_ref), (eig_hbm, eig_ref),
            (ids_hbm, ids_out_ref), (train_hbm, train_out_ref),
        ))
    ]
    for copy in copies:
        copy.start()
    for copy in copies[:5]:
        copy.wait()
    blocks, lines, _ = q_ref.shape
    chunks = eig_ref.shape[0]
    side = out_basis_ref.shape[1]
    half = side // 2
    count = blocks * (lines // chunks)
    left_lanes = lax.broadcasted_iota(jnp.int32, (half, LANES), 1) < side

    def swapped(x):
        return jnp.concatenate([x[:, side:], x[:, :side]], axis=1)

    scale = 1.0 / (eig_ref[...] + DAMPING)
    turned = swapped(scale)
    eig_scr[pl.ds(0, half, stride=2), :] = jnp.where(left_lanes, scale, turned)
    eig_scr[pl.ds(1, half, stride=2), :] = jnp.where(left_lanes, turned, scale)
    scale = jnp.concatenate([eig_scr[...]] * blocks, axis=1)
    o_scr[:, :side] = out_basis_ref[0]
    basis = jnp.concatenate(
        [o_scr[pl.ds(0, half, stride=2), :side], o_scr[pl.ds(1, half, stride=2), :side]], axis=0
    )
    b_hi, b_lo = split2(basis)
    t_hi, t_lo = split2(basis.T)
    left = jnp.concatenate([t_hi, t_hi, t_lo], axis=1)
    back = jnp.concatenate([b_hi, b_hi, b_lo], axis=1)
    twice_hi, twice_lo = split2(jnp.concatenate([in_basis_ref[0]] * 2, axis=1))
    none = jnp.zeros_like(twice_hi)
    raw = jnp.concatenate([q_ref[order_ref[j]] for j in range(blocks)], axis=0)
    rotated = mm(jnp.concatenate([raw, raw], axis=1), jnp.concatenate([
        jnp.concatenate([twice_hi, none, twice_lo, none], axis=0),
        jnp.concatenate([none, twice_hi, none, twice_lo], axis=0),
    ], axis=1))
    even_scr[...] = rotated[:, :LANES]
    odd_scr[...] = rotated[:, LANES:]
    pairs = []
    for j in range(blocks):
        first, second = pl.ds(j * lines, half, stride=2), pl.ds(j * lines + 1, half, stride=2)
        pairs.append(jnp.concatenate(
            [jnp.where(left_lanes, scr[first, :], scr[second, :]) for scr in (even_scr, odd_scr)], axis=0
        ))
    hi, lo = split2(jnp.concatenate(pairs, axis=1))
    rotated = mm(left, jnp.concatenate([hi, lo, hi], axis=0))
    hi, lo = split2(rotated * scale)
    again = mm(back, jnp.concatenate([hi, lo, hi], axis=0))
    rows = jnp.concatenate([
        jnp.concatenate([again[at:at + half, j * LANES:(j + 1) * LANES] for j in range(blocks)], axis=0)
        for at in (0, half)
    ], axis=1)
    hi, lo = split2(rows)
    left_side = lax.broadcasted_iota(jnp.int32, (side, LANES), 1) < side

    def placed(twice):
        one, two = jnp.where(left_side, twice, 0), jnp.where(left_side, 0, twice)
        zero = jnp.zeros_like(one)
        return jnp.concatenate([
            jnp.concatenate([one, zero], axis=1), jnp.concatenate([zero, one], axis=1),
            jnp.concatenate([two, zero], axis=1), jnp.concatenate([zero, two], axis=1),
        ], axis=0).astype(BF16)

    w_hi, w_lo = placed(twice_hi.astype(F32)), placed(twice_lo.astype(F32))
    total = mm_nt(hi, w_hi) + mm_nt(lo, w_hi) + mm_nt(hi, w_lo)
    for j in range(blocks):
        for e in range(2):
            at = (2 * j + e) * chunks
            x_scr[at:at + chunks, :] = total[j * half:(j + 1) * half, e * LANES:(e + 1) * LANES]
    per = chunks // SEGMENTS
    for c in range(per):
        piece = x_scr[pl.ds(c, count * SEGMENTS, stride=per), :].astype(BF16)
        sent_ref[:, c * LANES:(c + 1) * LANES] = piece
    for copy in copies[5:]:
        copy.wait()


def precondition(block_order, query_grads, out_basis, in_basis, eigenvalues, row_ids, train):
    blocks, qdev, width = query_grads.shape
    count = blocks * qdev
    side = out_basis.shape[1]
    chunks = width // LANES
    query_grads = query_grads.reshape(blocks, qdev, chunks, LANES).swapaxes(1, 2).reshape(blocks, -1, LANES)
    eigenvalues = eigenvalues.reshape(chunks, LANES)
    vmem = pl.BlockSpec(memory_space=pltpu.VMEM)
    hbm = pl.BlockSpec(memory_space=pltpu.HBM)
    free = pl.BlockSpec(memory_space=pl.ANY)
    rows = pltpu.VMEM((count * chunks, LANES), F32)
    return pl.pallas_call(
        precondition_kernel,
        out_shape=(
            jax.ShapeDtypeStruct((count * SEGMENTS, width // SEGMENTS), BF16),
            jax.ShapeDtypeStruct(row_ids.shape, row_ids.dtype),
            jax.ShapeDtypeStruct(train.shape, train.dtype),
        ),
        in_specs=[hbm] * 7,
        out_specs=(vmem, free, free),
        scratch_shapes=[
            pltpu.SMEM(block_order.shape, block_order.dtype),
            pltpu.VMEM(query_grads.shape, BF16),
            pltpu.VMEM(out_basis.shape, F32),
            pltpu.VMEM(in_basis.shape, F32),
            pltpu.VMEM(eigenvalues.shape, F32),
            rows, rows, rows,
            pltpu.VMEM((side, LANES), F32),
            pltpu.VMEM((side, LANES), F32),
            pltpu.SemaphoreType.DMA((7,)),
        ],
        compiler_params=pltpu.CompilerParams(vmem_limit_bytes=4 * 2**20),
        name="precondition",
    )(*(
        pltpu.with_memory_space_constraint(x, pltpu.HBM)
        for x in (block_order, query_grads, out_basis, in_basis, eigenvalues, row_ids, train)
    ))


def split3(x):
    hi = x.astype(BF16)
    rest = x - hi.astype(F32)
    mid = rest.astype(BF16)
    return hi, mid, (rest - mid.astype(F32)).astype(BF16)


def slot_of(n_row, mask):
    mask, flip = mask
    source, per = lax.axis_index("row") ^ mask ^ (lax.axis_index("grp") * flip), n_row // 2
    return source ^ (lax.axis_index("layer") * per)


def placed_terms(masks, parts, train_ref, place, flat_scr):
    lines, seg = parts[0].shape
    n_row = len(masks)
    per_seg = seg // LANES
    for b, mask in enumerate(masks):
        at = pl.ds(pl.multiple_of(slot_of(n_row, mask) * lines, lines), lines)
        flat = parts[b][...].astype(F32) if b < len(parts) else jnp.zeros((lines, seg), F32)
        for c in range(per_seg):
            flat_scr[c, at, :] = flat[:, c * LANES:(c + 1) * LANES]
    terms = None
    for j in range(SEGMENTS):
        queries = jnp.concatenate([
            jnp.concatenate(
                [flat_scr[c, pl.ds(t + j, n_row, stride=lines), :] for t in range(0, lines, SEGMENTS)], axis=0
            )
            for c in range(per_seg)
        ], axis=1)
        term = mm_nt(queries.astype(BF16), train_ref[:, j * seg:(j + 1) * seg])
        terms = term if terms is None else terms + term
    a, b, c = split3(terms)
    return mm(a, place) + mm(b, place) + mm(c, place)


def early_kernel(masks, train_ref, ids_ref, *refs):
    parts, (terms_ref, place_ref, flat_scr) = refs[:-3], refs[-3:]
    rows = train_ref.shape[0]
    here = lax.broadcasted_iota(jnp.int32, (rows, rows), 0)
    place = (here == ids_ref[...]).astype(BF16)
    place_ref[...] = place
    terms_ref[...] = placed_terms(masks, parts, train_ref, place, flat_scr)


def late_kernel(masks, blocks, qdev, train_ref, place_ref, early_ref, *refs):
    parts, (mine_ref, other_ref, flat_scr, out_scr) = refs[:-4], refs[-4:]
    n_row = len(masks)
    per = n_row // 2
    terms = early_ref[...] + placed_terms(masks, parts, train_ref, place_ref[...], flat_scr)
    halves = terms.shape[1] // LANES
    half_rows = blocks * per * qdev
    for q in range(blocks * qdev):
        for which in range(2):
            first = which * half_rows + (q // qdev) * per * qdev + q % qdev
            at = q * n_row + which * per
            for h in range(halves):
                out_scr[h, pl.ds(first, per, stride=qdev), :] = terms[at:at + per, h * LANES:(h + 1) * LANES]
    for h in range(halves):
        mine_ref[:, h * LANES:(h + 1) * LANES] = out_scr[h, :half_rows]
        other_ref[:, h * LANES:(h + 1) * LANES] = out_scr[h, half_rows:]


def scores(masks, early, train, row_ids, parts, blocks, qdev):
    rows, width = train.shape
    n_row = len(masks)
    lines, seg = parts[0].shape
    queries = blocks * n_row * qdev
    vmem = pl.BlockSpec(memory_space=pltpu.VMEM)
    params = pltpu.CompilerParams(vmem_limit_bytes=(16 if n_row <= 16 else 40) * 2**20)
    cost = pl.CostEstimate(
        flops=2 * queries * rows * width, bytes_accessed=2 * (rows * width + n_row * lines * seg // 2),
        transcendentals=0,
    )
    flat_scr = pltpu.VMEM((seg // LANES, n_row * lines, LANES), F32)
    terms, place = pl.pallas_call(
        functools.partial(early_kernel, masks),
        out_shape=(
            jax.ShapeDtypeStruct((queries, rows), F32),
            jax.ShapeDtypeStruct((rows, rows), BF16),
        ),
        in_specs=[vmem] * (2 + early),
        out_specs=(vmem, vmem),
        scratch_shapes=[flat_scr],
        compiler_params=params,
        cost_estimate=cost,
        name="scores_early",
    )(train, row_ids, *parts[:early])
    out = jax.ShapeDtypeStruct((queries // 2, rows), F32)
    return pl.pallas_call(
        functools.partial(late_kernel, masks[early:] + masks[:early], blocks, qdev),
        out_shape=(out, out),
        in_specs=[vmem] * (3 + n_row - early),
        out_specs=(vmem, vmem),
        scratch_shapes=[flat_scr, pltpu.VMEM((rows // LANES, queries, LANES), F32)],
        compiler_params=params,
        cost_estimate=cost,
        name="scores_late",
    )(train, place, terms, *parts[early:])


def make_body(n_grp, n_row):
    def swap(x, mask, flip=0, cross=0):
        pairs = [
            (g * n_row + r, (g ^ cross) * n_row + (r ^ mask ^ (g * flip))) for g in range(n_grp) for r in range(n_row)
        ]
        return lax.ppermute(x, ("grp", "row"), pairs)

    def gather(own):
        if (n_grp, n_row) != (2, 8):
            near = {0: own, **{m: swap(own, m) for m in range(2, n_row, 2)}}
            parts = {**near, **{m ^ 1: swap(x, 1) for m, x in near.items()}}
            return {(m, 0): x for m, x in parts.items()}, n_row // 2
        far = swap(own, 4, 2)
        near = swap(own, 2)
        return {
            (0, 0): own, (1, 0): swap(own, 1), (2, 0): near, (4, 2): far,
            (7, 2): swap(own, 7, 2), (3, 0): swap(near, 1), (5, 2): swap(far, 1), (6, 2): swap(far, 0, cross=1),
        }, 4

    def body(train_grads, query_grads, out_basis, in_basis, eigenvalues, block_order, row_ids):
        blocks, qdev, _, width = query_grads.shape
        rows = train_grads.shape[0]
        own, row_ids, train = precondition(
            block_order, query_grads.reshape(blocks, qdev, width), out_basis, in_basis, eigenvalues, row_ids,
            train_grads.reshape(rows, width),
        )
        parts, early = gather(own)
        mine, other = scores(tuple(parts), early, train, row_ids, tuple(parts.values()), blocks, qdev)
        got = lax.ppermute(other, "layer", [(0, 1), (1, 0)])
        total = (mine + got).astype(BF16)
        return total.reshape(blocks, -1, rows).transpose(0, 2, 1)

    return body


def solution(mesh):
    in_specs = (
        P(("grp", "row"), "layer", None),
        P(None, "row", "layer", None),
        P("layer", None, None),
        P("layer", None, None),
        P("layer", None),
        P(),
        P(("grp", "row"), None),
    )
    out_specs = P(None, ("grp", "row"), "layer")
    body = make_body(mesh.shape["grp"], mesh.shape["row"])
    return jax.shard_map(body, mesh=mesh, in_specs=in_specs, out_specs=out_specs, check_vma=False)
```

```python
import functools

import jax
import jax.numpy as jnp
from jax import lax
from jax.experimental import pallas as pl
from jax.experimental.pallas import tpu as pltpu
from jax.sharding import PartitionSpec as P

DAMPING = 0.01
LANES = 128
SEGMENTS = 4
F32, BF16 = jnp.float32, jnp.bfloat16
NT = (((1,), (1,)), ((), ()))


def split2(x):
    high = x.astype(BF16)
    return high, (x - high.astype(F32)).astype(BF16)


def mm(a, b):
    return jnp.dot(a, b, preferred_element_type=F32)


def mm_nt(a, b):
    return lax.dot_general(a, b, NT, preferred_element_type=F32)


def precondition_kernel(
    order_hbm, q_hbm, out_basis_hbm, in_basis_hbm, eig_hbm, ids_hbm, train_hbm,
    sent_ref, ids_out_ref, train_out_ref,
    order_ref, q_ref, out_basis_ref, in_basis_ref, eig_ref, x_scr, even_scr, odd_scr, o_scr, eig_scr, sems,
):
    copies = [
        pltpu.make_async_copy(src, dst, sems.at[n])
        for n, (src, dst) in enumerate((
            (order_hbm, order_ref), (q_hbm, q_ref), (in_basis_hbm, in_basis_ref), (out_basis_hbm, out_basis_ref), (eig_hbm, eig_ref),
            (ids_hbm, ids_out_ref), (train_hbm, train_out_ref),
        ))
    ]
    for copy in copies:
        copy.start()
    for copy in copies[:5]:
        copy.wait()
    blocks, lines, _ = q_ref.shape
    chunks = eig_ref.shape[0]
    side = out_basis_ref.shape[1]
    half = side // 2
    count = blocks * (lines // chunks)
    left_lanes = lax.broadcasted_iota(jnp.int32, (half, LANES), 1) < side

    def swapped(x):
        return jnp.concatenate([x[:, side:], x[:, :side]], axis=1)

    scale = 1.0 / (eig_ref[...] + DAMPING)
    turned = swapped(scale)
    eig_scr[pl.ds(0, half, stride=2), :] = jnp.where(left_lanes, scale, turned)
    eig_scr[pl.ds(1, half, stride=2), :] = jnp.where(left_lanes, turned, scale)
    scale = jnp.concatenate([eig_scr[...]] * blocks, axis=1)
    o_scr[:, :side] = out_basis_ref[0]
    basis = jnp.concatenate(
        [o_scr[pl.ds(0, half, stride=2), :side], o_scr[pl.ds(1, half, stride=2), :side]], axis=0
    )
    b_hi, b_lo = split2(basis)
    t_hi, t_lo = split2(basis.T)
    left = jnp.concatenate([t_hi, t_hi, t_lo], axis=1)
    back = jnp.concatenate([b_hi, b_hi, b_lo], axis=1)
    twice_hi, twice_lo = split2(jnp.concatenate([in_basis_ref[0]] * 2, axis=1))
    none = jnp.zeros_like(twice_hi)
    raw = jnp.concatenate([q_ref[order_ref[j]] for j in range(blocks)], axis=0)
    rotated = mm(jnp.concatenate([raw, raw], axis=1), jnp.concatenate([
        jnp.concatenate([twice_hi, none, twice_lo, none], axis=0),
        jnp.concatenate([none, twice_hi, none, twice_lo], axis=0),
    ], axis=1))
    even_scr[...] = rotated[:, :LANES]
    odd_scr[...] = rotated[:, LANES:]
    pairs = []
    for j in range(blocks):
        first, second = pl.ds(j * lines, half, stride=2), pl.ds(j * lines + 1, half, stride=2)
        pairs.append(jnp.concatenate(
            [jnp.where(left_lanes, scr[first, :], scr[second, :]) for scr in (even_scr, odd_scr)], axis=0
        ))
    hi, lo = split2(jnp.concatenate(pairs, axis=1))
    rotated = mm(left, jnp.concatenate([hi, lo, hi], axis=0))
    hi, lo = split2(rotated * scale)
    again = mm(back, jnp.concatenate([hi, lo, hi], axis=0))
    rows = jnp.concatenate([
        jnp.concatenate([again[at:at + half, j * LANES:(j + 1) * LANES] for j in range(blocks)], axis=0)
        for at in (0, half)
    ], axis=1)
    hi, lo = split2(rows)
    left_side = lax.broadcasted_iota(jnp.int32, (side, LANES), 1) < side

    def placed(twice):
        one, two = jnp.where(left_side, twice, 0), jnp.where(left_side, 0, twice)
        zero = jnp.zeros_like(one)
        return jnp.concatenate([
            jnp.concatenate([one, zero], axis=1), jnp.concatenate([zero, one], axis=1),
            jnp.concatenate([two, zero], axis=1), jnp.concatenate([zero, two], axis=1),
        ], axis=0).astype(BF16)

    w_hi, w_lo = placed(twice_hi.astype(F32)), placed(twice_lo.astype(F32))
    total = mm_nt(hi, w_hi) + mm_nt(lo, w_hi) + mm_nt(hi, w_lo)
    for j in range(blocks):
        for e in range(2):
            at = (2 * j + e) * chunks
            x_scr[at:at + chunks, :] = total[j * half:(j + 1) * half, e * LANES:(e + 1) * LANES]
    per = chunks // SEGMENTS
    for c in range(per):
        piece = x_scr[pl.ds(c, count * SEGMENTS, stride=per), :].astype(BF16)
        sent_ref[:, c * LANES:(c + 1) * LANES] = piece
    for copy in copies[5:]:
        copy.wait()


def precondition(block_order, query_grads, out_basis, in_basis, eigenvalues, row_ids, train):
    blocks, qdev, width = query_grads.shape
    count = blocks * qdev
    side = out_basis.shape[1]
    chunks = width // LANES
    query_grads = query_grads.reshape(blocks, qdev, chunks, LANES).swapaxes(1, 2).reshape(blocks, -1, LANES)
    eigenvalues = eigenvalues.reshape(chunks, LANES)
    vmem = pl.BlockSpec(memory_space=pltpu.VMEM)
    hbm = pl.BlockSpec(memory_space=pltpu.HBM)
    free = pl.BlockSpec(memory_space=pl.ANY)
    rows = pltpu.VMEM((count * chunks, LANES), F32)
    return pl.pallas_call(
        precondition_kernel,
        out_shape=(
            jax.ShapeDtypeStruct((count * SEGMENTS, width // SEGMENTS), BF16),
            jax.ShapeDtypeStruct(row_ids.shape, row_ids.dtype),
            jax.ShapeDtypeStruct(train.shape, train.dtype),
        ),
        in_specs=[hbm] * 7,
        out_specs=(vmem, free, free),
        scratch_shapes=[
            pltpu.SMEM(block_order.shape, block_order.dtype),
            pltpu.VMEM(query_grads.shape, BF16),
            pltpu.VMEM(out_basis.shape, F32),
            pltpu.VMEM(in_basis.shape, F32),
            pltpu.VMEM(eigenvalues.shape, F32),
            rows, rows, rows,
            pltpu.VMEM((side, LANES), F32),
            pltpu.VMEM((side, LANES), F32),
            pltpu.SemaphoreType.DMA((7,)),
        ],
        compiler_params=pltpu.CompilerParams(vmem_limit_bytes=4 * 2**20),
        name="precondition",
    )(*(
        pltpu.with_memory_space_constraint(x, pltpu.HBM)
        for x in (block_order, query_grads, out_basis, in_basis, eigenvalues, row_ids, train)
    ))


def split3(x):
    hi = x.astype(BF16)
    rest = x - hi.astype(F32)
    mid = rest.astype(BF16)
    return hi, mid, (rest - mid.astype(F32)).astype(BF16)


def slot_of(n_row, mask):
    mask, flip = mask
    source, per = lax.axis_index("row") ^ mask ^ (lax.axis_index("grp") * flip), n_row // 2
    return source ^ (lax.axis_index("layer") * per)


def placed_terms(masks, parts, train_ref, place, flat_scr):
    lines, seg = parts[0].shape
    n_row = len(masks)
    per_seg = seg // LANES
    for b, mask in enumerate(masks):
        at = pl.ds(pl.multiple_of(slot_of(n_row, mask) * lines, lines), lines)
        flat = parts[b][...].astype(F32) if b < len(parts) else jnp.zeros((lines, seg), F32)
        for c in range(per_seg):
            flat_scr[c, at, :] = flat[:, c * LANES:(c + 1) * LANES]
    terms = None
    for j in range(SEGMENTS):
        queries = jnp.concatenate([
            jnp.concatenate(
                [flat_scr[c, pl.ds(t + j, n_row, stride=lines), :] for t in range(0, lines, SEGMENTS)], axis=0
            )
            for c in range(per_seg)
        ], axis=1)
        term = mm_nt(queries.astype(BF16), train_ref[:, j * seg:(j + 1) * seg])
        terms = term if terms is None else terms + term
    a, b, c = split3(terms)
    return mm(a, place) + mm(b, place) + mm(c, place)


def early_kernel(masks, train_ref, ids_ref, *refs):
    parts, (terms_ref, place_ref, flat_scr) = refs[:-3], refs[-3:]
    rows = train_ref.shape[0]
    here = lax.broadcasted_iota(jnp.int32, (rows, rows), 0)
    place = (here == ids_ref[...]).astype(BF16)
    place_ref[...] = place
    terms_ref[...] = placed_terms(masks, parts, train_ref, place, flat_scr)


def late_kernel(masks, blocks, qdev, train_ref, place_ref, early_ref, *refs):
    parts, (mine_ref, other_ref, flat_scr, out_scr) = refs[:-4], refs[-4:]
    n_row = len(masks)
    per = n_row // 2
    terms = early_ref[...] + placed_terms(masks, parts, train_ref, place_ref[...], flat_scr)
    halves = terms.shape[1] // LANES
    half_rows = blocks * per * qdev
    for q in range(blocks * qdev):
        for which in range(2):
            first = which * half_rows + (q // qdev) * per * qdev + q % qdev
            at = q * n_row + which * per
            for h in range(halves):
                out_scr[h, pl.ds(first, per, stride=qdev), :] = terms[at:at + per, h * LANES:(h + 1) * LANES]
    for h in range(halves):
        mine_ref[:, h * LANES:(h + 1) * LANES] = out_scr[h, :half_rows]
        other_ref[:, h * LANES:(h + 1) * LANES] = out_scr[h, half_rows:]


def scores(masks, early, train, row_ids, parts, blocks, qdev):
    rows, width = train.shape
    n_row = len(masks)
    lines, seg = parts[0].shape
    queries = blocks * n_row * qdev
    vmem = pl.BlockSpec(memory_space=pltpu.VMEM)
    params = pltpu.CompilerParams(vmem_limit_bytes=(16 if n_row <= 16 else 40) * 2**20)
    cost = pl.CostEstimate(
        flops=2 * queries * rows * width, bytes_accessed=2 * (rows * width + n_row * lines * seg // 2),
        transcendentals=0,
    )
    flat_scr = pltpu.VMEM((seg // LANES, n_row * lines, LANES), F32)
    terms, place = pl.pallas_call(
        functools.partial(early_kernel, masks),
        out_shape=(
            jax.ShapeDtypeStruct((queries, rows), F32),
            jax.ShapeDtypeStruct((rows, rows), BF16),
        ),
        in_specs=[vmem] * (2 + early),
        out_specs=(vmem, vmem),
        scratch_shapes=[flat_scr],
        compiler_params=params,
        cost_estimate=cost,
        name="scores_early",
    )(train, row_ids, *parts[:early])
    out = jax.ShapeDtypeStruct((queries // 2, rows), F32)
    return pl.pallas_call(
        functools.partial(late_kernel, masks[early:] + masks[:early], blocks, qdev),
        out_shape=(out, out),
        in_specs=[vmem] * (3 + n_row - early),
        out_specs=(vmem, vmem),
        scratch_shapes=[flat_scr, pltpu.VMEM((rows // LANES, queries, LANES), F32)],
        compiler_params=params,
        cost_estimate=cost,
        name="scores_late",
    )(train, place, terms, *parts[early:])


def make_body(n_grp, n_row):
    def swap(x, mask, flip=0, cross=0):
        pairs = [
            (g * n_row + r, (g ^ cross) * n_row + (r ^ mask ^ (g * flip))) for g in range(n_grp) for r in range(n_row)
        ]
        return lax.ppermute(x, ("grp", "row"), pairs)

    def gather(own):
        if (n_grp, n_row) != (2, 8):
            near = {0: own, **{m: swap(own, m) for m in range(2, n_row, 2)}}
            parts = {**near, **{m ^ 1: swap(x, 1) for m, x in near.items()}}
            return {(m, 0): x for m, x in parts.items()}, n_row // 2
        far = swap(own, 6, 2)
        near = swap(own, 2)
        return {
            (0, 0): own, (1, 0): swap(own, 1), (2, 0): near, (6, 2): far,
            (5, 2): swap(own, 5, 2), (3, 0): swap(near, 1), (7, 2): swap(far, 1), (4, 2): swap(far, 0, cross=1),
        }, 4

    def body(train_grads, query_grads, out_basis, in_basis, eigenvalues, block_order, row_ids):
        blocks, qdev, _, width = query_grads.shape
        rows = train_grads.shape[0]
        own, row_ids, train = precondition(
            block_order, query_grads.reshape(blocks, qdev, width), out_basis, in_basis, eigenvalues, row_ids,
            train_grads.reshape(rows, width),
        )
        parts, early = gather(own)
        mine, other = scores(tuple(parts), early, train, row_ids, tuple(parts.values()), blocks, qdev)
        got = lax.ppermute(other, "layer", [(0, 1), (1, 0)])
        total = (mine + got).astype(BF16)
        return total.reshape(blocks, -1, rows).transpose(0, 2, 1)

    return body


def solution(mesh):
    in_specs = (
        P(("grp", "row"), "layer", None),
        P(None, "row", "layer", None),
        P("layer", None, None),
        P("layer", None, None),
        P("layer", None),
        P(),
        P(("grp", "row"), None),
    )
    out_specs = P(None, ("grp", "row"), "layer")
    body = make_body(mesh.shape["grp"], mesh.shape["row"])
    return jax.shard_map(body, mesh=mesh, in_specs=in_specs, out_specs=out_specs, check_vma=False)
```

```python
import functools

import jax
import jax.numpy as jnp
from jax import lax
from jax.experimental import pallas as pl
from jax.experimental.pallas import tpu as pltpu
from jax.sharding import PartitionSpec as P

DAMPING = 0.01
LANES = 128
SEGMENTS = 4
F32, BF16 = jnp.float32, jnp.bfloat16
NT = (((1,), (1,)), ((), ()))


def split2(x):
    high = x.astype(BF16)
    return high, (x - high.astype(F32)).astype(BF16)


def mm(a, b):
    return jnp.dot(a, b, preferred_element_type=F32)


def mm_nt(a, b):
    return lax.dot_general(a, b, NT, preferred_element_type=F32)


def precondition_kernel(
    order_hbm, q_hbm, out_basis_hbm, in_basis_hbm, eig_hbm, ids_hbm, train_hbm,
    sent_ref, ids_out_ref, train_out_ref,
    order_ref, q_ref, out_basis_ref, in_basis_ref, eig_ref, x_scr, even_scr, odd_scr, o_scr, eig_scr, sems,
):
    copies = [
        pltpu.make_async_copy(src, dst, sems.at[n])
        for n, (src, dst) in enumerate((
            (order_hbm, order_ref), (q_hbm, q_ref), (in_basis_hbm, in_basis_ref), (out_basis_hbm, out_basis_ref), (eig_hbm, eig_ref),
            (ids_hbm, ids_out_ref), (train_hbm, train_out_ref),
        ))
    ]
    for copy in copies:
        copy.start()
    for copy in copies[:5]:
        copy.wait()
    blocks, lines, _ = q_ref.shape
    chunks = eig_ref.shape[0]
    side = out_basis_ref.shape[1]
    half = side // 2
    count = blocks * (lines // chunks)
    left_lanes = lax.broadcasted_iota(jnp.int32, (half, LANES), 1) < side

    def swapped(x):
        return jnp.concatenate([x[:, side:], x[:, :side]], axis=1)

    scale = 1.0 / (eig_ref[...] + DAMPING)
    turned = swapped(scale)
    eig_scr[pl.ds(0, half, stride=2), :] = jnp.where(left_lanes, scale, turned)
    eig_scr[pl.ds(1, half, stride=2), :] = jnp.where(left_lanes, turned, scale)
    scale = jnp.concatenate([eig_scr[...]] * blocks, axis=1)
    o_scr[:, :side] = out_basis_ref[0]
    basis = jnp.concatenate(
        [o_scr[pl.ds(0, half, stride=2), :side], o_scr[pl.ds(1, half, stride=2), :side]], axis=0
    )
    b_hi, b_lo = split2(basis)
    t_hi, t_lo = split2(basis.T)
    left = jnp.concatenate([t_hi, t_hi, t_lo], axis=1)
    back = jnp.concatenate([b_hi, b_hi, b_lo], axis=1)
    twice_hi, twice_lo = split2(jnp.concatenate([in_basis_ref[0]] * 2, axis=1))
    none = jnp.zeros_like(twice_hi)
    raw = jnp.concatenate([q_ref[order_ref[j]] for j in range(blocks)], axis=0)
    rotated = mm(jnp.concatenate([raw, raw], axis=1), jnp.concatenate([
        jnp.concatenate([twice_hi, none, twice_lo, none], axis=0),
        jnp.concatenate([none, twice_hi, none, twice_lo], axis=0),
    ], axis=1))
    even_scr[...] = rotated[:, :LANES]
    odd_scr[...] = rotated[:, LANES:]
    pairs = []
    for j in range(blocks):
        first, second = pl.ds(j * lines, half, stride=2), pl.ds(j * lines + 1, half, stride=2)
        pairs.append(jnp.concatenate(
            [jnp.where(left_lanes, scr[first, :], scr[second, :]) for scr in (even_scr, odd_scr)], axis=0
        ))
    hi, lo = split2(jnp.concatenate(pairs, axis=1))
    rotated = mm(left, jnp.concatenate([hi, lo, hi], axis=0))
    hi, lo = split2(rotated * scale)
    again = mm(back, jnp.concatenate([hi, lo, hi], axis=0))
    rows = jnp.concatenate([
        jnp.concatenate([again[at:at + half, j * LANES:(j + 1) * LANES] for j in range(blocks)], axis=0)
        for at in (0, half)
    ], axis=1)
    hi, lo = split2(rows)
    left_side = lax.broadcasted_iota(jnp.int32, (side, LANES), 1) < side

    def placed(twice):
        one, two = jnp.where(left_side, twice, 0), jnp.where(left_side, 0, twice)
        zero = jnp.zeros_like(one)
        return jnp.concatenate([
            jnp.concatenate([one, zero], axis=1), jnp.concatenate([zero, one], axis=1),
            jnp.concatenate([two, zero], axis=1), jnp.concatenate([zero, two], axis=1),
        ], axis=0).astype(BF16)

    w_hi, w_lo = placed(twice_hi.astype(F32)), placed(twice_lo.astype(F32))
    total = mm_nt(hi, w_hi) + mm_nt(lo, w_hi) + mm_nt(hi, w_lo)
    for j in range(blocks):
        for e in range(2):
            at = (2 * j + e) * chunks
            x_scr[at:at + chunks, :] = total[j * half:(j + 1) * half, e * LANES:(e + 1) * LANES]
    per = chunks // SEGMENTS
    for c in range(per):
        piece = x_scr[pl.ds(c, count * SEGMENTS, stride=per), :].astype(BF16)
        sent_ref[:, c * LANES:(c + 1) * LANES] = piece
    for copy in copies[5:]:
        copy.wait()


def precondition(block_order, query_grads, out_basis, in_basis, eigenvalues, row_ids, train):
    blocks, qdev, width = query_grads.shape
    count = blocks * qdev
    side = out_basis.shape[1]
    chunks = width // LANES
    query_grads = query_grads.reshape(blocks, qdev, chunks, LANES).swapaxes(1, 2).reshape(blocks, -1, LANES)
    eigenvalues = eigenvalues.reshape(chunks, LANES)
    vmem = pl.BlockSpec(memory_space=pltpu.VMEM)
    hbm = pl.BlockSpec(memory_space=pltpu.HBM)
    free = pl.BlockSpec(memory_space=pl.ANY)
    rows = pltpu.VMEM((count * chunks, LANES), F32)
    return pl.pallas_call(
        precondition_kernel,
        out_shape=(
            jax.ShapeDtypeStruct((count * SEGMENTS, width // SEGMENTS), BF16),
            jax.ShapeDtypeStruct(row_ids.shape, row_ids.dtype),
            jax.ShapeDtypeStruct(train.shape, train.dtype),
        ),
        in_specs=[hbm] * 7,
        out_specs=(vmem, free, free),
        scratch_shapes=[
            pltpu.SMEM(block_order.shape, block_order.dtype),
            pltpu.VMEM(query_grads.shape, BF16),
            pltpu.VMEM(out_basis.shape, F32),
            pltpu.VMEM(in_basis.shape, F32),
            pltpu.VMEM(eigenvalues.shape, F32),
            rows, rows, rows,
            pltpu.VMEM((side, LANES), F32),
            pltpu.VMEM((side, LANES), F32),
            pltpu.SemaphoreType.DMA((7,)),
        ],
        compiler_params=pltpu.CompilerParams(vmem_limit_bytes=4 * 2**20),
        name="precondition",
    )(*(
        pltpu.with_memory_space_constraint(x, pltpu.HBM)
        for x in (block_order, query_grads, out_basis, in_basis, eigenvalues, row_ids, train)
    ))


def split3(x):
    hi = x.astype(BF16)
    rest = x - hi.astype(F32)
    mid = rest.astype(BF16)
    return hi, mid, (rest - mid.astype(F32)).astype(BF16)


def slot_of(n_row, mask):
    source, per = lax.axis_index("row") ^ mask, n_row // 2
    return source ^ (lax.axis_index("layer") * per)


def placed_terms(masks, parts, train_ref, place, flat_scr):
    lines, seg = parts[0].shape
    n_row = len(masks)
    per_seg = seg // LANES
    for b, mask in enumerate(masks):
        at = pl.ds(pl.multiple_of(slot_of(n_row, mask) * lines, lines), lines)
        flat = parts[b][...].astype(F32) if b < len(parts) else jnp.zeros((lines, seg), F32)
        for c in range(per_seg):
            flat_scr[c, at, :] = flat[:, c * LANES:(c + 1) * LANES]
    terms = None
    for j in range(SEGMENTS):
        queries = jnp.concatenate([
            jnp.concatenate(
                [flat_scr[c, pl.ds(t + j, n_row, stride=lines), :] for t in range(0, lines, SEGMENTS)], axis=0
            )
            for c in range(per_seg)
        ], axis=1)
        term = mm_nt(queries.astype(BF16), train_ref[:, j * seg:(j + 1) * seg])
        terms = term if terms is None else terms + term
    a, b, c = split3(terms)
    return mm(a, place) + mm(b, place) + mm(c, place)


def early_kernel(masks, train_ref, ids_ref, *refs):
    parts, (terms_ref, place_ref, flat_scr) = refs[:-3], refs[-3:]
    rows = train_ref.shape[0]
    here = lax.broadcasted_iota(jnp.int32, (rows, rows), 0)
    place = (here == ids_ref[...]).astype(BF16)
    place_ref[...] = place
    terms_ref[...] = placed_terms(masks, parts, train_ref, place, flat_scr)


def late_kernel(masks, blocks, qdev, train_ref, place_ref, early_ref, *refs):
    parts, (mine_ref, other_ref, flat_scr, out_scr) = refs[:-4], refs[-4:]
    n_row = len(masks)
    per = n_row // 2
    terms = early_ref[...] + placed_terms(masks, parts, train_ref, place_ref[...], flat_scr)
    halves = terms.shape[1] // LANES
    half_rows = blocks * per * qdev
    for q in range(blocks * qdev):
        for which in range(2):
            first = which * half_rows + (q // qdev) * per * qdev + q % qdev
            at = q * n_row + which * per
            for h in range(halves):
                out_scr[h, pl.ds(first, per, stride=qdev), :] = terms[at:at + per, h * LANES:(h + 1) * LANES]
    for h in range(halves):
        mine_ref[:, h * LANES:(h + 1) * LANES] = out_scr[h, :half_rows]
        other_ref[:, h * LANES:(h + 1) * LANES] = out_scr[h, half_rows:]


def scores(masks, early, train, row_ids, parts, blocks, qdev):
    rows, width = train.shape
    n_row = len(masks)
    lines, seg = parts[0].shape
    queries = blocks * n_row * qdev
    vmem = pl.BlockSpec(memory_space=pltpu.VMEM)
    params = pltpu.CompilerParams(vmem_limit_bytes=(16 if n_row <= 16 else 40) * 2**20)
    cost = pl.CostEstimate(
        flops=2 * queries * rows * width, bytes_accessed=2 * (rows * width + n_row * lines * seg // 2),
        transcendentals=0,
    )
    flat_scr = pltpu.VMEM((seg // LANES, n_row * lines, LANES), F32)
    terms, place = pl.pallas_call(
        functools.partial(early_kernel, masks),
        out_shape=(
            jax.ShapeDtypeStruct((queries, rows), F32),
            jax.ShapeDtypeStruct((rows, rows), BF16),
        ),
        in_specs=[vmem] * (2 + early),
        out_specs=(vmem, vmem),
        scratch_shapes=[flat_scr],
        compiler_params=params,
        cost_estimate=cost,
        name="scores_early",
    )(train, row_ids, *parts[:early])
    out = jax.ShapeDtypeStruct((queries // 2, rows), F32)
    return pl.pallas_call(
        functools.partial(late_kernel, masks[early:] + masks[:early], blocks, qdev),
        out_shape=(out, out),
        in_specs=[vmem] * (3 + n_row - early),
        out_specs=(vmem, vmem),
        scratch_shapes=[flat_scr, pltpu.VMEM((rows // LANES, queries, LANES), F32)],
        compiler_params=params,
        cost_estimate=cost,
        name="scores_late",
    )(train, place, terms, *parts[early:])


def make_body(n_row):
    def swap(x, mask):
        return lax.ppermute(x, "row", [(r, r ^ mask) for r in range(n_row)])

    def gather(own):
        if n_row != 8:
            near = {0: own, **{m: swap(own, m) for m in range(2, n_row, 2)}}
            return {**near, **{m ^ 1: swap(x, 1) for m, x in near.items()}}, n_row // 2
        far = {m: swap(own, m) for m in (4, 6)}
        diagonal = {3: swap(own, 3)}
        near = {m: swap(own, m) for m in (2, 1)}
        return {0: own, **near, **far, **diagonal, **{m ^ 1: swap(x, 1) for m, x in far.items()}}, 5

    def body(train_grads, query_grads, out_basis, in_basis, eigenvalues, block_order, row_ids):
        blocks, qdev, _, width = query_grads.shape
        rows = train_grads.shape[0]
        own, row_ids, train = precondition(
            block_order, query_grads.reshape(blocks, qdev, width), out_basis, in_basis, eigenvalues, row_ids,
            train_grads.reshape(rows, width),
        )
        parts, early = gather(own)
        mine, other = scores(tuple(parts), early, train, row_ids, tuple(parts.values()), blocks, qdev)
        got = lax.ppermute(other, "layer", [(0, 1), (1, 0)])
        total = (mine + got).astype(BF16)
        return total.reshape(blocks, -1, rows).transpose(0, 2, 1)

    return body


def solution(mesh):
    in_specs = (
        P(("grp", "row"), "layer", None),
        P(None, "row", "layer", None),
        P("layer", None, None),
        P("layer", None, None),
        P("layer", None),
        P(),
        P(("grp", "row"), None),
    )
    out_specs = P(None, ("grp", "row"), "layer")
    body = make_body(mesh.shape["row"])
    return jax.shard_map(body, mesh=mesh, in_specs=in_specs, out_specs=out_specs, check_vma=False)
```

```python
import functools

import jax
import jax.numpy as jnp
from jax import lax
from jax.experimental import pallas as pl
from jax.experimental.pallas import tpu as pltpu
from jax.sharding import PartitionSpec as P

DAMPING = 0.01
LANES = 128
SEGMENTS = 4
F32, BF16 = jnp.float32, jnp.bfloat16
NT = (((1,), (1,)), ((), ()))


def split2(x):
    high = x.astype(BF16)
    return high, (x - high.astype(F32)).astype(BF16)


def mm(a, b):
    return jnp.dot(a, b, preferred_element_type=F32)


def mm_nt(a, b):
    return lax.dot_general(a, b, NT, preferred_element_type=F32)


def precondition_kernel(
    order_hbm, q_hbm, out_basis_hbm, in_basis_hbm, eig_hbm, ids_hbm, train_hbm,
    sent_ref, ids_out_ref, train_out_ref,
    order_ref, q_ref, out_basis_ref, in_basis_ref, eig_ref, x_scr, even_scr, odd_scr, o_scr, eig_scr, sems,
):
    copies = [
        pltpu.make_async_copy(src, dst, sems.at[n])
        for n, (src, dst) in enumerate((
            (order_hbm, order_ref), (q_hbm, q_ref), (in_basis_hbm, in_basis_ref), (out_basis_hbm, out_basis_ref), (eig_hbm, eig_ref),
            (ids_hbm, ids_out_ref), (train_hbm, train_out_ref),
        ))
    ]
    for copy in copies:
        copy.start()
    for copy in copies[:5]:
        copy.wait()
    blocks, lines, _ = q_ref.shape
    chunks = eig_ref.shape[0]
    side = out_basis_ref.shape[1]
    half = side // 2
    count = blocks * (lines // chunks)
    left_lanes = lax.broadcasted_iota(jnp.int32, (half, LANES), 1) < side

    def swapped(x):
        return jnp.concatenate([x[:, side:], x[:, :side]], axis=1)

    scale = 1.0 / (eig_ref[...] + DAMPING)
    turned = swapped(scale)
    eig_scr[pl.ds(0, half, stride=2), :] = jnp.where(left_lanes, scale, turned)
    eig_scr[pl.ds(1, half, stride=2), :] = jnp.where(left_lanes, turned, scale)
    scale = jnp.concatenate([eig_scr[...]] * blocks, axis=1)
    o_scr[:, :side] = out_basis_ref[0]
    basis = jnp.concatenate(
        [o_scr[pl.ds(0, half, stride=2), :side], o_scr[pl.ds(1, half, stride=2), :side]], axis=0
    )
    b_hi, b_lo = split2(basis)
    t_hi, t_lo = split2(basis.T)
    left = jnp.concatenate([t_hi, t_hi, t_lo], axis=1)
    back = jnp.concatenate([b_hi, b_hi, b_lo], axis=1)
    twice_hi, twice_lo = split2(jnp.concatenate([in_basis_ref[0]] * 2, axis=1))
    none = jnp.zeros_like(twice_hi)
    raw = jnp.concatenate([q_ref[order_ref[j]] for j in range(blocks)], axis=0)
    rotated = mm(jnp.concatenate([raw, raw], axis=1), jnp.concatenate([
        jnp.concatenate([twice_hi, none, twice_lo, none], axis=0),
        jnp.concatenate([none, twice_hi, none, twice_lo], axis=0),
    ], axis=1))
    even_scr[...] = rotated[:, :LANES]
    odd_scr[...] = rotated[:, LANES:]
    pairs = []
    for j in range(blocks):
        first, second = pl.ds(j * lines, half, stride=2), pl.ds(j * lines + 1, half, stride=2)
        pairs.append(jnp.concatenate(
            [jnp.where(left_lanes, scr[first, :], scr[second, :]) for scr in (even_scr, odd_scr)], axis=0
        ))
    hi, lo = split2(jnp.concatenate(pairs, axis=1))
    rotated = mm(left, jnp.concatenate([hi, lo, hi], axis=0))
    hi, lo = split2(rotated * scale)
    again = mm(back, jnp.concatenate([hi, lo, hi], axis=0))
    rows = jnp.concatenate([
        jnp.concatenate([again[at:at + half, j * LANES:(j + 1) * LANES] for j in range(blocks)], axis=0)
        for at in (0, half)
    ], axis=1)
    hi, lo = split2(rows)
    left_side = lax.broadcasted_iota(jnp.int32, (side, LANES), 1) < side

    def placed(twice):
        one, two = jnp.where(left_side, twice, 0), jnp.where(left_side, 0, twice)
        zero = jnp.zeros_like(one)
        return jnp.concatenate([
            jnp.concatenate([one, zero], axis=1), jnp.concatenate([zero, one], axis=1),
            jnp.concatenate([two, zero], axis=1), jnp.concatenate([zero, two], axis=1),
        ], axis=0).astype(BF16)

    w_hi, w_lo = placed(twice_hi.astype(F32)), placed(twice_lo.astype(F32))
    total = mm_nt(hi, w_hi) + mm_nt(lo, w_hi) + mm_nt(hi, w_lo)
    for j in range(blocks):
        for e in range(2):
            at = (2 * j + e) * chunks
            x_scr[at:at + chunks, :] = total[j * half:(j + 1) * half, e * LANES:(e + 1) * LANES]
    per = chunks // SEGMENTS
    for c in range(per):
        piece = x_scr[pl.ds(c, count * SEGMENTS, stride=per), :].astype(BF16)
        sent_ref[:, c * LANES:(c + 1) * LANES] = piece
    for copy in copies[5:]:
        copy.wait()


def precondition(block_order, query_grads, out_basis, in_basis, eigenvalues, row_ids, train):
    blocks, qdev, width = query_grads.shape
    count = blocks * qdev
    side = out_basis.shape[1]
    chunks = width // LANES
    query_grads = query_grads.reshape(blocks, qdev, chunks, LANES).swapaxes(1, 2).reshape(blocks, -1, LANES)
    eigenvalues = eigenvalues.reshape(chunks, LANES)
    vmem = pl.BlockSpec(memory_space=pltpu.VMEM)
    hbm = pl.BlockSpec(memory_space=pltpu.HBM)
    free = pl.BlockSpec(memory_space=pl.ANY)
    rows = pltpu.VMEM((count * chunks, LANES), F32)
    return pl.pallas_call(
        precondition_kernel,
        out_shape=(
            jax.ShapeDtypeStruct((count * SEGMENTS, width // SEGMENTS), BF16),
            jax.ShapeDtypeStruct(row_ids.shape, row_ids.dtype),
            jax.ShapeDtypeStruct(train.shape, train.dtype),
        ),
        in_specs=[hbm] * 7,
        out_specs=(vmem, free, free),
        scratch_shapes=[
            pltpu.SMEM(block_order.shape, block_order.dtype),
            pltpu.VMEM(query_grads.shape, BF16),
            pltpu.VMEM(out_basis.shape, F32),
            pltpu.VMEM(in_basis.shape, F32),
            pltpu.VMEM(eigenvalues.shape, F32),
            rows, rows, rows,
            pltpu.VMEM((side, LANES), F32),
            pltpu.VMEM((side, LANES), F32),
            pltpu.SemaphoreType.DMA((7,)),
        ],
        compiler_params=pltpu.CompilerParams(vmem_limit_bytes=4 * 2**20),
        name="precondition",
    )(*(
        pltpu.with_memory_space_constraint(x, pltpu.HBM)
        for x in (block_order, query_grads, out_basis, in_basis, eigenvalues, row_ids, train)
    ))


def slot_of(n_row, mask):
    source, per = lax.axis_index("row") ^ mask, n_row // 2
    return source ^ (lax.axis_index("layer") * per)


def placed_terms(masks, parts, train_ref, place, flat_scr):
    lines, seg = parts[0].shape
    n_row = len(masks)
    per_seg = seg // LANES
    for b, mask in enumerate(masks):
        at = pl.ds(pl.multiple_of(slot_of(n_row, mask) * lines, lines), lines)
        flat = parts[b][...].astype(F32) if b < len(parts) else jnp.zeros((lines, seg), F32)
        for c in range(per_seg):
            flat_scr[c, at, :] = flat[:, c * LANES:(c + 1) * LANES]
    terms = None
    for j in range(SEGMENTS):
        queries = jnp.concatenate([
            jnp.concatenate(
                [flat_scr[c, pl.ds(t + j, n_row, stride=lines), :] for t in range(0, lines, SEGMENTS)], axis=0
            )
            for c in range(per_seg)
        ], axis=1)
        term = mm_nt(queries.astype(BF16), train_ref[:, j * seg:(j + 1) * seg])
        terms = term if terms is None else terms + term
    hi, lo = split2(terms)
    return mm(hi, place) + mm(lo, place)


def early_kernel(masks, train_ref, ids_ref, *refs):
    parts, (terms_ref, place_ref, flat_scr) = refs[:-3], refs[-3:]
    rows = train_ref.shape[0]
    here = lax.broadcasted_iota(jnp.int32, (rows, rows), 0)
    place = (here == ids_ref[...]).astype(BF16)
    place_ref[...] = place
    terms_ref[...] = placed_terms(masks, parts, train_ref, place, flat_scr)


def late_kernel(masks, blocks, qdev, train_ref, place_ref, early_ref, *refs):
    parts, (mine_ref, other_ref, flat_scr, out_scr) = refs[:-4], refs[-4:]
    n_row = len(masks)
    per = n_row // 2
    terms = early_ref[...] + placed_terms(masks, parts, train_ref, place_ref[...], flat_scr)
    halves = terms.shape[1] // LANES
    half_rows = blocks * per * qdev
    for q in range(blocks * qdev):
        for which in range(2):
            first = which * half_rows + (q // qdev) * per * qdev + q % qdev
            at = q * n_row + which * per
            for h in range(halves):
                out_scr[h, pl.ds(first, per, stride=qdev), :] = terms[at:at + per, h * LANES:(h + 1) * LANES]
    for h in range(halves):
        mine_ref[:, h * LANES:(h + 1) * LANES] = out_scr[h, :half_rows]
        other_ref[:, h * LANES:(h + 1) * LANES] = out_scr[h, half_rows:]


def scores(masks, early, train, row_ids, parts, blocks, qdev):
    rows, width = train.shape
    n_row = len(masks)
    lines, seg = parts[0].shape
    queries = blocks * n_row * qdev
    vmem = pl.BlockSpec(memory_space=pltpu.VMEM)
    params = pltpu.CompilerParams(vmem_limit_bytes=(16 if n_row <= 16 else 40) * 2**20)
    cost = pl.CostEstimate(
        flops=2 * queries * rows * width, bytes_accessed=2 * (rows * width + n_row * lines * seg // 2),
        transcendentals=0,
    )
    flat_scr = pltpu.VMEM((seg // LANES, n_row * lines, LANES), F32)
    terms, place = pl.pallas_call(
        functools.partial(early_kernel, masks),
        out_shape=(
            jax.ShapeDtypeStruct((queries, rows), F32),
            jax.ShapeDtypeStruct((rows, rows), BF16),
        ),
        in_specs=[vmem] * (2 + early),
        out_specs=(vmem, vmem),
        scratch_shapes=[flat_scr],
        compiler_params=params,
        cost_estimate=cost,
        name="scores_early",
    )(train, row_ids, *parts[:early])
    out = jax.ShapeDtypeStruct((queries // 2, rows), F32)
    return pl.pallas_call(
        functools.partial(late_kernel, masks[early:] + masks[:early], blocks, qdev),
        out_shape=(out, out),
        in_specs=[vmem] * (3 + n_row - early),
        out_specs=(vmem, vmem),
        scratch_shapes=[flat_scr, pltpu.VMEM((rows // LANES, queries, LANES), F32)],
        compiler_params=params,
        cost_estimate=cost,
        name="scores_late",
    )(train, place, terms, *parts[early:])


def make_body(n_row):
    def swap(x, mask):
        return lax.ppermute(x, "row", [(r, r ^ mask) for r in range(n_row)])

    def gather(own):
        if n_row != 8:
            near = {0: own, **{m: swap(own, m) for m in range(2, n_row, 2)}}
            return {**near, **{m ^ 1: swap(x, 1) for m, x in near.items()}}, n_row // 2
        far = {m: swap(own, m) for m in (6, 4)}
        diagonal = {3: swap(own, 3)}
        near = {m: swap(own, m) for m in (1, 2)}
        return {0: own, **near, **far, **diagonal, **{m ^ 1: swap(x, 1) for m, x in far.items()}}, 5

    def body(train_grads, query_grads, out_basis, in_basis, eigenvalues, block_order, row_ids):
        blocks, qdev, _, width = query_grads.shape
        rows = train_grads.shape[0]
        own, row_ids, train = precondition(
            block_order, query_grads.reshape(blocks, qdev, width), out_basis, in_basis, eigenvalues, row_ids,
            train_grads.reshape(rows, width),
        )
        parts, early = gather(own)
        mine, other = scores(tuple(parts), early, train, row_ids, tuple(parts.values()), blocks, qdev)
        got = lax.ppermute(other, "layer", [(0, 1), (1, 0)])
        total = (mine + got).astype(BF16)
        return total.reshape(blocks, -1, rows).transpose(0, 2, 1)

    return body


def solution(mesh):
    in_specs = (
        P(("grp", "row"), "layer", None),
        P(None, "row", "layer", None),
        P("layer", None, None),
        P("layer", None, None),
        P("layer", None),
        P(),
        P(("grp", "row"), None),
    )
    out_specs = P(None, ("grp", "row"), "layer")
    body = make_body(mesh.shape["row"])
    return jax.shard_map(body, mesh=mesh, in_specs=in_specs, out_specs=out_specs, check_vma=False)
```
